32 devices in a mesh: dp: 8 (over z, x), rows: 4 (over y, core).
Axes of the slice: x: 2, y: 2, z: 4, core: 2. Of those that a mesh axis runs over, the one named last changes fastest.
Arguments:
- input_a: bfloat16 [16, 32, 14, 1024], P('rows', 'dp'), may hold values from -48 to 48
- input_b: bfloat16 [16, 96, 10, 1024], P('rows', 'dp'), may hold values from -48 to 48
- live_views: int32 [8, 2], replicated, may hold values from 2 to 12, as said below
- reduce_one: bfloat16 [1024, 256], replicated, may hold values from -0.1875 to 0.1875
- spatial_one: bfloat16 [256, 3, 3, 256], replicated, may hold values from -0.125 to 0.125
- expand_one: bfloat16 [256, 1024], replicated, may hold values from -0.375 to 0.375
- reduce_two: bfloat16 [1024, 512], replicated, may hold values from -0.1875 to 0.1875
- spatial_two: bfloat16 [512, 3, 3, 512], replicated, may hold values from -0.09375 to 0.09375
- expand_two: bfloat16 [512, 2048], replicated, may hold values from -0.25 to 0.25
- shortcut_two: bfloat16 [1024, 2048], replicated, may hold values from -0.1875 to 0.1875
- gain_narrow: float32 [256], replicated, may hold values from 0.5 to 1.5
- bias_narrow: float32 [256], replicated, may hold values from -0.5 to 0.5
- gain_spatial: float32 [256], replicated, may hold values from 0.5 to 1.5
- bias_spatial: float32 [256], replicated, may hold values from -0.5 to 0.5
- gain_widened: float32 [1024], replicated, may hold values from 0.5 to 1.5
- bias_widened: float32 [1024], replicated, may hold values from -0.5 to 0.5
- gain_squeeze: float32 [512], replicated, may hold values from 0.5 to 1.5
- bias_squeeze: float32 [512], replicated, may hold values from -0.5 to 0.5
- gain_strided: float32 [512], replicated, may hold values from 0.5 to 1.5
- bias_strided: float32 [512], replicated, may hold values from -0.5 to 0.5
- gain_output: float32 [2048], replicated, may hold values from 0.5 to 1.5
- bias_output: float32 [2048], replicated, may hold values from -0.5 to 0.5
- gain_shortcut: float32 [2048], replicated, may hold values from 0.5 to 1.5
- bias_shortcut: float32 [2048], replicated, may hold values from -0.5 to 0.5
- cotangent_a: bfloat16 [8, 32, 7, 2048], P('rows', 'dp'), may hold values from -6 to 6
- cotangent_b: bfloat16 [8, 96, 5, 2048], P('rows', 'dp'), may hold values from -6 to 6
Outputs:
- block_out_a: bfloat16 [8, 32, 7, 2048], P('rows', 'dp')
- block_out_b: bfloat16 [8, 96, 5, 2048], P('rows', 'dp')
- grad_input_a: bfloat16 [16, 32, 14, 1024], P('rows', 'dp')
- grad_input_b: bfloat16 [16, 96, 10, 1024], P('rows', 'dp')
- grad_reduce_one: float32 [1024, 256], P(('dp', 'rows'))
- grad_spatial_one: float32 [256, 3, 3, 256], P(('dp', 'rows'))
- grad_expand_one: float32 [256, 1024], P(('dp', 'rows'))
- grad_reduce_two: float32 [1024, 512], P(('dp', 'rows'))
- grad_spatial_two: float32 [512, 3, 3, 512], P(('dp', 'rows'))
- grad_expand_two: float32 [512, 2048], P(('dp', 'rows'))
- grad_shortcut_two: float32 [1024, 2048], P(('dp', 'rows'))
- grad_gain_narrow: float32 [256], replicated
- grad_bias_narrow: float32 [256], replicated
- grad_gain_spatial: float32 [256], replicated
- grad_bias_spatial: float32 [256], replicated
- grad_gain_widened: float32 [1024], replicated
- grad_bias_widened: float32 [1024], replicated
- grad_gain_squeeze: float32 [512], replicated
- grad_bias_squeeze: float32 [512], replicated
- grad_gain_strided: float32 [512], replicated
- grad_bias_strided: float32 [512], replicated
- grad_gain_output: float32 [2048], replicated
- grad_bias_output: float32 [2048], replicated
- grad_gain_shortcut: float32 [2048], replicated
- grad_bias_shortcut: float32 [2048], replicated
The draws below stay inside these ranges and needn't reach their ends.
Inputs may be any that keep to these rules, and one draw needn't show every extreme that they name: `live_views`: row d gives the live views in the slots of index d of dp: column 0 for the first group (at most 4), column 1 for the second (at most 12); live views fill the first slots, at least half of them, and in every draw some index holds 4 live views of the first group and some index 12 of the second.
All inputs are finite; a program needn't handle non-finite values.
Results may differ from the reference program's by a relative error of at most 0.023.
Values may be sent and summed in bfloat16 or wider, within the bound.
A program may use at most 192 MiB of HBM per device.

```python
import math
import jax
import jax.numpy as jnp
from jax import lax

C_IN = 1024
C_MID = 256
C_MID2 = 512
C_OUT = 2048
HA = 14
WA = 14
HB = 10
WB = 10
VA = 4
VB = 12
HPA = 16
HPB = 16
VIEWS_A = 32
VIEWS_B = 96
N_DP = 8


def scaled_views(key, base, views, chans):
    first, second = jax.random.split(key)
    view_scale = jnp.exp(jax.random.uniform(first, (1, views, 1, 1), jnp.float32, math.log(0.4), math.log(4.0)))
    chan_scale = jnp.exp(jax.random.uniform(second, (1, 1, 1, chans), jnp.float32, math.log(0.5), math.log(2.0)))
    return (base * chan_scale * view_scale).astype(jnp.bfloat16)


def draw_input_a(key, part):
    key = jax.random.fold_in(key, 11)
    first, second = jax.random.split(key, 2)
    shape = (HPA, VIEWS_A, WA, C_IN)
    base = jnp.clip(jax.random.normal(first, shape, jnp.float32), -5.0, 5.0)
    return scaled_views(second, base, VIEWS_A, C_IN)


def draw_input_b(key, part):
    key = jax.random.fold_in(key, 13)
    first, second = jax.random.split(key, 2)
    shape = (HPB, VIEWS_B, WB, C_IN)
    base = jnp.clip(jax.random.normal(first, shape, jnp.float32), -5.0, 5.0)
    return scaled_views(second, base, VIEWS_B, C_IN)


def draw_live_views(key, part):
    key = jax.random.fold_in(key, 7)
    first, second, third, fourth = jax.random.split(key, 4)
    column_a = jax.random.randint(first, (N_DP,), (VA + 1) // 2, VA + 1)
    column_b = jax.random.randint(second, (N_DP,), (VB + 1) // 2, VB + 1)
    full_a = jax.random.randint(third, (), 0, N_DP)
    full_b = jax.random.randint(fourth, (), 0, N_DP)
    column_a = jnp.where(jnp.arange(N_DP) == full_a, VA, column_a)
    column_b = jnp.where(jnp.arange(N_DP) == full_b, VB, column_b)
    return jnp.stack([column_a, column_b], axis=1).astype(jnp.int32)


def levels(stream_key, extent, shards, least, largest):
    level = 1.0
    for position, blocks in shards:
        steps = jax.random.uniform(jax.random.fold_in(jax.random.fold_in(stream_key, 6), position), (blocks,), jnp.float32, least / len(shards), largest / len(shards))
        level = level * jnp.repeat(jnp.exp(steps), extent[position] // blocks).reshape((-1,) + (1,) * (len(extent) - 1 - position))
    return level


def gaussian(key, dims, deviation, reach, cuts=(), held_as=jnp.bfloat16):
    entries = deviation * jax.random.normal(key, dims, jnp.float32)
    if cuts:
        entries = entries * levels(key, dims, cuts, -0.22, 0.18)
    return jnp.clip(entries, -reach, reach).astype(held_as)


def setup_inputs(seed: int = 0) -> dict:
    key_of = jax.random.split(jax.random.key(seed), 27)
    return {
        "input_a": draw_input_a(jax.random.fold_in(key_of[26], 71), 0),
        "input_b": draw_input_b(jax.random.fold_in(key_of[26], 71), 0),
        "live_views": draw_live_views(jax.random.fold_in(key_of[26], 71), 0),
        "reduce_one": gaussian(key_of[3], (C_IN, C_MID), C_IN ** -0.5, 0.1875),
        "spatial_one": gaussian(key_of[4], (C_MID, 3, 3, C_MID), (9 * C_MID) ** -0.5, 0.125),
        "expand_one": gaussian(key_of[5], (C_MID, C_IN), C_MID ** -0.5, 0.375),
        "reduce_two": gaussian(key_of[6], (C_IN, C_MID2), C_IN ** -0.5, 0.1875),
        "spatial_two": gaussian(key_of[7], (C_MID2, 3, 3, C_MID2), (9 * C_MID2) ** -0.5, 0.09375),
        "expand_two": gaussian(key_of[8], (C_MID2, C_OUT), C_MID2 ** -0.5, 0.25),
        "shortcut_two": gaussian(key_of[9], (C_IN, C_OUT), C_IN ** -0.5, 0.1875),
        "gain_narrow": jnp.clip(jax.random.uniform(key_of[10], (C_MID,), jnp.float32, 0.5, 1.5), 0.5, 1.5),
        "bias_narrow": jnp.clip(jax.random.uniform(key_of[11], (C_MID,), jnp.float32, -0.5, 0.5), -0.5, 0.5),
        "gain_spatial": jnp.clip(jax.random.uniform(key_of[12], (C_MID,), jnp.float32, 0.5, 1.5), 0.5, 1.5),
        "bias_spatial": jnp.clip(jax.random.uniform(key_of[13], (C_MID,), jnp.float32, -0.5, 0.5), -0.5, 0.5),
        "gain_widened": jnp.clip(jax.random.uniform(key_of[14], (C_IN,), jnp.float32, 0.5, 1.5), 0.5, 1.5),
        "bias_widened": jnp.clip(jax.random.uniform(key_of[15], (C_IN,), jnp.float32, -0.5, 0.5), -0.5, 0.5),
        "gain_squeeze": jnp.clip(jax.random.uniform(key_of[16], (C_MID2,), jnp.float32, 0.5, 1.5), 0.5, 1.5),
        "bias_squeeze": jnp.clip(jax.random.uniform(key_of[17], (C_MID2,), jnp.float32, -0.5, 0.5), -0.5, 0.5),
        "gain_strided": jnp.clip(jax.random.uniform(key_of[18], (C_MID2,), jnp.float32, 0.5, 1.5), 0.5, 1.5),
        "bias_strided": jnp.clip(jax.random.uniform(key_of[19], (C_MID2,), jnp.float32, -0.5, 0.5), -0.5, 0.5),
        "gain_output": jnp.clip(jax.random.uniform(key_of[20], (C_OUT,), jnp.float32, 0.5, 1.5), 0.5, 1.5),
        "bias_output": jnp.clip(jax.random.uniform(key_of[21], (C_OUT,), jnp.float32, -0.5, 0.5), -0.5, 0.5),
        "gain_shortcut": jnp.clip(jax.random.uniform(key_of[22], (C_OUT,), jnp.float32, 0.5, 1.5), 0.5, 1.5),
        "bias_shortcut": jnp.clip(jax.random.uniform(key_of[23], (C_OUT,), jnp.float32, -0.5, 0.5), -0.5, 0.5),
        "cotangent_a": gaussian(key_of[24], (HPA // 2, VIEWS_A, WA // 2, C_OUT), 1.0, 6.0, ((0, 4), (1, 8))),
        "cotangent_b": gaussian(key_of[25], (HPB // 2, VIEWS_B, WB // 2, C_OUT), 1.0, 6.0, ((0, 4), (1, 8))),
    }


@jax.custom_vjp
def low(v):
    return lax.optimization_barrier(v.astype(jnp.bfloat16)).astype(jnp.float32)

@jax.custom_vjp
def low_back(v):
    return v

def low_keep(v):
    return (low(v), None)

def low_pass(kept, grad):
    return (grad,)

def back_keep(v):
    return (v, None)

def back_low(kept, grad):
    return (low(grad),)
low.defvjp(low_keep, low_pass)
low_back.defvjp(back_keep, back_low)
EPS = 1e-05
HIGH = lax.Precision.HIGHEST

def silu(value):
    return value * jax.nn.sigmoid(value)

def group_mask(live_views, group, slots, height, rows_total):
    views = live_views.shape[0] * slots
    owner = jnp.arange(views) // slots
    slot = jnp.arange(views) - owner * slots
    live = live_views[:, group][owner]
    view_ok = slot < live
    row_ok = jnp.arange(rows_total) < height
    return (row_ok[:, None] & view_ok[None, :]).astype(jnp.float32)[:, :, None, None]

def pointwise(acts, matrix):
    return jnp.einsum('hvwc,cd->hvwd', acts, matrix, precision=HIGH)

def conv_grid(acts, weight, stride, padding):
    lhs = jnp.transpose(acts, (1, 0, 2, 3))
    kernel = jnp.transpose(weight, (1, 2, 0, 3))
    out = lax.conv_general_dilated(lhs, kernel, (stride, stride), padding, dimension_numbers=('NHWC', 'HWIO', 'NHWC'), precision=HIGH)
    return jnp.transpose(out, (1, 0, 2, 3))

def batch_norm(parts, masks, gain, bias, count):
    total = lax.optimization_barrier(jnp.sum(parts[0] * masks[0], axis=(0, 1, 2))) + lax.optimization_barrier(jnp.sum(parts[1] * masks[1], axis=(0, 1, 2)))
    square = lax.optimization_barrier(jnp.sum(parts[0] * parts[0] * masks[0], axis=(0, 1, 2))) + lax.optimization_barrier(jnp.sum(parts[1] * parts[1] * masks[1], axis=(0, 1, 2)))
    mean = total / count
    scale = lax.rsqrt(square / count - mean * mean + EPS)
    return [(value - mean) * scale * gain + bias for value in parts]

def reference(input_a, input_b, live_views, reduce_one, spatial_one, expand_one, reduce_two, spatial_two, expand_two, shortcut_two, gain_narrow, bias_narrow, gain_spatial, bias_spatial, gain_widened, bias_widened, gain_squeeze, bias_squeeze, gain_strided, bias_strided, gain_output, bias_output, gain_shortcut, bias_shortcut, cotangent_a, cotangent_b):
    masks = (group_mask(live_views, 0, VA, HA, input_a.shape[0]), group_mask(live_views, 1, VB, HB, input_b.shape[0]))
    halves = (group_mask(live_views, 0, VA, (HA + 1) // 2, input_a.shape[0] // 2), group_mask(live_views, 1, VB, (HB + 1) // 2, input_b.shape[0] // 2))
    totals = lax.optimization_barrier(jnp.sum(live_views, axis=0)).astype(jnp.float32)
    full_count = HA * WA * totals[0] + HB * WB * totals[1]
    half_count = (HA + 1) // 2 * ((WA + 1) // 2) * totals[0] + (HB + 1) // 2 * ((WB + 1) // 2) * totals[1]

    def forward(inputs, weights, gains, biases):
        first_reduce, first_spatial, first_expand, second_reduce, second_spatial, second_expand, second_short = weights
        pre_one = [low_back(pointwise(value, first_reduce)) for value in inputs]
        normed = batch_norm(pre_one, masks, gains[0], biases[0], full_count)
        hidden_one = [low(silu(value) * mask) for value, mask in zip(normed, masks)]
        pre_two = [low_back(conv_grid(value, first_spatial, 1, ((1, 1), (1, 1)))) for value in hidden_one]
        normed = batch_norm(pre_two, masks, gains[1], biases[1], full_count)
        hidden_two = [low(silu(value) * mask) for value, mask in zip(normed, masks)]
        pre_three = [low_back(pointwise(value, first_expand)) for value in hidden_two]
        normed = batch_norm(pre_three, masks, gains[2], biases[2], full_count)
        feed = [low(silu(value + source) * mask) for value, source, mask in zip(normed, inputs, masks)]
        pre_four = [low_back(pointwise(value, second_reduce)) for value in feed]
        normed = batch_norm(pre_four, masks, gains[3], biases[3], full_count)
        hidden_four = [low(silu(value) * mask) for value, mask in zip(normed, masks)]
        pre_five = [low_back(conv_grid(value, second_spatial, 2, ((1, 0), (1, 0)))) for value in hidden_four]
        normed = batch_norm(pre_five, halves, gains[4], biases[4], half_count)
        hidden_five = [low(silu(value) * mask) for value, mask in zip(normed, halves)]
        pre_six = [low_back(pointwise(value, second_expand)) for value in hidden_five]
        pre_short = [low_back(pointwise(value[0::2, :, 0::2], second_short)) for value in feed]
        main_branch = batch_norm(pre_six, halves, gains[5], biases[5], half_count)
        side_branch = batch_norm(pre_short, halves, gains[6], biases[6], half_count)
        return (silu(main_branch[0] + side_branch[0]) * halves[0], silu(main_branch[1] + side_branch[1]) * halves[1])
    inputs = (input_a.astype(jnp.float32), input_b.astype(jnp.float32))
    weights = tuple((value.astype(jnp.float32) for value in (reduce_one, spatial_one, expand_one, reduce_two, spatial_two, expand_two, shortcut_two)))
    gains = (gain_narrow, gain_spatial, gain_widened, gain_squeeze, gain_strided, gain_output, gain_shortcut)
    biases = (bias_narrow, bias_spatial, bias_widened, bias_squeeze, bias_strided, bias_output, bias_shortcut)
    outputs, pullback = jax.vjp(forward, inputs, weights, gains, biases)
    grad_inputs, grad_weights, grad_gains, grad_biases = pullback((cotangent_a.astype(jnp.float32), cotangent_b.astype(jnp.float32)))
    return (outputs[0].astype(jnp.bfloat16), outputs[1].astype(jnp.bfloat16), grad_inputs[0].astype(jnp.bfloat16), grad_inputs[1].astype(jnp.bfloat16), grad_weights[0], grad_weights[1], grad_weights[2], grad_weights[3], grad_weights[4], grad_weights[5], grad_weights[6], grad_gains[0], grad_biases[0], grad_gains[1], grad_biases[1], grad_gains[2], grad_biases[2], grad_gains[3], grad_biases[3], grad_gains[4], grad_biases[4], grad_gains[5], grad_biases[5], grad_gains[6], grad_biases[6])
```

```python
import functools
import math

import jax
import jax.numpy as jnp
from jax import lax
from jax.experimental import pallas as pl
from jax.experimental.pallas import tpu as pltpu
from jax.sharding import PartitionSpec as P

MESH = pl.DeviceIdType.MESH

HA = 14
WA = 14
HB = 10
WB = 10


EPS = 1e-05
TAPS = ((0, 0), (0, 1), (1, 0))

def greet_all(spans):
    d_size, r_size = spans
    total = d_size * r_size
    barrier = pltpu.get_barrier_semaphore()
    me = lax.axis_index("dp") * r_size + lax.axis_index("rows")

    def greet(step, carry):
        other = lax.rem(me + step, total)
        pl.semaphore_signal(
            barrier,
            inc=1,
            device_id=(other // r_size, lax.rem(other, r_size)),
            device_id_type=MESH,
        )
        return carry

    lax.fori_loop(1, total, greet, 0)
    pl.semaphore_wait(barrier, total - 1)


def sum_kernel(spans, in_ref, out_ref, near, mid, far, near_send, near_recv, far_send, far_recv):
    d_size, r_size = spans
    d, r = lax.axis_index("dp"), lax.axis_index("rows")
    greet_all(spans)
    for step in range(1, r_size):
        pltpu.make_async_remote_copy(
            in_ref,
            near.at[r],
            near_send,
            near_recv,
            device_id=(d, lax.rem(r + step, r_size)),
            device_id_type=MESH,
        ).start()
    near[r] = in_ref[...]
    several = near.at[0 : r_size - 1]
    pltpu.make_async_copy(several, several, near_recv).wait()
    mid[...] = jnp.sum(near[...], axis=0)
    for step in range(1, d_size):
        pltpu.make_async_remote_copy(
            mid,
            far.at[d],
            far_send,
            far_recv,
            device_id=(lax.rem(d + step, d_size), r),
            device_id_type=MESH,
        ).start()
    far[d] = mid[...]
    many = far.at[0 : d_size - 1]
    pltpu.make_async_copy(many, many, far_recv).wait()
    pltpu.make_async_copy(several, several, near_send).wait()
    pltpu.make_async_copy(many, many, far_send).wait()
    out_ref[...] = jnp.sum(far[...], axis=0)


def summed(values):
    spans = (lax.axis_size("dp"), lax.axis_size("rows"))
    flat = jnp.stack(values)
    dma = pltpu.SemaphoreType.DMA
    out = pl.pallas_call(
        functools.partial(sum_kernel, spans),
        out_shape=jax.ShapeDtypeStruct(flat.shape, flat.dtype),
        in_specs=[pl.BlockSpec(memory_space=pltpu.VMEM)],
        out_specs=pl.BlockSpec(memory_space=pltpu.VMEM),
        scratch_shapes=[
            pltpu.VMEM((spans[1],) + flat.shape, flat.dtype),
            pltpu.VMEM(flat.shape, flat.dtype),
            pltpu.VMEM((spans[0],) + flat.shape, flat.dtype),
            dma,
            dma,
            dma,
            dma,
        ],
        compiler_params=pltpu.CompilerParams(
            collective_id=flat.size // 512,
            has_side_effects=True,
            vmem_limit_bytes=32 * 2**20,
        ),
    )(flat)
    return tuple(out[i] for i in range(len(values)))


def shortened(value):
    return jax.tree.map(lambda a: a.astype(jnp.bfloat16) if a.dtype == jnp.float32 else a, value)


def padded_2(cells, sides, width):
    for axis, dim in sides:
        count = lax.axis_size(axis)
        ends = count - 1
        head = lax.slice_in_dim(cells, 0, width, axis=dim)
        tail = lax.slice_in_dim(cells, cells.shape[dim] - width, cells.shape[dim], axis=dim)
        cells = jnp.concatenate(
            [
                lax.ppermute(tail, axis, [(i, (i + 1) % count) for i in range(ends)]),
                cells,
                lax.ppermute(head, axis, [((i + 1) % count, i) for i in range(ends)]),
            ],
            axis=dim,
        )
    return cells


def passed_along(block, axis, distance):
    devices = range(lax.axis_size(axis))
    route = [(i - distance, i) for i in devices if i - distance in devices]
    return lax.ppermute(block, axis, route)


def silu(value):
    return value * jax.nn.sigmoid(value)


def silu_slope(value):
    sigma = jax.nn.sigmoid(value)
    return sigma * (1.0 + value * (1.0 - sigma))


def apply_matrix(acts, matrix):
    flat = acts.reshape(-1, acts.shape[-1])
    out = jnp.dot(flat, matrix, preferred_element_type=jnp.float32)
    return out.reshape(acts.shape[:-1] + (matrix.shape[1],))


def apply_transpose(grads, matrix):
    flat = grads.reshape(-1, grads.shape[-1])
    out = lax.dot_general(
        flat, matrix, (((1,), (1,)), ((), ())), preferred_element_type=jnp.float32
    )
    return out.reshape(grads.shape[:-1] + (matrix.shape[0],))


def outer_sum(acts, grads):
    return lax.dot_general(
        acts.reshape(-1, acts.shape[-1]),
        grads.reshape(-1, grads.shape[-1]),
        (((0,), (0,)), ((), ())),
        preferred_element_type=jnp.float32,
    )


def strip_mask(live_views, group, rows, views, height):
    column = live_views[:, group]
    live = jnp.sum(jnp.where(jnp.arange(column.shape[0]) == lax.axis_index("dp"), column, 0))
    view_ok = jnp.arange(views) < live
    row_ok = lax.axis_index("rows") * rows + jnp.arange(rows) < height
    return (row_ok[:, None] & view_ok[None, :]).astype(jnp.float32)[:, :, None, None]


def masked_sums(parts, masks):
    total = 0.0
    square = 0.0
    for value, mask in zip(parts, masks):
        kept = value * mask
        total = total + jnp.sum(kept, axis=(0, 1, 2))
        square = square + jnp.sum(kept * value, axis=(0, 1, 2))
    return (total, square)


def shared_sums(parts, masks):
    total, square = masked_sums(parts, masks)
    return summed((total, square))


def standardize(parts, total, square, count):
    mean = total / count
    scale = lax.rsqrt(square / count - mean * mean + EPS)
    return ([(value - mean) * scale for value in parts], scale)


def slope_sums(slopes, normed):
    first = 0.0
    second = 0.0
    for slope, unit in zip(slopes, normed):
        first = first + jnp.sum(slope, axis=(0, 1, 2))
        second = second + jnp.sum(slope * unit, axis=(0, 1, 2))
    return (first, second)


def shared_grads(slopes, normed):
    first, second = slope_sums(slopes, normed)
    return summed((first, second))


def norm_back(slopes, normed, masks, scale, gain, first, second, count):
    factor = scale * gain
    return [
        (factor * (slope - first / count - unit * (second / count)) * mask).astype(jnp.bfloat16)
        for slope, unit, mask in zip(slopes, normed, masks)
    ]


def rim_pack(parts):
    return jnp.concatenate(
        [jnp.stack([value[0].reshape(-1), value[-1].reshape(-1)]) for value in parts], axis=1
    )


def rim_split(flat, parts):
    pieces = []
    start = 0
    for value in parts:
        size = value[0].size
        pieces.append(flat[start : start + size].reshape(value.shape[1:]))
        start = start + size
    return pieces


def spatial_same(padded, weight):
    rows = padded.shape[0] - 2
    width = padded.shape[2]
    wide = jnp.pad(padded, ((0, 0), (0, 0), (1, 1), (0, 0)))
    total = 0.0
    for across in range(3):
        for along in range(3):
            total = total + apply_matrix(
                wide[across : across + rows, :, along : along + width], weight[:, across, along]
            )
    return (total, wide)


def spatial_same_back(wide, grads, weight):
    rows = grads.shape[0]
    width = grads.shape[2]
    weight_grad = jnp.stack(
        [
            jnp.stack(
                [
                    outer_sum(wide[across : across + rows, :, along : along + width], grads)
                    for along in range(3)
                ],
                axis=1,
            )
            for across in range(3)
        ],
        axis=1,
    )
    back = 0.0
    for across in range(3):
        for along in range(3):
            term = apply_transpose(grads, weight[:, across, along])
            back = back + jnp.pad(term, ((across, 2 - across), (0, 0), (along, 2 - along), (0, 0)))
    return (weight_grad, back[:, :, 1 : width + 1])


def strided_grid(acts, above):
    rows, views, width, chans = acts.shape
    full = jnp.concatenate([above[None], acts, jnp.zeros_like(above)[None]], axis=0)
    full = jnp.pad(full, ((0, 0), (0, 0), (1, 1), (0, 0)))
    return full.reshape(rows // 2 + 1, 2, views, width // 2 + 1, 2, chans)


def strided_forward(grid, weight):
    out_rows = grid.shape[0] - 1
    out_cols = grid.shape[3] - 1
    total = 0.0
    for across in range(3):
        lead, row_bit = TAPS[across]
        for along in range(3):
            side, col_bit = TAPS[along]
            total = total + apply_matrix(
                grid[lead : lead + out_rows, row_bit, :, side : side + out_cols, col_bit],
                weight[:, across, along],
            )
    return total


def strided_back(grid, grads, weight):
    out_rows = grads.shape[0]
    out_cols = grads.shape[2]
    rows_grad = []
    blocks = [[0.0, 0.0], [0.0, 0.0]]
    for across in range(3):
        lead, row_bit = TAPS[across]
        cols_grad = []
        for along in range(3):
            side, col_bit = TAPS[along]
            cols_grad.append(
                outer_sum(
                    grid[lead : lead + out_rows, row_bit, :, side : side + out_cols, col_bit], grads
                )
            )
            term = apply_transpose(grads, weight[:, across, along])
            blocks[row_bit][col_bit] = blocks[row_bit][col_bit] + jnp.pad(
                term, ((lead, 1 - lead), (0, 0), (side, 1 - side), (0, 0))
            )
        rows_grad.append(jnp.stack(cols_grad, axis=1))
    weight_grad = jnp.stack(rows_grad, axis=1)
    whole = jnp.stack([jnp.stack(blocks[bit], axis=3) for bit in range(2)], axis=1)
    return (
        weight_grad,
        whole.reshape(2 * out_rows + 2, grads.shape[1], 2 * out_cols + 2, whole.shape[-1]),
    )


def spread_even(term):
    count, views, cols, chans = term.shape
    spaced = jnp.stack([term, jnp.zeros_like(term)], axis=3).reshape(count, views, 2 * cols, chans)
    return jnp.stack([spaced, jnp.zeros_like(spaced)], axis=1).reshape(
        2 * count, views, 2 * cols, chans
    )


def spread_grads(grads):
    partial_sums = jax.tree.map(
        lambda part: part.astype(jnp.float32),
        lax.psum_scatter(shortened(grads), "dp", scatter_dimension=0, tiled=True),
    )
    return jax.tree.map(
        lambda part: part.astype(jnp.float32),
        lax.psum_scatter(shortened(partial_sums), "rows", scatter_dimension=0, tiled=True),
    )


def on_device(
    input_a,
    input_b,
    live_views,
    reduce_one,
    spatial_one,
    expand_one,
    reduce_two,
    spatial_two,
    expand_two,
    shortcut_two,
    gain_narrow,
    bias_narrow,
    gain_spatial,
    bias_spatial,
    gain_widened,
    bias_widened,
    gain_squeeze,
    bias_squeeze,
    gain_strided,
    bias_strided,
    gain_output,
    bias_output,
    gain_shortcut,
    bias_shortcut,
    cotangent_a,
    cotangent_b,
):
    inputs = [input_a, input_b]
    heights = [HA, HB]
    masks = [
        strip_mask(
            live_views, group, inputs[group].shape[0], inputs[group].shape[1], heights[group]
        )
        for group in range(2)
    ]
    halves = [
        strip_mask(
            live_views,
            group,
            inputs[group].shape[0] // 2,
            inputs[group].shape[1],
            (heights[group] + 1) // 2,
        )
        for group in range(2)
    ]
    totals = jnp.sum(live_views, axis=0).astype(jnp.float32)
    full_count = HA * WA * totals[0] + HB * WB * totals[1]
    half_count = (HA + 1) // 2 * ((WA + 1) // 2) * totals[0] + (HB + 1) // 2 * (
        (WB + 1) // 2
    ) * totals[1]
    pre_one = [apply_matrix(value, reduce_one) for value in inputs]
    total, square = shared_sums(pre_one, masks)
    unit_one, scale_one = standardize(pre_one, total, square, full_count)
    act_one = [unit * gain_narrow + bias_narrow for unit in unit_one]
    hidden_one = [(silu(value) * mask).astype(jnp.bfloat16) for value, mask in zip(act_one, masks)]
    beside_all = padded_2(rim_pack(hidden_one), (("rows", 0),), 1)
    above_rows = rim_split(beside_all[0], hidden_one)
    below_rows = rim_split(beside_all[3], hidden_one)
    spatial_pairs = [
        spatial_same(jnp.concatenate([upper[None], value, lower[None]], axis=0), spatial_one)
        for upper, value, lower in zip(above_rows, hidden_one, below_rows)
    ]
    pre_two = [pair[0] for pair in spatial_pairs]
    wide_one = [pair[1] for pair in spatial_pairs]
    total, square = shared_sums(pre_two, masks)
    unit_two, scale_two = standardize(pre_two, total, square, full_count)
    act_two = [unit * gain_spatial + bias_spatial for unit in unit_two]
    hidden_two = [(silu(value) * mask).astype(jnp.bfloat16) for value, mask in zip(act_two, masks)]
    pre_three = [apply_matrix(value, expand_one) for value in hidden_two]
    total, square = shared_sums(pre_three, masks)
    unit_three, scale_three = standardize(pre_three, total, square, full_count)
    sum_one = [
        unit * gain_widened + bias_widened + source.astype(jnp.float32)
        for unit, source in zip(unit_three, inputs)
    ]
    feed = [(silu(value) * mask).astype(jnp.bfloat16) for value, mask in zip(sum_one, masks)]
    pre_four = [apply_matrix(value, reduce_two) for value in feed]
    total, square = shared_sums(pre_four, masks)
    unit_four, scale_four = standardize(pre_four, total, square, full_count)
    act_four = [unit * gain_squeeze + bias_squeeze for unit in unit_four]
    hidden_four = [
        (silu(value) * mask).astype(jnp.bfloat16) for value, mask in zip(act_four, masks)
    ]
    last_rows = jnp.concatenate([value[-1].reshape(-1) for value in hidden_four])
    from_above = rim_split(passed_along(last_rows, "rows", 1), hidden_four)
    grids = [strided_grid(value, upper) for value, upper in zip(hidden_four, from_above)]
    pre_five = [strided_forward(grid, spatial_two) for grid in grids]
    total, square = shared_sums(pre_five, halves)
    unit_five, scale_five = standardize(pre_five, total, square, half_count)
    act_five = [unit * gain_strided + bias_strided for unit in unit_five]
    hidden_five = [
        (silu(value) * mask).astype(jnp.bfloat16) for value, mask in zip(act_five, halves)
    ]
    pre_six = [apply_matrix(value, expand_two) for value in hidden_five]
    short_in = [value[0::2, :, 0::2] for value in feed]
    pre_short = [apply_matrix(value, shortcut_two) for value in short_in]
    total_main, square_main, total_side, square_side = summed(
        masked_sums(pre_six, halves) + masked_sums(pre_short, halves)
    )
    unit_six, scale_six = standardize(pre_six, total_main, square_main, half_count)
    unit_short, scale_short = standardize(pre_short, total_side, square_side, half_count)
    sum_two = [
        main * gain_output + bias_output + (side * gain_shortcut + bias_shortcut)
        for main, side in zip(unit_six, unit_short)
    ]
    block_out = [(silu(value) * mask).astype(jnp.bfloat16) for value, mask in zip(sum_two, halves)]
    cotangents = [cotangent_a, cotangent_b]
    slope_two = [
        cotangent.astype(jnp.float32) * mask * silu_slope(value)
        for cotangent, mask, value in zip(cotangents, halves, sum_two)
    ]
    first, second = slope_sums(slope_two, unit_six)
    third = slope_sums(slope_two, unit_short)[1]
    grad_bias_output, grad_gain_output, grad_gain_shortcut = summed((first, second, third))
    grad_bias_shortcut = grad_bias_output
    grad_pre_six = norm_back(
        slope_two,
        unit_six,
        halves,
        scale_six,
        gain_output,
        grad_bias_output,
        grad_gain_output,
        half_count,
    )
    grad_pre_short = norm_back(
        slope_two,
        unit_short,
        halves,
        scale_short,
        gain_shortcut,
        grad_bias_shortcut,
        grad_gain_shortcut,
        half_count,
    )
    grad_expand_two = outer_sum(hidden_five[0], grad_pre_six[0]) + outer_sum(
        hidden_five[1], grad_pre_six[1]
    )
    grad_shortcut_two = outer_sum(short_in[0], grad_pre_short[0]) + outer_sum(
        short_in[1], grad_pre_short[1]
    )
    slope_five = [
        apply_transpose(grad, expand_two) * mask * silu_slope(value)
        for grad, mask, value in zip(grad_pre_six, halves, act_five)
    ]
    grad_bias_strided, grad_gain_strided = shared_grads(slope_five, unit_five)
    grad_pre_five = norm_back(
        slope_five,
        unit_five,
        halves,
        scale_five,
        gain_strided,
        grad_bias_strided,
        grad_gain_strided,
        half_count,
    )
    strided_pairs = [
        strided_back(grid, grad, spatial_two) for grid, grad in zip(grids, grad_pre_five)
    ]
    grad_spatial_two = strided_pairs[0][0] + strided_pairs[1][0]
    wholes = [pair[1] for pair in strided_pairs]
    widths = [value.shape[2] for value in hidden_four]
    sent_up = jnp.concatenate(
        [whole[0, :, 1 : width + 1].reshape(-1) for whole, width in zip(wholes, widths)]
    )
    from_below = rim_split(
        passed_along(sent_up.astype(jnp.bfloat16), "rows", -1).astype(sent_up.dtype), hidden_four
    )
    grad_four = []
    for whole, width, extra, value in zip(wholes, widths, from_below, hidden_four):
        local = whole[1 : value.shape[0] + 1, :, 1 : width + 1]
        grad_four.append(local.at[-1].add(extra))
    slope_four = [
        grad * mask * silu_slope(value) for grad, mask, value in zip(grad_four, masks, act_four)
    ]
    grad_bias_squeeze, grad_gain_squeeze = shared_grads(slope_four, unit_four)
    grad_pre_four = norm_back(
        slope_four,
        unit_four,
        masks,
        scale_four,
        gain_squeeze,
        grad_bias_squeeze,
        grad_gain_squeeze,
        full_count,
    )
    grad_reduce_two = outer_sum(feed[0], grad_pre_four[0]) + outer_sum(feed[1], grad_pre_four[1])
    grad_feed = [
        apply_transpose(grad, reduce_two) + spread_even(apply_transpose(side, shortcut_two))
        for grad, side in zip(grad_pre_four, grad_pre_short)
    ]
    second_block = spread_grads(
        (grad_reduce_two, grad_spatial_two, grad_expand_two, grad_shortcut_two)
    )
    slope_three = [
        grad * mask * silu_slope(value) for grad, mask, value in zip(grad_feed, masks, sum_one)
    ]
    grad_bias_widened, grad_gain_widened = shared_grads(slope_three, unit_three)
    grad_pre_three = norm_back(
        slope_three,
        unit_three,
        masks,
        scale_three,
        gain_widened,
        grad_bias_widened,
        grad_gain_widened,
        full_count,
    )
    grad_expand_one = outer_sum(hidden_two[0], grad_pre_three[0]) + outer_sum(
        hidden_two[1], grad_pre_three[1]
    )
    slope_spatial = [
        apply_transpose(grad, expand_one) * mask * silu_slope(value)
        for grad, mask, value in zip(grad_pre_three, masks, act_two)
    ]
    grad_bias_spatial, grad_gain_spatial = shared_grads(slope_spatial, unit_two)
    grad_pre_two = norm_back(
        slope_spatial,
        unit_two,
        masks,
        scale_two,
        gain_spatial,
        grad_bias_spatial,
        grad_gain_spatial,
        full_count,
    )
    same_pairs = [
        spatial_same_back(wide, grad, spatial_one) for wide, grad in zip(wide_one, grad_pre_two)
    ]
    grad_spatial_one = same_pairs[0][0] + same_pairs[1][0]
    backs = [pair[1] for pair in same_pairs]
    returned = padded_2(rim_pack(backs).astype(jnp.bfloat16), (("rows", 0),), 1).astype(jnp.float32)
    from_upper = rim_split(returned[0], hidden_one)
    from_lower = rim_split(returned[3], hidden_one)
    grad_one = [
        back[1:-1].at[0].add(upper).at[-1].add(lower)
        for back, upper, lower in zip(backs, from_upper, from_lower)
    ]
    slope_narrow = [
        grad * mask * silu_slope(value) for grad, mask, value in zip(grad_one, masks, act_one)
    ]
    grad_bias_narrow, grad_gain_narrow = shared_grads(slope_narrow, unit_one)
    grad_pre_one = norm_back(
        slope_narrow,
        unit_one,
        masks,
        scale_one,
        gain_narrow,
        grad_bias_narrow,
        grad_gain_narrow,
        full_count,
    )
    grad_reduce_one = outer_sum(inputs[0], grad_pre_one[0]) + outer_sum(inputs[1], grad_pre_one[1])
    grad_inputs = [
        (slope + apply_transpose(grad, reduce_one)).astype(jnp.bfloat16)
        for slope, grad in zip(slope_three, grad_pre_one)
    ]
    first_block = spread_grads((grad_reduce_one, grad_spatial_one, grad_expand_one))
    return (
        block_out[0],
        block_out[1],
        grad_inputs[0],
        grad_inputs[1],
        first_block[0],
        first_block[1],
        first_block[2],
        second_block[0],
        second_block[1],
        second_block[2],
        second_block[3],
        grad_gain_narrow,
        grad_bias_narrow,
        grad_gain_spatial,
        grad_bias_spatial,
        grad_gain_widened,
        grad_bias_widened,
        grad_gain_squeeze,
        grad_bias_squeeze,
        grad_gain_strided,
        grad_bias_strided,
        grad_gain_output,
        grad_bias_output,
        grad_gain_shortcut,
        grad_bias_shortcut,
    )


def solution(mesh):
    placed = (
        P("rows", "dp", None, None),
        P("rows", "dp", None, None),
        P(),
        P(),
        P(),
        P(),
        P(),
        P(),
        P(),
        P(),
        P(),
        P(),
        P(),
        P(),
        P(),
        P(),
        P(),
        P(),
        P(),
        P(),
        P(),
        P(),
        P(),
        P(),
        P("rows", "dp", None, None),
        P("rows", "dp", None, None),
    )
    return jax.shard_map(
        on_device,
        mesh=mesh,
        in_specs=placed,
        out_specs=(
            P("rows", "dp", None, None),
            P("rows", "dp", None, None),
            P("rows", "dp", None, None),
            P("rows", "dp", None, None),
            P(("dp", "rows"), None),
            P(("dp", "rows"), None, None, None),
            P(("dp", "rows"), None),
            P(("dp", "rows"), None),
            P(("dp", "rows"), None, None, None),
            P(("dp", "rows"), None),
            P(("dp", "rows"), None),
            P(),
            P(),
            P(),
            P(),
            P(),
            P(),
            P(),
            P(),
            P(),
            P(),
            P(),
            P(),
            P(),
            P(),
        ),
        check_vma=False,
    )
```

```python
import functools
from types import SimpleNamespace

import jax
import jax.numpy as jnp
from jax import lax
from jax.experimental import pallas as pl
from jax.experimental.pallas import tpu as pltpu
from jax.sharding import PartitionSpec as P

MESH = pl.DeviceIdType.MESH
F32 = jnp.float32
BF16 = jnp.bfloat16

HA = 14
WA = 14
HB = 10
WB = 10

EPS = 1e-05
LEAF = 1024
NARROW, SPATIAL, WIDENED, SQUEEZE, STRIDED, OUTPUT, SHORTCUT = range(7)
NEAR = (0, 1, 2, 3, 4)
FAR = (0, 2, 3, 4, 1)
BITS = 5
SHARDS = 1 << BITS
G_REDUCE_ONE, G_SPATIAL_ONE, G_EXPAND_ONE, G_REDUCE_TWO, G_SPATIAL_TWO, G_EXPAND_TWO, G_SHORTCUT_TWO = range(7)
GRADS = (
    (32, 256, NEAR),
    (144, 128, FAR),
    (16, 512, NEAR),
    (32, 512, FAR),
    (144, 512, NEAR),
    (16, 2048, FAR),
    (32, 2048, FAR),
)
(
    AT_ONE,
    AT_TWO,
    AT_THREE,
    AT_FOUR,
    AT_FIVE,
    AT_SHORT,
    AT_SIX,
    AT_SEVEN,
    AT_EIGHT,
    AT_NINE,
    AT_TEN,
    AT_ELEVEN,
    AT_TWELVE,
) = range(13)
SUMS = (
    (2, 256),
    (2, 256),
    (2, 1024),
    (2, 512),
    (2, 512),
    (2, 2048),
    (2, 2048),
    (3, 2048),
    (2, 512),
    (2, 512),
    (2, 1024),
    (2, 256),
    (2, 256),
)


def mm(left, right):
    return lax.dot_general(left, right, (((1,), (0,)), ((), ())), preferred_element_type=F32)


def mm_nt(left, right):
    return lax.dot_general(left, right, (((1,), (1,)), ((), ())), preferred_element_type=F32)


def mm_tn(left, right):
    return lax.dot_general(left, right, (((0,), (0,)), ((), ())), preferred_element_type=F32)


def sigmoid(value):
    return 0.5 + 0.5 * jnp.tanh(0.5 * value)


def slope_of(value):
    sigma = sigmoid(value)
    return sigma * (1.0 + value * (1.0 - sigma))


def flat(block):
    return block.reshape(-1, block.shape[-1])


def col_sum(value):
    return jnp.sum(value, axis=0, keepdims=True)


def wide(mask, lanes):
    return jnp.concatenate([mask] * (lanes // 128), axis=1)


def loop(count, body, init=None):
    if init is None:

        def plain(step, carry):
            body(step)
            return carry

        return lax.fori_loop(0, count, plain, 0)
    return lax.fori_loop(0, count, body, init)


def bit_of(number, bit):
    return lax.rem(number // (1 << bit), 2)


class Kernel:
    def __init__(self, sizes, refs):
        self.d_size, self.r_size, self.live_a, self.live_b = sizes
        self.total = self.d_size * self.r_size
        self.__dict__.update(refs)
        self.d = lax.axis_index("dp")
        self.r = lax.axis_index("rows")
        self.me = self.d * self.r_size + self.r
        self.low = (self.total // SHARDS).bit_length() - 1
        self.shard = self.me // (1 << self.low)
        self.r_bits = self.r_size.bit_length() - 1


    def device(self, number):
        return (number // self.r_size, lax.rem(number, self.r_size))

    def greet(self):
        barrier = pltpu.get_barrier_semaphore()

        def one(step):
            pl.semaphore_signal(
                barrier,
                inc=1,
                device_id=self.device(lax.rem(self.me + step + 1, self.total)),
                device_id_type=MESH,
            )

        loop(self.total - 1, one)

    def greeted(self):
        pl.semaphore_wait(pltpu.get_barrier_semaphore(), self.total - 1)

    def direct(self, name):
        return self.sums[name].direct

    def sum_start(self, name, vectors):
        s = self.sums[name]
        for i, vector in enumerate(vectors):
            s.pay[i : i + 1, :] = vector
        if s.direct:

            def send(step):
                pltpu.make_async_remote_copy(
                    s.pay,
                    s.near.at[self.me],
                    s.sems.at[0],
                    s.sems.at[1],
                    device_id=self.device(lax.rem(self.me + step + 1, self.total)),
                    device_id_type=MESH,
                ).start()

            loop(self.total - 1, send)
            s.near[self.me] = s.pay[...]
        else:
            for step in range(1, self.r_size):
                pltpu.make_async_remote_copy(
                    s.pay,
                    s.near.at[self.r],
                    s.sems.at[0],
                    s.sems.at[1],
                    device_id=(self.d, lax.rem(self.r + step, self.r_size)),
                    device_id_type=MESH,
                ).start()
            s.near[self.r] = s.pay[...]

    def sum_turn(self, name):
        s = self.sums[name]
        if s.direct:
            return
        several = s.near.at[0 : self.r_size - 1]
        pltpu.make_async_copy(several, several, s.sems.at[1]).wait()
        s.mid[...] = jnp.sum(s.near[...], axis=0)

        def send(step):
            pltpu.make_async_remote_copy(
                s.mid,
                s.far.at[self.d],
                s.sems.at[2],
                s.sems.at[3],
                device_id=(lax.rem(self.d + step + 1, self.d_size), self.r),
                device_id_type=MESH,
            ).start()

        loop(self.d_size - 1, send)
        s.far[self.d] = s.mid[...]

    def sum_finish(self, name):
        s = self.sums[name]
        if s.direct:
            many = s.near.at[0 : self.total - 1]
            pltpu.make_async_copy(many, many, s.sems.at[1]).wait()
            return jnp.sum(s.near[...], axis=0)
        many = s.far.at[0 : self.d_size - 1]
        pltpu.make_async_copy(many, many, s.sems.at[3]).wait()
        return jnp.sum(s.far[...], axis=0)

    def sums_sent(self):
        for s in self.sums:
            if s.direct:
                many = s.near.at[0 : self.total - 1]
                pltpu.make_async_copy(many, many, s.sems.at[0]).wait()
            else:
                several = s.near.at[0 : self.r_size - 1]
                pltpu.make_async_copy(several, several, s.sems.at[0]).wait()
                many = s.far.at[0 : self.d_size - 1]
                pltpu.make_async_copy(many, many, s.sems.at[2]).wait()


    def norm_ready(self, norm, totals, count):
        coef = self.coef[norm]
        mean = totals[0:1] / count
        scale = lax.rsqrt(totals[1:2] / count - mean * mean + EPS)
        factor = scale * self.gain[norm][...]
        coef[0:1, :] = factor
        coef[1:2, :] = self.bias[norm][...] - mean * factor
        coef[2:3, :] = mean
        coef[3:4, :] = scale

    def norm_back_ready(self, norm, first, second, count):
        coef = self.coef[norm]
        factor, mean, scale = coef[0:1, :], coef[2:3, :], coef[3:4, :]
        second = second * scale
        self.grad_gain[norm][...] = second
        self.grad_bias[norm][...] = first
        slant = factor * scale * (second / count)
        coef[4:5, :] = slant
        coef[5:6, :] = factor * (first / count) - mean * slant

    def act(self, norm, value, lanes=slice(None)):
        coef = self.coef[norm]
        return value * coef[0:1, lanes] + coef[1:2, lanes]

    def off_mean(self, norm, value, lanes=slice(None)):
        return value - self.coef[norm][2:3, lanes]

    def back(self, norm, slope, value, mask, lanes=slice(None)):
        coef = self.coef[norm]
        grad = slope * coef[0:1, lanes] - value * coef[4:5, lanes] - coef[5:6, lanes]
        return (grad * mask).astype(BF16)


    def to_strip(self, step, src, dst, slot):
        return pltpu.make_async_remote_copy(
            src,
            dst,
            self.halo_send.at[slot],
            self.halo_recv.at[slot],
            device_id=(self.d, self.r + step),
            device_id_type=MESH,
        )


    def place(self, name, shard):
        order = GRADS[name][2]
        if isinstance(shard, int):
            return sum(((shard >> b) & 1) << (BITS - 1 - k) for k, b in enumerate(order))
        where = 0
        for k, b in enumerate(order):
            where = where + bit_of(shard, b) * (1 << (BITS - 1 - k))
        return where

    def halving(self, name, stage):
        order = GRADS[name][2]
        start = 0
        for k in range(stage):
            start = start + bit_of(self.shard, order[k]) * (1 << (BITS - 1 - k))
        half = 1 << (BITS - 1 - stage)
        mine = bit_of(self.shard, order[stage])
        offset = SHARDS - 2 * half
        bit = order[stage] + self.low
        if bit < self.r_bits:
            partner = (self.d, self.r + (1 - 2 * mine) * (1 << bit))
        else:
            partner = (self.d + (1 - 2 * mine) * (1 << (bit - self.r_bits)), self.r)
        return start + mine * half, start + (1 - mine) * half, half, offset, partner

    def grad_copy(self, name, stage):
        rows = GRADS[name][0]
        _, away, half, offset, partner = self.halving(name, stage)
        index = name * BITS + stage
        return pltpu.make_async_remote_copy(
            self.grads[name].at[pl.ds(pl.multiple_of(away * rows, 16), half * rows)],
            self.recv[name].at[pl.ds(offset * rows, half * rows)],
            self.grad_send.at[index],
            self.grad_recv.at[index],
            device_id=partner,
            device_id_type=MESH,
        )

    def grad_start(self, name):
        self.grad_copy(name, 0).start()

    def grad_step(self, name, stage):
        rows, lanes, _ = GRADS[name]
        keep, _, half, offset, _ = self.halving(name, stage)
        self.grad_copy(name, stage).wait_recv()
        own, came = self.grads[name], self.recv[name]
        if stage < BITS - 1:
            height = 16
            while height * lanes < 32768 and (half * rows) % (2 * height) == 0:
                height *= 2

            def add(step):
                here = pl.ds(pl.multiple_of(keep * rows + step * height, 16), height)
                there = pl.ds(pl.multiple_of(offset * rows + step * height, 16), height)
                own[here, :] = (own[here, :].astype(F32) + came[there, :].astype(F32)).astype(BF16)

            loop(half * rows // height, add)
            self.grad_copy(name, stage + 1).start()
            return
        here = pl.ds(pl.multiple_of(keep * rows, 16), rows)
        there = pl.ds(offset * rows, rows)
        out = self.grad_out[name]
        total = own[here, :].astype(F32) + came[there, :].astype(F32)
        if name == G_SPATIAL_ONE:
            for tap in range(9):
                out[tap, :, 0:128] = total[tap * 16 : tap * 16 + 8]
                out[tap, :, 128:256] = total[tap * 16 + 8 : tap * 16 + 16]
        elif name == G_EXPAND_ONE:
            out[:, 0:512] = total[0:8]
            out[:, 512:1024] = total[8:16]
        else:
            out[...] = total

    def grads_sent(self):
        for name in range(len(GRADS)):
            for stage in range(BITS):
                self.grad_copy(name, stage).wait_send()

    def grad_store(self, name, block, value, lanes=slice(None), row=0):
        rows, _, _ = GRADS[name]
        per = 16 if name == G_SPATIAL_TWO else rows
        count = 256 // per
        base = self.place(name, block * count) * rows + row
        for s in range(count):
            where = base + self.place(name, s) * rows
            if not isinstance(where, int):
                where = pl.multiple_of(where, 16)
            self.grads[name][pl.ds(where, per), lanes] = value[s * per : (s + 1) * per].astype(BF16)


    def run(self):
        self.greet()
        pairs = dict(
            xa=(self.xa_in, self.xa),
            xb=(self.xb_in, self.xb),
            w1=(self.w1_in, self.w1),
            ca=(self.ca_in, self.ca),
            cb=(self.cb_in, self.cb),
            w2=(self.w2_in, self.w2),
            w3=(self.w3_in, self.w3),
            w4=(self.w4_in, self.w4),
            ws=(self.ws_in, self.ws),
            w5=(self.w5_in, self.w5),
            w6=(self.w6_in, self.w6),
        )
        loads = SimpleNamespace()
        for i, name in enumerate(pairs):
            copy = pltpu.make_async_copy(*pairs[name], self.load_sem.at[i])
            copy.start()
            setattr(loads, name, copy)

        x, z1, z2, z3, z4, z5 = self.x, self.z1, self.z2, self.z3, self.z4, self.z5
        h1, h2, feed, h4, h5 = self.h1, self.h2, self.feed, self.h4, self.h5
        big, mask = self.big, self.mask
        rows, cols, views, _ = x.shape
        half = cols // 2
        natural = [2 * (k % half) + k // half for k in range(cols)]
        zeros = functools.partial(jnp.zeros, dtype=BF16)

        live_a = self.live[0, self.d]
        live_b = self.live[1, self.d]
        all_a = self.live[0, 0]
        all_b = self.live[1, 0]
        for i in range(1, self.d_size):
            all_a = all_a + self.live[0, i]
            all_b = all_b + self.live[1, i]
        line = jnp.zeros((1, 128), jnp.int32)
        line_a = (line + all_a).astype(F32)
        line_b = (line + all_b).astype(F32)
        full_one = HA * WA * line_a + HB * WB * line_b
        half_one = ((HA + 1) // 2) * ((WA + 1) // 2) * line_a + ((HB + 1) // 2) * (
            (WB + 1) // 2
        ) * line_b
        self.full_count[...] = full_one
        self.half_count[...] = half_one

        def full(lanes):
            return wide(self.full_count[...], lanes)

        def part(lanes):
            return wide(self.half_count[...], lanes)

        def make_mask(row):
            place = lax.broadcasted_iota(jnp.int32, (cols, views, 128), 0)
            column = jnp.where(place < half, 2 * place, 2 * (place - half) + 1)
            view = lax.broadcasted_iota(jnp.int32, (cols, views, 128), 1)
            where = self.r * rows + row
            tall_a = jnp.where(where < HA, live_a, 0)
            tall_b = jnp.where(where < HB, live_b, 0)
            in_a = (view < self.live_a) & (view < tall_a)
            in_b = (view >= self.live_a) & (view - self.live_a < tall_b) & (column < WB)
            mask[row] = jnp.where(in_a | in_b, 1.0, 0.0).astype(F32)

        loop(rows, make_mask)

        for ref in (h1, self.dz2):
            lanes = ref.shape[-1]
            ref[0] = zeros((cols + 2, views, lanes))
            ref[rows + 1] = zeros((cols + 2, views, lanes))
            for row in range(1, rows + 1):
                ref[row, 0] = zeros((views, lanes))
                ref[row, cols + 1] = zeros((views, lanes))
        h4[0] = zeros(h4.shape[1:])
        for row in range(1, rows + 1):
            h4[row, half] = zeros((views, h4.shape[-1]))
        self.dz5[rows // 2] = zeros(self.dz5.shape[1:])
        for row in range(rows // 2):
            self.dz5[row, half] = zeros((views, self.dz5.shape[-1]))

        def row_mask(row, lanes):
            return wide(flat(mask[row]), lanes)

        none = jnp.zeros((1, 256), F32)

        loads.xa.wait()
        loads.xb.wait()

        def gather_row(row):
            for k in range(cols):
                c = natural[k]
                near = self.xa[row, c].astype(F32)
                if c < self.xb.shape[1]:
                    rest = self.xb[row, c].astype(F32)
                else:
                    rest = jnp.zeros((self.live_b, near.shape[-1]), F32)
                value = jnp.concatenate([near, rest], axis=0)
                x[row, k] = (value * wide(mask[row, k], value.shape[-1])).astype(BF16)

        loop(rows, gather_row)
        loads.w1.wait()

        def reduce_row(row, carry):
            total, square = carry
            value = mm(flat(x[row]), self.w1[...])
            z1[row] = value.reshape(cols, views, -1)
            return (total + col_sum(value), square + col_sum(value * value))

        sums = loop(rows, reduce_row, (none, none))
        self.greeted()
        self.sum_start(AT_ONE, sums)
        self.sum_turn(AT_ONE)
        loads.ca.wait()
        loads.cb.wait()
        for o in range(rows // 2):
            for p in range(half):
                for h in range(2):
                    lanes = slice(h * LEAF, h * LEAF + LEAF)
                    near = self.ca[o, p, :, lanes].astype(F32)
                    if p < self.cb.shape[1]:
                        rest = self.cb[o, p, :, lanes].astype(F32)
                    else:
                        rest = jnp.zeros((self.live_b, LEAF), F32)
                    self.cot[h, o * half + p] = jnp.concatenate([near, rest], axis=0).astype(BF16)
        self.norm_ready(NARROW, self.sum_finish(AT_ONE), full(256))

        def hidden_one(row):
            value = self.act(NARROW, flat(z1[row]))
            value = (value * sigmoid(value) * row_mask(row, 256)).astype(BF16)
            value = value.reshape(cols, views, -1)
            for k in range(cols):
                h1[row + 1, natural[k] + 1] = value[k]

        first, last = self.r == 0, self.r == self.r_size - 1
        hidden_one(0)
        hidden_one(rows - 1)
        up = self.to_strip(-1, h1.at[1], h1.at[rows + 1], 0)
        down = self.to_strip(1, h1.at[rows], h1.at[0], 1)

        @pl.when(jnp.logical_not(first))
        def _():
            up.start()

        @pl.when(jnp.logical_not(last))
        def _():
            down.start()

        loop(rows - 2, lambda i: hidden_one(i + 1))
        loads.w2.wait()

        def conv_row(row, carry):
            total, square = carry
            value = 0.0
            for i in range(3):
                for j in range(3):
                    tap = (i * 3 + j) * 256
                    value = value + mm(flat(h1[row + i, j : j + cols]), self.w2[tap : tap + 256, :])
            value = value.reshape(cols, views, -1)
            ordered = jnp.concatenate([value[c] for c in natural], axis=0)
            z2[row] = ordered.reshape(cols, views, -1)
            kept = ordered * row_mask(row, 256)
            return (total + col_sum(kept), square + col_sum(kept * ordered))

        sums = loop(rows - 2, lambda i, carry: conv_row(i + 1, carry), (none, none))

        @pl.when(jnp.logical_not(last))
        def _():
            self.to_strip(1, h1.at[rows], h1.at[rows + 1], 0).wait_recv()

        @pl.when(jnp.logical_not(first))
        def _():
            self.to_strip(-1, h1.at[1], h1.at[0], 1).wait_recv()

        sums = conv_row(rows - 1, conv_row(0, sums))
        self.sum_start(AT_TWO, sums)
        self.sum_turn(AT_TWO)
        loads.w3.wait()
        self.norm_ready(SPATIAL, self.sum_finish(AT_TWO), full(256))

        def hidden_two(row):
            value = self.act(SPATIAL, flat(z2[row]))
            value = (value * sigmoid(value) * row_mask(row, 256)).astype(BF16)
            h2[row] = value.reshape(cols, views, -1)

        loop(rows, hidden_two)

        def expand_row(row, carry):
            given = flat(h2[row])
            done = []
            for n in range(2):
                lanes = slice(n * 512, n * 512 + 512)
                value = mm(given, self.w3[:, lanes])
                z3[row, :, :, lanes] = value.reshape(cols, views, -1)
                done.append((carry[n][0] + col_sum(value), carry[n][1] + col_sum(value * value)))
            return tuple(done)

        nothing = jnp.zeros((1, 512), F32)
        sums = loop(rows, expand_row, ((nothing, nothing), (nothing, nothing)))
        sums = [jnp.concatenate([sums[0][i], sums[1][i]], axis=1) for i in range(2)]
        self.sum_start(AT_THREE, sums)
        self.sum_turn(AT_THREE)
        loads.w4.wait()
        loads.ws.wait()
        self.norm_ready(WIDENED, self.sum_finish(AT_THREE), full(1024))

        def feed_step(step):
            row, pair = step // half, lax.rem(step, half)
            here = pl.ds(pair * 2, 2)
            value = self.act(WIDENED, flat(z3[row, here])) + flat(x[row, here]).astype(F32)
            value = value * sigmoid(value) * wide(flat(mask[row, here]), 1024)
            feed[row, here] = value.astype(BF16).reshape(2, views, -1)

        loop(rows * half, feed_step)

        def squeeze_row(row, carry):
            total, square = carry
            value = mm(flat(feed[row]), self.w4[...])
            z4[row] = value.reshape(cols, views, -1)
            return (total + col_sum(value), square + col_sum(value * value))

        sums = loop(rows, squeeze_row, (nothing, nothing))
        self.sum_start(AT_FOUR, sums)
        self.sum_turn(AT_FOUR)

        def even(ref):
            return jnp.concatenate([flat(ref[2 * o, 0:half]) for o in range(rows // 2)], axis=0)

        for h in range(2):
            sums = []
            for n in range(2):
                lanes = slice(h * LEAF + n * 512, h * LEAF + n * 512 + 512)
                value = mm(even(feed), self.ws[:, lanes])
                big[2 + h, :, :, n * 512 : n * 512 + 512] = value.reshape(cols, views, -1)
                sums.append((col_sum(value), col_sum(value * value)))
            for i in range(2):
                self.short_sum[i : i + 1, h * LEAF : h * LEAF + LEAF] = jnp.concatenate(
                    [sums[0][i], sums[1][i]], axis=1
                )
        self.sum_start(AT_SHORT, [self.short_sum[0:1, :], self.short_sum[1:2, :]])
        self.norm_ready(SQUEEZE, self.sum_finish(AT_FOUR), full(512))

        def hidden_four(row):
            for p in range(2):
                value = self.act(SQUEEZE, flat(z4[row, p * half : p * half + half]))
                value = value * sigmoid(value) * wide(flat(mask[row, p * half : p * half + half]), 512)
                start = p * (half + 1)
                h4[row + 1, start : start + half] = value.astype(BF16).reshape(half, views, -1)

        hidden_four(rows - 1)
        below = self.to_strip(1, h4.at[rows], h4.at[0], 2)

        @pl.when(jnp.logical_not(last))
        def _():
            below.start()

        loop(rows - 1, hidden_four)
        loads.w5.wait()
        starts = (half, 0, half + 1)

        def taken(i, j):
            return jnp.concatenate(
                [flat(h4[2 * o + i, starts[j] : starts[j] + half]) for o in range(rows // 2)], axis=0
            )

        value = 0.0
        for i in (1, 2, 0):
            if i == 0:

                @pl.when(jnp.logical_not(first))
                def _():
                    self.to_strip(-1, h4.at[rows], h4.at[0], 2).wait_recv()

            for j in range(3):
                tap = (i * 3 + j) * 512
                value = value + mm(taken(i, j), self.w5[tap : tap + 512, :])
        z5[...] = value
        half_mask = jnp.concatenate(
            [flat(mask[2 * o, 0:half]) for o in range(rows // 2)], axis=0
        )
        self.half_mask[...] = half_mask
        kept = value * wide(half_mask, 512)
        self.sum_start(AT_FIVE, (col_sum(kept), col_sum(kept * value)))
        self.sum_turn(AT_FIVE)
        self.sum_turn(AT_SHORT)
        loads.w6.wait()
        self.norm_ready(STRIDED, self.sum_finish(AT_FIVE), part(512))
        value = self.act(STRIDED, z5[...])
        h5[...] = (value * sigmoid(value) * wide(self.half_mask[...], 512)).astype(BF16)

        for h in range(2):
            sums = []
            for n in range(2):
                lanes = slice(h * LEAF + n * 512, h * LEAF + n * 512 + 512)
                value = mm(h5[...], self.w6[:, lanes])
                big[h, :, :, n * 512 : n * 512 + 512] = value.reshape(cols, views, -1)
                sums.append((col_sum(value), col_sum(value * value)))
            for i in range(2):
                self.main_sum[i : i + 1, h * LEAF : h * LEAF + LEAF] = jnp.concatenate(
                    [sums[0][i], sums[1][i]], axis=1
                )
        self.sum_start(AT_SIX, [self.main_sum[0:1, :], self.main_sum[1:2, :]])
        self.norm_ready(SHORTCUT, self.sum_finish(AT_SHORT), part(2048))
        self.sum_turn(AT_SIX)
        self.norm_ready(OUTPUT, self.sum_finish(AT_SIX), part(2048))

        top, cot = self.top, self.cot
        zero = jnp.zeros((1, LEAF), F32)
        for h in range(2):
            lanes = slice(h * LEAF, h * LEAF + LEAF)

            def out_step(pair, carry):
                here = pl.ds(pair * 2, 2)
                main, side = flat(big[h, here]), flat(big[2 + h, here])
                value = self.act(OUTPUT, main, lanes) + self.act(SHORTCUT, side, lanes)
                there = wide(self.half_mask[pl.ds(pl.multiple_of(pair * 2 * views, 8), 2 * views), :], LEAF)
                sigma = sigmoid(value)
                given = flat(cot[h, here]).astype(F32)
                slope = given * there * (sigma * (1.0 + value * (1.0 - sigma)))
                cot[h, here] = (value * sigma * there).astype(BF16).reshape(2, views, -1)
                top[h, here] = slope.reshape(2, views, -1)
                return (
                    carry[0] + col_sum(slope),
                    carry[1] + col_sum(slope * self.off_mean(OUTPUT, main, lanes)),
                    carry[2] + col_sum(slope * self.off_mean(SHORTCUT, side, lanes)),
                )

            sums = loop(half, out_step, (zero, zero, zero))
            for i in range(3):
                self.top_sum[i : i + 1, lanes] = sums[i]
        self.sum_start(AT_SEVEN, [self.top_sum[i : i + 1, :] for i in range(3)])
        for o in range(rows // 2):
            for p in range(half):
                for h in range(2):
                    lanes = slice(h * LEAF, h * LEAF + LEAF)
                    done = cot[h, o * half + p].astype(F32)
                    self.ca[o, p, :, lanes] = done[0 : self.live_a].astype(BF16)
                    if p < self.cb.shape[1]:
                        self.cb[o, p, :, lanes] = done[self.live_a :].astype(BF16)
        stores = [
            pltpu.make_async_copy(self.ca, self.out_a_to, self.store_sem.at[0]),
            pltpu.make_async_copy(self.cb, self.out_b_to, self.store_sem.at[1]),
        ]
        for copy in stores:
            copy.start()
        self.sum_turn(AT_SEVEN)
        totals = self.sum_finish(AT_SEVEN)
        self.norm_back_ready(OUTPUT, totals[0:1], totals[1:2], part(2048))
        self.norm_back_ready(SHORTCUT, totals[0:1], totals[2:3], part(2048))

        dz6, dzs = self.dz6, self.dzs
        for h in range(2):
            lanes = slice(h * LEAF, h * LEAF + LEAF)

            def top_step(pair):
                here = pl.ds(pair * 2, 2)
                there = pl.ds(pl.multiple_of(pair * 2 * views, 16), 2 * views)
                live = wide(self.half_mask[there, :], LEAF)
                slope = flat(top[h, here])
                dz6[there, lanes] = self.back(OUTPUT, slope, flat(big[h, here]), live, lanes)
                dzs[there, lanes] = self.back(SHORTCUT, slope, flat(big[2 + h, here]), live, lanes)

            loop(half, top_step)

        value = mm_nt(dz6[...], self.w6[...]) * slope_of(self.act(STRIDED, z5[...]))
        self.slope5[...] = value
        self.sum_start(AT_EIGHT, (col_sum(value), col_sum(value * self.off_mean(STRIDED, z5[...]))))

        def clear(row):
            big[row] = jnp.zeros(big.shape[1:], F32)

        def shortcut_back(n):
            lanes = pl.ds(pl.multiple_of(n * 256, 256), 256)
            value = mm_nt(dzs[...], self.ws[lanes, :]).reshape(rows // 2, half, views, -1)
            for o in range(rows // 2):
                big[2 * o, 0:half, :, lanes] = value[o]

        def grad_expand_two(step):
            m, n = step // 4, lax.rem(step, 4)
            left = h5[:, pl.ds(pl.multiple_of(m * 256, 256), 256)]
            lanes = pl.ds(pl.multiple_of(n * 512, 512), 512)
            self.grad_store(G_EXPAND_TWO, m, mm_tn(left, dz6[:, lanes]), lanes)

        def grad_shortcut_two(step):
            m, n = step // 4, lax.rem(step, 4)
            here = pl.ds(pl.multiple_of(m * 256, 256), 256)
            left = jnp.concatenate(
                [flat(feed[2 * o, 0:half, :, here]) for o in range(rows // 2)], axis=0
            )
            lanes = pl.ds(pl.multiple_of(n * 512, 512), 512)
            self.grad_store(G_SHORTCUT_TWO, m, mm_tn(left, dzs[:, lanes]), lanes)

        loop(8, grad_expand_two)
        self.grad_start(G_EXPAND_TWO)
        self.sum_turn(AT_EIGHT)
        loop(rows, clear)
        loop(4, shortcut_back)
        totals = self.sum_finish(AT_EIGHT)
        self.norm_back_ready(STRIDED, totals[0:1], totals[1:2], part(512))
        dz5 = self.dz5
        value = self.back(STRIDED, self.slope5[...], z5[...], wide(self.half_mask[...], 512))
        for o in range(rows // 2):
            dz5[o, 0:half] = value[o * half * views : (o + 1) * half * views].reshape(half, views, -1)
        above = self.to_strip(-1, dz5.at[0], dz5.at[rows // 2], 3)

        @pl.when(jnp.logical_not(first))
        def _():
            above.start()

        loop(16, grad_shortcut_two)
        self.grad_start(G_SHORTCUT_TWO)
        self.grad_step(G_EXPAND_TWO, 0)

        dh4 = self.dh4
        for i in (1, 2, 0):
            if i == 0:

                @pl.when(jnp.logical_not(last))
                def _():
                    self.to_strip(1, dz5.at[0], dz5.at[rows // 2], 3).wait_recv()

            lead = 1 if i == 0 else 0
            for j in (1, 2, 0):
                tap = (i * 3 + j) * 512
                start = 1 if j == 0 else 0
                given = jnp.concatenate(
                    [flat(dz5[o + lead, start : start + half]) for o in range(rows // 2)], axis=0
                )
                value = mm_nt(given, self.w5[tap : tap + 512, :]).reshape(rows // 2, half, views, -1)
                spot = slice(0, half) if j == 1 else slice(half, 2 * half)
                for o in range(rows // 2):
                    target = 2 * o if i == 1 else 2 * o + 1
                    if j == 0 or i == 0:
                        dh4[target, spot] = dh4[target, spot] + value[o]
                    else:
                        dh4[target, spot] = value[o]

        def slope_four(step, carry):
            row, p = step // 2, lax.rem(step, 2)
            here = pl.ds(p * half, half)
            before = flat(z4[row, here])
            value = flat(dh4[row, here]) * slope_of(self.act(SQUEEZE, before))
            dh4[row, here] = value.reshape(half, views, -1)
            return (
                carry[0] + col_sum(value),
                carry[1] + col_sum(value * self.off_mean(SQUEEZE, before)),
            )

        sums = loop(rows * 2, slope_four, (nothing, nothing))
        self.sum_start(AT_NINE, sums)
        self.sum_turn(AT_NINE)
        self.grad_step(G_SHORTCUT_TWO, 0)
        self.grad_step(G_EXPAND_TWO, 1)
        for j in range(3):

            def grad_spatial_two(step):
                i, m = step // 2, lax.rem(step, 2)
                here = pl.ds(pl.multiple_of(m * 256, 256), 256)
                left = jnp.concatenate(
                    [
                        flat(h4[2 * o + i, starts[j] : starts[j] + half, :, here])
                        for o in range(rows // 2)
                    ],
                    axis=0,
                )
                right = jnp.concatenate([flat(dz5[o, 0:half]) for o in range(rows // 2)], axis=0)
                self.grad_store(G_SPATIAL_TWO, m, mm_tn(left, right), row=(i * 3 + j) * 16)

            loop(6, grad_spatial_two)
        self.grad_start(G_SPATIAL_TWO)
        totals = self.sum_finish(AT_NINE)
        self.norm_back_ready(SQUEEZE, totals[0:1], totals[1:2], full(512))
        dz4 = self.dz4

        def back_four(step):
            row, p = step // 2, lax.rem(step, 2)
            here = pl.ds(p * half, half)
            value = self.back(
                SQUEEZE, flat(dh4[row, here]), flat(z4[row, here]), wide(flat(mask[row, here]), 512)
            )
            dz4[row, here] = value.reshape(half, views, -1)

        loop(rows * 2, back_four)

        def slope_three(row, carry):
            done = []
            for n in range(2):
                lanes = slice(n * 512, n * 512 + 512)
                before = flat(z3[row, :, :, lanes])
                grad = mm_nt(flat(dz4[row]), self.w4[lanes, :]) + flat(big[row, :, :, lanes])
                point = self.act(WIDENED, before, lanes) + flat(x[row, :, :, lanes]).astype(F32)
                value = grad * slope_of(point)
                big[row, :, :, lanes] = value.reshape(cols, views, -1)
                done.append(
                    (
                        carry[n][0] + col_sum(value),
                        carry[n][1] + col_sum(value * self.off_mean(WIDENED, before, lanes)),
                    )
                )
            return tuple(done)

        sums = loop(rows, slope_three, ((nothing, nothing), (nothing, nothing)))
        sums = [jnp.concatenate([sums[0][i], sums[1][i]], axis=1) for i in range(2)]
        self.sum_start(AT_TEN, sums)
        self.grad_step(G_SHORTCUT_TWO, 1)
        self.sum_turn(AT_TEN)
        self.grad_step(G_SPATIAL_TWO, 0)
        self.grad_step(G_EXPAND_TWO, 2)

        def grad_reduce_two(m):
            here = pl.ds(pl.multiple_of(m * 256, 256), 256)
            left = feed[:, :, :, here].reshape(-1, 256)
            self.grad_store(G_REDUCE_TWO, m, mm_tn(left, dz4[...].reshape(-1, 512)))

        loop(4, grad_reduce_two)
        self.grad_start(G_REDUCE_TWO)
        totals = self.sum_finish(AT_TEN)
        self.norm_back_ready(WIDENED, totals[0:1], totals[1:2], full(1024))
        dz3 = feed

        def back_three(step):
            row, pair = step // half, lax.rem(step, half)
            here = pl.ds(pair * 2, 2)
            live = wide(flat(mask[row, here]), 1024)
            value = self.back(WIDENED, flat(big[row, here]), flat(z3[row, here]), live)
            dz3[row, here] = value.reshape(2, views, -1)

        loop(rows * half, back_three)


        def slope_spatial(row, carry):
            before = flat(z2[row])
            value = mm_nt(flat(dz3[row]), self.w3[...]) * slope_of(self.act(SPATIAL, before))
            dh4[row, :, :, 0:256] = value.reshape(cols, views, -1)
            return (
                carry[0] + col_sum(value),
                carry[1] + col_sum(value * self.off_mean(SPATIAL, before)),
            )

        sums = loop(rows, slope_spatial, (none, none))
        self.sum_start(AT_ELEVEN, sums)
        self.sum_turn(AT_ELEVEN)

        left = h2[...].reshape(-1, 256)
        g_low = mm_tn(left, dz3[:, :, :, 0:512].reshape(-1, 512))
        g_high = mm_tn(left, dz3[:, :, :, 512:1024].reshape(-1, 512))
        for s in range(SHARDS):
            at = self.place(G_EXPAND_ONE, s) * 16
            piece = jnp.concatenate([g_low[s * 8 : s * 8 + 8], g_high[s * 8 : s * 8 + 8]], axis=0)
            self.grads[G_EXPAND_ONE][at : at + 16, :] = piece.astype(BF16)
        self.grad_start(G_EXPAND_ONE)
        self.grad_step(G_SPATIAL_TWO, 1)
        self.grad_step(G_REDUCE_TWO, 0)
        totals = self.sum_finish(AT_ELEVEN)
        self.norm_back_ready(SPATIAL, totals[0:1], totals[1:2], full(256))
        dz2 = self.dz2

        def back_two(row):
            value = self.back(SPATIAL, flat(dh4[row, :, :, 0:256]), flat(z2[row]), row_mask(row, 256))
            value = value.reshape(cols, views, -1)
            for k in range(cols):
                dz2[row + 1, natural[k] + 1] = value[k]

        back_two(0)
        back_two(rows - 1)
        up = self.to_strip(-1, dz2.at[1], dz2.at[rows + 1], 4)
        down = self.to_strip(1, dz2.at[rows], dz2.at[0], 5)

        @pl.when(jnp.logical_not(first))
        def _():
            up.start()

        @pl.when(jnp.logical_not(last))
        def _():
            down.start()

        loop(rows - 2, lambda i: back_two(i + 1))
        for i in range(3):
            for j in range(3):
                left = h1[i : i + rows, j : j + cols].reshape(-1, 256)
                value = mm_tn(left, dz2[1 : rows + 1, 1 : cols + 1].reshape(-1, 256))
                for s in range(SHARDS):
                    at = self.place(G_SPATIAL_ONE, s) * 144 + (i * 3 + j) * 16
                    piece = value[s * 8 : s * 8 + 8]
                    piece = jnp.concatenate([piece[:, 0:128], piece[:, 128:256]], axis=0)
                    self.grads[G_SPATIAL_ONE][at : at + 16, :] = piece.astype(BF16)
        self.grad_start(G_SPATIAL_ONE)

        @pl.when(jnp.logical_not(last))
        def _():
            self.to_strip(1, dz2.at[rows], dz2.at[rows + 1], 4).wait_recv()

        @pl.when(jnp.logical_not(first))
        def _():
            self.to_strip(-1, dz2.at[1], dz2.at[0], 5).wait_recv()

        def slope_narrow(row, carry):
            value = 0.0
            for i in range(3):
                for j in range(3):
                    tap = (i * 3 + j) * 256
                    given = flat(dz2[row + 2 - i, 2 - j : 2 - j + cols])
                    value = value + mm_nt(given, self.w2[tap : tap + 256, :])
            value = value.reshape(cols, views, -1)
            value = jnp.concatenate([value[c] for c in natural], axis=0)
            before = flat(z1[row])
            value = value * row_mask(row, 256) * slope_of(self.act(NARROW, before))
            dh4[row, :, :, 0:256] = value.reshape(cols, views, -1)
            return (
                carry[0] + col_sum(value),
                carry[1] + col_sum(value * self.off_mean(NARROW, before)),
            )

        sums = loop(rows, slope_narrow, (none, none))
        self.sum_start(AT_TWELVE, sums)
        self.sum_turn(AT_TWELVE)
        self.grad_step(G_EXPAND_ONE, 0)
        self.grad_step(G_SPATIAL_ONE, 0)
        self.grad_step(G_SHORTCUT_TWO, 2)
        self.grad_step(G_SPATIAL_TWO, 2)
        self.grad_step(G_REDUCE_TWO, 1)
        self.grad_step(G_EXPAND_TWO, 3)
        totals = self.sum_finish(AT_TWELVE)
        self.norm_back_ready(NARROW, totals[0:1], totals[1:2], full(256))
        dz1 = h2

        def back_one(row):
            value = self.back(NARROW, flat(dh4[row, :, :, 0:256]), flat(z1[row]), row_mask(row, 256))
            dz1[row] = value.reshape(cols, views, -1)

        loop(rows, back_one)

        def grad_reduce_one(m):
            here = pl.ds(pl.multiple_of(m * 256, 256), 256)
            left = x[:, :, :, here].reshape(-1, 256)
            self.grad_store(G_REDUCE_ONE, m, mm_tn(left, dz1[...].reshape(-1, 256)))

        loop(4, grad_reduce_one)
        self.grad_start(G_REDUCE_ONE)

        def input_row(row):
            for n in range(2):
                lanes = slice(n * 512, n * 512 + 512)
                value = mm_nt(flat(dz1[row]), self.w1[lanes, :]) + flat(big[row, :, :, lanes])
                value = value.reshape(cols, views, -1)
                for k in range(cols):
                    self.xa[row, natural[k], :, lanes] = value[k, 0 : self.live_a].astype(BF16)
                    if natural[k] < self.xb.shape[1]:
                        self.xb[row, natural[k], :, lanes] = value[k, self.live_a :].astype(BF16)

        loop(rows, input_row)
        for i, pair in enumerate(((self.xa, self.in_a_to), (self.xb, self.in_b_to))):
            copy = pltpu.make_async_copy(*pair, self.store_sem.at[2 + i])
            copy.start()
            stores.append(copy)
        for name, stage in (
            (G_EXPAND_ONE, 1),
            (G_SPATIAL_ONE, 1),
            (G_REDUCE_ONE, 0),
            (G_SHORTCUT_TWO, 3),
            (G_SPATIAL_TWO, 3),
            (G_REDUCE_TWO, 2),
            (G_EXPAND_TWO, 4),
            (G_EXPAND_ONE, 2),
            (G_SPATIAL_ONE, 2),
            (G_REDUCE_ONE, 1),
            (G_SHORTCUT_TWO, 4),
            (G_SPATIAL_TWO, 4),
            (G_REDUCE_TWO, 3),
            (G_EXPAND_ONE, 3),
            (G_SPATIAL_ONE, 3),
            (G_REDUCE_ONE, 2),
            (G_REDUCE_TWO, 4),
            (G_EXPAND_ONE, 4),
            (G_SPATIAL_ONE, 4),
            (G_REDUCE_ONE, 3),
            (G_REDUCE_ONE, 4),
        ):
            self.grad_step(name, stage)

        for copy in stores:
            copy.wait()
        self.sums_sent()
        self.grads_sent()

        @pl.when(jnp.logical_not(first))
        def _():
            self.to_strip(-1, h1.at[1], h1.at[rows + 1], 0).wait_send()
            self.to_strip(-1, dz5.at[0], dz5.at[rows // 2], 3).wait_send()
            self.to_strip(-1, dz2.at[1], dz2.at[rows + 1], 4).wait_send()

        @pl.when(jnp.logical_not(last))
        def _():
            self.to_strip(1, h1.at[rows], h1.at[0], 1).wait_send()
            self.to_strip(1, h4.at[rows], h4.at[0], 2).wait_send()
            self.to_strip(1, dz2.at[rows], dz2.at[0], 5).wait_send()


def settle(*refs):
    half = len(refs) // 2
    for i in range(half):
        refs[half + i][...] = refs[i][...]


def settled(values):
    inside = pl.BlockSpec(memory_space=pltpu.VMEM)
    return pl.pallas_call(
        settle,
        out_shape=[jax.ShapeDtypeStruct(v.shape, v.dtype) for v in values],
        in_specs=[inside] * len(values),
        out_specs=[inside] * len(values),
    )(*values)


def sum_of(pay, near, mid, far, sems):
    return SimpleNamespace(direct=far is None, pay=pay, near=near, mid=mid, far=far, sems=sems)


def both_blocks(given, live_views, weights, gains, biases):
    d_size, r_size = lax.axis_size("dp"), lax.axis_size("rows")
    total = d_size * r_size
    rows, cols, views_a, c_in = given[0].shape
    views_b = given[1].shape[2]
    views = views_a + views_b
    half = cols // 2
    c_mid, c_mid2, c_out = gains[0].shape[1], gains[3].shape[1], gains[5].shape[1]
    pixels = (rows // 2) * half * views
    vmem, dma = pltpu.VMEM, pltpu.SemaphoreType.DMA
    anywhere = pl.BlockSpec(memory_space=pl.ANY)
    inside = pl.BlockSpec(memory_space=pltpu.VMEM)

    def full(lanes, kind):
        return vmem((rows, cols, views, lanes), kind)

    def like(value):
        return vmem(value.shape, value.dtype)

    sums = []
    for count, lanes in SUMS:
        direct = lanes <= 512 and total <= 32
        sums.append(
            dict(
                pay=vmem((count, lanes), F32),
                near=vmem((total if direct else r_size, count, lanes), F32),
                mid=None if direct else vmem((count, lanes), F32),
                far=None if direct else vmem((d_size, count, lanes), F32),
                sems=dma((4,)),
            )
        )
    w = weights
    scratch = dict(
        xa=like(given[0]),
        xb=like(given[1]),
        ca=like(given[2]),
        cb=like(given[3]),
        x=full(c_in, BF16),
        w1=like(w[0]),
        w2=like(w[1]),
        w3=like(w[2]),
        w4=like(w[3]),
        w5=like(w[4]),
        w6=like(w[5]),
        ws=like(w[6]),
        cot=vmem((2, cols, views, LEAF), BF16),
        mask=full(128, F32),
        half_mask=vmem((pixels, 128), F32),
        full_count=vmem((1, 128), F32),
        half_count=vmem((1, 128), F32),
        z1=full(c_mid, F32),
        z2=full(c_mid, F32),
        z3=full(c_in, F32),
        z4=full(c_mid2, F32),
        z5=vmem((pixels, c_mid2), F32),
        h1=vmem((rows + 2, cols + 2, views, c_mid), BF16),
        h2=full(c_mid, BF16),
        feed=full(c_in, BF16),
        h4=vmem((rows + 1, cols + 1, views, c_mid2), BF16),
        h5=vmem((pixels, c_mid2), BF16),
        big=full(c_in, F32),
        top=vmem((2, cols, views, LEAF), F32),
        short_sum=vmem((2, c_out), F32),
        main_sum=vmem((2, c_out), F32),
        top_sum=vmem((3, c_out), F32),
        dz6=vmem((pixels, c_out), BF16),
        dzs=vmem((pixels, c_out), BF16),
        slope5=vmem((pixels, c_mid2), F32),
        dz5=vmem((rows // 2 + 1, half + 1, views, c_mid2), BF16),
        dh4=full(c_mid2, F32),
        dz4=full(c_mid2, BF16),
        dz2=vmem((rows + 2, cols + 2, views, c_mid), BF16),
        g2=vmem((SHARDS * 144, 128), BF16),
        g3=vmem((SHARDS * 16, 512), BF16),
        load_sem=dma((11,)),
        store_sem=dma((4,)),
        halo_send=dma((6,)),
        halo_recv=dma((6,)),
        grad_send=dma((len(GRADS) * BITS,)),
        grad_recv=dma((len(GRADS) * BITS,)),
        coef=[vmem((8, gain.shape[1]), F32) for gain in gains],
        recv=[vmem(((SHARDS - 1) * height, lanes), BF16) for height, lanes, _ in GRADS],
        sums=sums,
    )
    grad_shapes = ((32, 256), (9, 8, 256), (8, 1024), (32, 512), (144, 512), (16, 2048), (32, 2048))
    ins = dict(
        live=live_views,
        xa_in=given[0],
        xb_in=given[1],
        ca_in=given[2],
        cb_in=given[3],
        w1_in=w[0],
        w2_in=w[1],
        w3_in=w[2],
        w4_in=w[3],
        w5_in=w[4],
        w6_in=w[5],
        ws_in=w[6],
        gain=list(gains),
        bias=list(biases),
    )
    shape = jax.ShapeDtypeStruct
    outs = dict(
        out_a_to=shape(given[2].shape, BF16),
        out_b_to=shape(given[3].shape, BF16),
        in_a_to=shape(given[0].shape, BF16),
        in_b_to=shape(given[1].shape, BF16),
        grad_out=[shape(s, F32) for s in grad_shapes],
        grad_gain=[shape(g.shape, F32) for g in gains],
        grad_bias=[shape(g.shape, F32) for g in gains],
    )
    parts = []
    trees = []
    for group in (ins, outs, scratch):
        leaves, tree = jax.tree.flatten(group, is_leaf=lambda v: not isinstance(v, (dict, list, type(None))))
        parts.append(leaves)
        trees.append(tree)
    in_specs = dict(ins)
    for name in ins:
        in_specs[name] = [inside] * len(gains) if isinstance(ins[name], list) else anywhere
    in_specs.update(live=pl.BlockSpec(memory_space=pltpu.SMEM))
    out_specs = {
        name: [inside] * len(outs[name]) if isinstance(outs[name], list) else anywhere for name in outs
    }
    spec_leaves = [
        jax.tree.flatten(group, is_leaf=lambda v: isinstance(v, pl.BlockSpec))[0]
        for group in (in_specs, out_specs)
    ]

    def body(*refs):
        fields = {}
        start = 0
        for leaves, tree in zip(parts, trees):
            fields.update(jax.tree.unflatten(tree, refs[start : start + len(leaves)]))
            start += len(leaves)
        g = SimpleNamespace(**fields)
        fields.update(
            grads=[g.w2, g.g2, g.g3, g.w4, g.w5, g.w6, g.ws],
            sums=[sum_of(**s) for s in g.sums],
        )
        Kernel((d_size, r_size, views_a, views_b), fields).run()

    results = pl.pallas_call(
        body,
        out_shape=parts[1],
        in_specs=spec_leaves[0],
        out_specs=spec_leaves[1],
        scratch_shapes=parts[2],
        compiler_params=pltpu.CompilerParams(
            collective_id=0, has_side_effects=True, vmem_limit_bytes=64 * 2**20 - 65536 * 4
        ),
        cost_estimate=pl.CostEstimate(flops=16 * 10**9, bytes_accessed=30 * 10**6, transcendentals=4 * 10**6),
    )(*parts[0])
    done = SimpleNamespace(**jax.tree.unflatten(trees[1], results))
    plain = settled([done.out_a_to, done.in_a_to, *done.grad_out, *done.grad_gain, *done.grad_bias])
    return plain[0], done.out_b_to, plain[1], done.in_b_to, list(plain[2:9]), plain[9:]


def on_device(input_a, input_b, live_views, *rest):
    weights, params, cotangents = rest[:7], rest[7:21], rest[21:]
    gains = [value.reshape(1, -1) for value in params[0::2]]
    biases = [value.reshape(1, -1) for value in params[1::2]]
    reduce_one, spatial_one, expand_one, reduce_two, spatial_two, expand_two, shortcut_two = weights
    weights = (
        reduce_one,
        spatial_one.transpose(1, 2, 0, 3).reshape(-1, spatial_one.shape[-1]),
        expand_one,
        reduce_two,
        spatial_two.transpose(1, 2, 0, 3).reshape(-1, spatial_two.shape[-1]),
        expand_two,
        shortcut_two,
    )
    given = [value.transpose(0, 2, 1, 3) for value in (input_a, input_b, *cotangents)]
    *moved, grads, norms = both_blocks(given, live_views.T, weights, gains, biases)
    maps = [value.transpose(0, 2, 1, 3) for value in moved]
    grads[1] = grads[1].reshape(3, 3, -1, grads[1].shape[-1]).transpose(2, 0, 1, 3)
    grads[4] = grads[4].reshape(3, 3, -1, grads[4].shape[-1]).transpose(2, 0, 1, 3)
    if lax.axis_size("dp") * lax.axis_size("rows") > SHARDS:
        grads = [lax.psum_scatter(g, "rows", scatter_dimension=0, tiled=True) for g in grads]
    small = []
    for i in range(7):
        small += [norms[i].reshape(-1), norms[7 + i].reshape(-1)]
    return (*maps, *grads, *small)


def solution(mesh):
    split = P("rows", "dp", None, None)
    whole = P()
    shard = P(("dp", "rows"), None)
    shard_4 = P(("dp", "rows"), None, None, None)
    return jax.shard_map(
        on_device,
        mesh=mesh,
        in_specs=(split, split) + (whole,) * 22 + (split, split),
        out_specs=(split,) * 4
        + (shard, shard_4, shard, shard, shard_4, shard, shard)
        + (whole,) * 14,
        check_vma=False,
    )
```

```python
import functools
from types import SimpleNamespace

import jax
import jax.numpy as jnp
from jax import lax
from jax.experimental import pallas as pl
from jax.experimental.pallas import tpu as pltpu
from jax.sharding import PartitionSpec as P

MESH = pl.DeviceIdType.MESH
F32 = jnp.float32
BF16 = jnp.bfloat16

HA = 14
WA = 14
HB = 10
WB = 10

EPS = 1e-05
LEAF = 1024
NARROW, SPATIAL, WIDENED, SQUEEZE, STRIDED, OUTPUT, SHORTCUT = range(7)
Y_FIRST = (0, 1, 2, 3, 4)
X_FIRST = (0, 2, 1, 3, 4)
Z_FIRST = (0, 3, 2, 1, 4)
BITS = 5
SHARDS = 1 << BITS
REDUCE_ONE, SPATIAL_ONE, EXPAND_ONE, REDUCE_TWO, SPATIAL_TWO, EXPAND_TWO, SHORTCUT_TWO = range(7)
(
    G_REDUCE_ONE,
    G_SPATIAL_ONE,
    G_EXPAND_ONE,
    G_REDUCE_TWO,
    G_SPATIAL_TWO_0,
    G_SPATIAL_TWO_1,
    G_SPATIAL_TWO_2,
    G_EXPAND_TWO_0,
    G_EXPAND_TWO_1,
    G_SHORTCUT_TWO_0,
    G_SHORTCUT_TWO_1,
    G_SHORTCUT_TWO_2,
) = range(12)
GRADS = (
    (REDUCE_ONE, 32, 0, 0, 256, Y_FIRST),
    (SPATIAL_ONE, 144, 0, 0, 128, Z_FIRST),
    (EXPAND_ONE, 16, 0, 0, 512, Y_FIRST),
    (REDUCE_TWO, 32, 0, 0, 512, Z_FIRST),
    (SPATIAL_TWO, 48, 0, 0, 512, Y_FIRST),
    (SPATIAL_TWO, 48, 1, 0, 512, X_FIRST),
    (SPATIAL_TWO, 48, 2, 0, 512, Z_FIRST),
    (EXPAND_TWO, 16, 0, 0, 1024, X_FIRST),
    (EXPAND_TWO, 16, 0, 1024, 1024, Z_FIRST),
    (SHORTCUT_TWO, 32, 0, 0, 768, Z_FIRST),
    (SHORTCUT_TWO, 32, 0, 768, 640, Y_FIRST),
    (SHORTCUT_TWO, 32, 0, 1408, 640, X_FIRST),
)
SPATIAL_TWO_PARTS = (G_SPATIAL_TWO_0, G_SPATIAL_TWO_1, G_SPATIAL_TWO_2)
EXPAND_TWO_PARTS = (G_EXPAND_TWO_0, G_EXPAND_TWO_1)
SHORTCUT_TWO_PARTS = (G_SHORTCUT_TWO_0, G_SHORTCUT_TWO_1, G_SHORTCUT_TWO_2)
(
    AT_ONE,
    AT_TWO,
    AT_THREE,
    AT_FOUR,
    AT_FIVE,
    AT_SHORT,
    AT_SIX,
    AT_SEVEN,
    AT_EIGHT,
    AT_NINE,
    AT_TEN,
    AT_ELEVEN,
    AT_TWELVE,
) = range(13)
SUMS = (
    (2, 256, True),
    (2, 256, True),
    (2, 1024, False),
    (2, 512, True),
    (2, 512, True),
    (2, 2048, False),
    (2, 2048, False),
    (3, 2048, False),
    (2, 512, True),
    (2, 512, True),
    (2, 1024, True),
    (2, 256, True),
    (2, 256, True),
)


def mm(left, right):
    return lax.dot_general(left, right, (((1,), (0,)), ((), ())), preferred_element_type=F32)


def mm_nt(left, right):
    return lax.dot_general(left, right, (((1,), (1,)), ((), ())), preferred_element_type=F32)


def mm_tn(left, right):
    return lax.dot_general(left, right, (((0,), (0,)), ((), ())), preferred_element_type=F32)


def sigmoid(value):
    return 0.5 + 0.5 * jnp.tanh(0.5 * value)


def slope_of(value):
    sigma = sigmoid(value)
    return sigma * (1.0 + value * (1.0 - sigma))


def flat(block):
    return block.reshape(-1, block.shape[-1])


def col_sum(value):
    return jnp.sum(value, axis=0, keepdims=True)


def wide(mask, lanes):
    return jnp.concatenate([mask] * (lanes // 128), axis=1)


def loop(count, body, init=None):
    if init is None:

        def plain(step, carry):
            body(step)
            return carry

        return lax.fori_loop(0, count, plain, 0)
    return lax.fori_loop(0, count, body, init)


def bit_of(number, bit):
    return lax.rem(number // (1 << bit), 2)


class Kernel:
    def __init__(self, sizes, refs):
        self.d_size, self.r_size, self.live_a, self.live_b = sizes
        self.total = self.d_size * self.r_size
        self.__dict__.update(refs)
        self.d = lax.axis_index("dp")
        self.r = lax.axis_index("rows")
        self.me = self.d * self.r_size + self.r
        self.low = (self.total // SHARDS).bit_length() - 1
        self.shard = self.me // (1 << self.low)
        self.r_bits = self.r_size.bit_length() - 1


    def device(self, number):
        return (number // self.r_size, lax.rem(number, self.r_size))

    def greet(self):
        barrier = pltpu.get_barrier_semaphore()

        def one(step):
            pl.semaphore_signal(
                barrier,
                inc=1,
                device_id=self.device(lax.rem(self.me + step + 1, self.total)),
                device_id_type=MESH,
            )

        loop(self.total - 1, one)

    def greeted(self):
        pl.semaphore_wait(pltpu.get_barrier_semaphore(), self.total - 1)

    def direct(self, name):
        return self.sums[name].direct

    def sum_start(self, name, vectors):
        s = self.sums[name]
        for i, vector in enumerate(vectors):
            s.pay[i : i + 1, :] = vector
        if s.direct:

            def send(step):
                pltpu.make_async_remote_copy(
                    s.pay,
                    s.near.at[self.me],
                    s.sems.at[0],
                    s.sems.at[1],
                    device_id=self.device(lax.rem(self.me + step + 1, self.total)),
                    device_id_type=MESH,
                ).start()

            loop(self.total - 1, send)
            s.near[self.me] = s.pay[...]
        else:
            for step in range(1, self.r_size):
                pltpu.make_async_remote_copy(
                    s.pay,
                    s.near.at[self.r],
                    s.sems.at[0],
                    s.sems.at[1],
                    device_id=(self.d, lax.rem(self.r + step, self.r_size)),
                    device_id_type=MESH,
                ).start()
            s.near[self.r] = s.pay[...]

    def sum_turn(self, name):
        s = self.sums[name]
        if s.direct:
            return
        several = s.near.at[0 : self.r_size - 1]
        pltpu.make_async_copy(several, several, s.sems.at[1]).wait()
        s.mid[...] = jnp.sum(s.near[...], axis=0)

        def send(step):
            pltpu.make_async_remote_copy(
                s.mid,
                s.far.at[self.d],
                s.sems.at[2],
                s.sems.at[3],
                device_id=(lax.rem(self.d + step + 1, self.d_size), self.r),
                device_id_type=MESH,
            ).start()

        loop(self.d_size - 1, send)
        s.far[self.d] = s.mid[...]

    def sum_finish(self, name):
        s = self.sums[name]
        if s.direct:
            many = s.near.at[0 : self.total - 1]
            pltpu.make_async_copy(many, many, s.sems.at[1]).wait()
            return jnp.sum(s.near[...], axis=0)
        many = s.far.at[0 : self.d_size - 1]
        pltpu.make_async_copy(many, many, s.sems.at[3]).wait()
        return jnp.sum(s.far[...], axis=0)

    def sums_sent(self):
        for s in self.sums:
            if s.direct:
                many = s.near.at[0 : self.total - 1]
                pltpu.make_async_copy(many, many, s.sems.at[0]).wait()
            else:
                several = s.near.at[0 : self.r_size - 1]
                pltpu.make_async_copy(several, several, s.sems.at[0]).wait()
                many = s.far.at[0 : self.d_size - 1]
                pltpu.make_async_copy(many, many, s.sems.at[2]).wait()


    def norm_ready(self, norm, totals, count):
        coef = self.coef[norm]
        mean = totals[0:1] / count
        scale = lax.rsqrt(totals[1:2] / count - mean * mean + EPS)
        factor = scale * self.gain[norm][...]
        coef[0:1, :] = factor
        coef[1:2, :] = self.bias[norm][...] - mean * factor
        coef[2:3, :] = mean
        coef[3:4, :] = scale

    def norm_back_ready(self, norm, first, second, count):
        coef = self.coef[norm]
        factor, mean, scale = coef[0:1, :], coef[2:3, :], coef[3:4, :]
        second = second * scale
        self.grad_gain[norm][...] = second
        self.grad_bias[norm][...] = first
        slant = factor * scale * (second / count)
        coef[4:5, :] = slant
        coef[5:6, :] = factor * (first / count) - mean * slant

    def act(self, norm, value, lanes=slice(None)):
        coef = self.coef[norm]
        return value * coef[0:1, lanes] + coef[1:2, lanes]

    def off_mean(self, norm, value, lanes=slice(None)):
        return value - self.coef[norm][2:3, lanes]

    def back(self, norm, slope, value, mask, lanes=slice(None)):
        coef = self.coef[norm]
        grad = slope * coef[0:1, lanes] - value * coef[4:5, lanes] - coef[5:6, lanes]
        return (grad * mask).astype(BF16)


    def to_strip(self, step, src, dst, slot):
        return pltpu.make_async_remote_copy(
            src,
            dst,
            self.halo_send.at[slot],
            self.halo_recv.at[slot],
            device_id=(self.d, self.r + step),
            device_id_type=MESH,
        )


    def place(self, name, shard):
        order = GRADS[name][5]
        if isinstance(shard, int):
            return sum(((shard >> b) & 1) << (BITS - 1 - k) for k, b in enumerate(order))
        where = 0
        for k, b in enumerate(order):
            where = where + bit_of(shard, b) * (1 << (BITS - 1 - k))
        return where

    def halving(self, name, stage):
        order = GRADS[name][5]
        start = 0
        for k in range(stage):
            start = start + bit_of(self.shard, order[k]) * (1 << (BITS - 1 - k))
        half = 1 << (BITS - 1 - stage)
        mine = bit_of(self.shard, order[stage])
        offset = SHARDS - 2 * half
        bit = order[stage] + self.low
        if bit < self.r_bits:
            partner = (self.d, self.r + (1 - 2 * mine) * (1 << bit))
        else:
            partner = (self.d + (1 - 2 * mine) * (1 << (bit - self.r_bits)), self.r)
        return start + mine * half, start + (1 - mine) * half, half, offset, partner

    def grad_copy(self, name, stage):
        array, rows, part, lane, lanes, _ = GRADS[name]
        _, away, half, offset, partner = self.halving(name, stage)
        index = name * BITS + stage
        away = pl.ds(pl.multiple_of((part * SHARDS + away) * rows, 16), half * rows)
        return pltpu.make_async_remote_copy(
            self.grads[array].at[away, lane : lane + lanes],
            self.recv[name].at[pl.ds(offset * rows, half * rows)],
            self.grad_send.at[index],
            self.grad_recv.at[index],
            device_id=partner,
            device_id_type=MESH,
        )

    def grad_start(self, name):
        self.grad_copy(name, 0).start()

    def grad_steps(self, stage, *names):
        for name in names:
            self.grad_step(name, stage)

    def grad_step(self, name, stage):
        array, rows, part, lane, lanes, _ = GRADS[name]
        keep, _, half, offset, _ = self.halving(name, stage)
        keep = part * SHARDS + keep
        self.grad_copy(name, stage).wait_recv()
        own, came = self.grads[array], self.recv[name]
        across = slice(lane, lane + lanes)
        if stage < BITS - 1:
            height = 16
            while height * lanes < 32768 and (half * rows) % (2 * height) == 0:
                height *= 2

            def add(step):
                here = pl.ds(pl.multiple_of(keep * rows + step * height, 16), height)
                there = pl.ds(pl.multiple_of(offset * rows + step * height, 16), height)
                total = own[here, across].astype(F32) + came[there, :].astype(F32)
                own[here, across] = total.astype(BF16)

            loop(half * rows // height, add)
            self.grad_copy(name, stage + 1).start()
            return
        here = pl.ds(pl.multiple_of(keep * rows, 16), rows)
        there = pl.ds(offset * rows, rows)
        out = self.grad_out[array]
        total = own[here, across].astype(F32) + came[there, :].astype(F32)
        if array == SPATIAL_ONE:
            for tap in range(9):
                out[tap, :, 0:128] = total[tap * 16 : tap * 16 + 8]
                out[tap, :, 128:256] = total[tap * 16 + 8 : tap * 16 + 16]
        elif array == EXPAND_ONE:
            out[:, 0:512] = total[0:8]
            out[:, 512:1024] = total[8:16]
        else:
            out[part * rows : part * rows + rows, across] = total

    def grads_sent(self):
        for name in range(len(GRADS)):
            for stage in range(BITS):
                self.grad_copy(name, stage).wait_send()

    def grad_store(self, name, block, value, lanes=slice(None), row=0):
        array, rows, part, _, _, _ = GRADS[name]
        per = 16 if array == SPATIAL_TWO else rows
        count = 256 // per
        base = (part * SHARDS + self.place(name, block * count)) * rows + row
        for s in range(count):
            where = pl.multiple_of(base + self.place(name, s) * rows, 16)
            self.grads[array][pl.ds(where, per), lanes] = value[s * per : (s + 1) * per].astype(BF16)


    def run(self):
        self.greet()
        pairs = dict(
            xa=(self.xa_in, self.xa),
            xb=(self.xb_in, self.xb),
            w1=(self.w1_in, self.w1),
            ca=(self.ca_in, self.ca),
            cb=(self.cb_in, self.cb),
            w2=(self.w2_in, self.w2),
            w3=(self.w3_in, self.w3),
            w4=(self.w4_in, self.w4),
            ws=(self.ws_in, self.ws),
            w5=(self.w5_in, self.w5),
            w6=(self.w6_in, self.w6),
        )
        loads = SimpleNamespace()
        for i, name in enumerate(pairs):
            copy = pltpu.make_async_copy(*pairs[name], self.load_sem.at[i])
            copy.start()
            setattr(loads, name, copy)

        x, z1, z2, z3, z4, z5 = self.x, self.z1, self.z2, self.z3, self.z4, self.z5
        h1, h2, feed, h4, h5 = self.h1, self.h2, self.feed, self.h4, self.h5
        big, mask = self.big, self.mask
        rows, cols, views, _ = x.shape
        half = cols // 2
        natural = [2 * (k % half) + k // half for k in range(cols)]
        zeros = functools.partial(jnp.zeros, dtype=BF16)

        live_a = self.live[0, self.d]
        live_b = self.live[1, self.d]
        all_a = self.live[0, 0]
        all_b = self.live[1, 0]
        for i in range(1, self.d_size):
            all_a = all_a + self.live[0, i]
            all_b = all_b + self.live[1, i]
        line = jnp.zeros((1, 128), jnp.int32)
        line_a = (line + all_a).astype(F32)
        line_b = (line + all_b).astype(F32)
        full_one = HA * WA * line_a + HB * WB * line_b
        half_one = ((HA + 1) // 2) * ((WA + 1) // 2) * line_a + ((HB + 1) // 2) * (
            (WB + 1) // 2
        ) * line_b
        self.full_count[...] = full_one
        self.half_count[...] = half_one

        def full(lanes):
            return wide(self.full_count[...], lanes)

        def part(lanes):
            return wide(self.half_count[...], lanes)

        def make_mask(row):
            place = lax.broadcasted_iota(jnp.int32, (cols, views, 128), 0)
            column = jnp.where(place < half, 2 * place, 2 * (place - half) + 1)
            view = lax.broadcasted_iota(jnp.int32, (cols, views, 128), 1)
            where = self.r * rows + row
            tall_a = jnp.where(where < HA, live_a, 0)
            tall_b = jnp.where(where < HB, live_b, 0)
            in_a = (view < self.live_a) & (view < tall_a)
            in_b = (view >= self.live_a) & (view - self.live_a < tall_b) & (column < WB)
            mask[row] = jnp.where(in_a | in_b, 1.0, 0.0).astype(F32)

        loop(rows, make_mask)

        for ref in (h1, self.dz2):
            lanes = ref.shape[-1]
            ref[0] = zeros((cols + 2, views, lanes))
            ref[rows + 1] = zeros((cols + 2, views, lanes))
            for row in range(1, rows + 1):
                ref[row, 0] = zeros((views, lanes))
                ref[row, cols + 1] = zeros((views, lanes))
        h4[0] = zeros(h4.shape[1:])
        for row in range(1, rows + 1):
            h4[row, half] = zeros((views, h4.shape[-1]))
        self.dz5[rows // 2] = zeros(self.dz5.shape[1:])
        for row in range(rows // 2):
            self.dz5[row, half] = zeros((views, self.dz5.shape[-1]))

        def row_mask(row, lanes):
            return wide(flat(mask[row]), lanes)

        none = jnp.zeros((1, 256), F32)

        loads.xa.wait()
        loads.xb.wait()

        def gather_row(row):
            for k in range(cols):
                c = natural[k]
                near = self.xa[row, c].astype(F32)
                if c < self.xb.shape[1]:
                    rest = self.xb[row, c].astype(F32)
                else:
                    rest = jnp.zeros((self.live_b, near.shape[-1]), F32)
                value = jnp.concatenate([near, rest], axis=0)
                x[row, k] = (value * wide(mask[row, k], value.shape[-1])).astype(BF16)

        loop(rows, gather_row)
        loads.w1.wait()

        def reduce_row(row, carry):
            total, square = carry
            value = mm(flat(x[row]), self.w1[...])
            z1[row] = value.reshape(cols, views, -1)
            return (total + col_sum(value), square + col_sum(value * value))

        sums = loop(rows, reduce_row, (none, none))
        self.greeted()
        self.sum_start(AT_ONE, sums)
        self.sum_turn(AT_ONE)
        loads.ca.wait()
        loads.cb.wait()
        for o in range(rows // 2):
            for p in range(half):
                for h in range(2):
                    lanes = slice(h * LEAF, h * LEAF + LEAF)
                    near = self.ca[o, p, :, lanes].astype(F32)
                    if p < self.cb.shape[1]:
                        rest = self.cb[o, p, :, lanes].astype(F32)
                    else:
                        rest = jnp.zeros((self.live_b, LEAF), F32)
                    self.cot[h, o * half + p] = jnp.concatenate([near, rest], axis=0).astype(BF16)
        self.norm_ready(NARROW, self.sum_finish(AT_ONE), full(256))

        def hidden_one(row):
            value = self.act(NARROW, flat(z1[row]))
            value = (value * sigmoid(value) * row_mask(row, 256)).astype(BF16)
            value = value.reshape(cols, views, -1)
            for k in range(cols):
                h1[row + 1, natural[k] + 1] = value[k]

        first, last = self.r == 0, self.r == self.r_size - 1
        hidden_one(0)
        hidden_one(rows - 1)
        up = self.to_strip(-1, h1.at[1], h1.at[rows + 1], 0)
        down = self.to_strip(1, h1.at[rows], h1.at[0], 1)

        @pl.when(jnp.logical_not(first))
        def _():
            up.start()

        @pl.when(jnp.logical_not(last))
        def _():
            down.start()

        loop(rows - 2, lambda i: hidden_one(i + 1))
        loads.w2.wait()

        def conv_row(row, carry):
            total, square = carry
            value = 0.0
            for i in range(3):
                for j in range(3):
                    tap = (i * 3 + j) * 256
                    value = value + mm(flat(h1[row + i, j : j + cols]), self.w2[tap : tap + 256, :])
            value = value.reshape(cols, views, -1)
            ordered = jnp.concatenate([value[c] for c in natural], axis=0)
            z2[row] = ordered.reshape(cols, views, -1)
            kept = ordered * row_mask(row, 256)
            return (total + col_sum(kept), square + col_sum(kept * ordered))

        sums = loop(rows - 2, lambda i, carry: conv_row(i + 1, carry), (none, none))

        @pl.when(jnp.logical_not(last))
        def _():
            self.to_strip(1, h1.at[rows], h1.at[rows + 1], 0).wait_recv()

        @pl.when(jnp.logical_not(first))
        def _():
            self.to_strip(-1, h1.at[1], h1.at[0], 1).wait_recv()

        sums = conv_row(rows - 1, conv_row(0, sums))
        self.sum_start(AT_TWO, sums)
        self.sum_turn(AT_TWO)
        loads.w3.wait()
        self.norm_ready(SPATIAL, self.sum_finish(AT_TWO), full(256))

        def hidden_two(row):
            value = self.act(SPATIAL, flat(z2[row]))
            value = (value * sigmoid(value) * row_mask(row, 256)).astype(BF16)
            h2[row] = value.reshape(cols, views, -1)

        loop(rows, hidden_two)

        def expand_row(row, carry):
            given = flat(h2[row])
            done = []
            for n in range(2):
                lanes = slice(n * 512, n * 512 + 512)
                value = mm(given, self.w3[:, lanes])
                z3[row, :, :, lanes] = value.reshape(cols, views, -1)
                done.append((carry[n][0] + col_sum(value), carry[n][1] + col_sum(value * value)))
            return tuple(done)

        nothing = jnp.zeros((1, 512), F32)
        sums = loop(rows, expand_row, ((nothing, nothing), (nothing, nothing)))
        sums = [jnp.concatenate([sums[0][i], sums[1][i]], axis=1) for i in range(2)]
        self.sum_start(AT_THREE, sums)
        self.sum_turn(AT_THREE)
        loads.w4.wait()
        loads.ws.wait()
        self.norm_ready(WIDENED, self.sum_finish(AT_THREE), full(1024))

        def feed_step(step):
            row, pair = step // half, lax.rem(step, half)
            here = pl.ds(pair * 2, 2)
            value = self.act(WIDENED, flat(z3[row, here])) + flat(x[row, here]).astype(F32)
            value = value * sigmoid(value) * wide(flat(mask[row, here]), 1024)
            feed[row, here] = value.astype(BF16).reshape(2, views, -1)

        loop(rows * half, feed_step)

        def squeeze_row(row, carry):
            total, square = carry
            value = mm(flat(feed[row]), self.w4[...])
            z4[row] = value.reshape(cols, views, -1)
            return (total + col_sum(value), square + col_sum(value * value))

        sums = loop(rows, squeeze_row, (nothing, nothing))
        self.sum_start(AT_FOUR, sums)
        self.sum_turn(AT_FOUR)

        def even(ref):
            return jnp.concatenate([flat(ref[2 * o, 0:half]) for o in range(rows // 2)], axis=0)

        for h in range(2):
            sums = []
            for n in range(2):
                lanes = slice(h * LEAF + n * 512, h * LEAF + n * 512 + 512)
                value = mm(even(feed), self.ws[:, lanes])
                big[2 + h, :, :, n * 512 : n * 512 + 512] = value.reshape(cols, views, -1)
                sums.append((col_sum(value), col_sum(value * value)))
            for i in range(2):
                self.short_sum[i : i + 1, h * LEAF : h * LEAF + LEAF] = jnp.concatenate(
                    [sums[0][i], sums[1][i]], axis=1
                )
        self.sum_start(AT_SHORT, [self.short_sum[0:1, :], self.short_sum[1:2, :]])
        self.norm_ready(SQUEEZE, self.sum_finish(AT_FOUR), full(512))

        def hidden_four(row):
            for p in range(2):
                value = self.act(SQUEEZE, flat(z4[row, p * half : p * half + half]))
                value = value * sigmoid(value) * wide(flat(mask[row, p * half : p * half + half]), 512)
                start = p * (half + 1)
                h4[row + 1, start : start + half] = value.astype(BF16).reshape(half, views, -1)

        hidden_four(rows - 1)
        below = self.to_strip(1, h4.at[rows], h4.at[0], 2)

        @pl.when(jnp.logical_not(last))
        def _():
            below.start()

        loop(rows - 1, hidden_four)
        loads.w5.wait()
        starts = (half, 0, half + 1)

        def taken(i, j):
            return jnp.concatenate(
                [flat(h4[2 * o + i, starts[j] : starts[j] + half]) for o in range(rows // 2)], axis=0
            )

        value = 0.0
        for i in (1, 2, 0):
            if i == 0:

                @pl.when(jnp.logical_not(first))
                def _():
                    self.to_strip(-1, h4.at[rows], h4.at[0], 2).wait_recv()

            for j in range(3):
                tap = (i * 3 + j) * 512
                value = value + mm(taken(i, j), self.w5[tap : tap + 512, :])
        z5[...] = value
        half_mask = jnp.concatenate(
            [flat(mask[2 * o, 0:half]) for o in range(rows // 2)], axis=0
        )
        self.half_mask[...] = half_mask
        kept = value * wide(half_mask, 512)
        self.sum_start(AT_FIVE, (col_sum(kept), col_sum(kept * value)))
        self.sum_turn(AT_FIVE)
        self.sum_turn(AT_SHORT)
        loads.w6.wait()
        self.norm_ready(STRIDED, self.sum_finish(AT_FIVE), part(512))
        value = self.act(STRIDED, z5[...])
        h5[...] = (value * sigmoid(value) * wide(self.half_mask[...], 512)).astype(BF16)

        for h in range(2):
            sums = []
            for n in range(2):
                lanes = slice(h * LEAF + n * 512, h * LEAF + n * 512 + 512)
                value = mm(h5[...], self.w6[:, lanes])
                big[h, :, :, n * 512 : n * 512 + 512] = value.reshape(cols, views, -1)
                sums.append((col_sum(value), col_sum(value * value)))
            for i in range(2):
                self.main_sum[i : i + 1, h * LEAF : h * LEAF + LEAF] = jnp.concatenate(
                    [sums[0][i], sums[1][i]], axis=1
                )
        self.sum_start(AT_SIX, [self.main_sum[0:1, :], self.main_sum[1:2, :]])
        self.norm_ready(SHORTCUT, self.sum_finish(AT_SHORT), part(2048))
        self.sum_turn(AT_SIX)
        self.norm_ready(OUTPUT, self.sum_finish(AT_SIX), part(2048))

        top, cot = self.top, self.cot
        zero = jnp.zeros((1, LEAF), F32)
        for h in range(2):
            lanes = slice(h * LEAF, h * LEAF + LEAF)

            def out_step(pair, carry):
                here = pl.ds(pair * 2, 2)
                main, side = flat(big[h, here]), flat(big[2 + h, here])
                value = self.act(OUTPUT, main, lanes) + self.act(SHORTCUT, side, lanes)
                there = wide(self.half_mask[pl.ds(pl.multiple_of(pair * 2 * views, 8), 2 * views), :], LEAF)
                sigma = sigmoid(value)
                given = flat(cot[h, here]).astype(F32)
                slope = given * there * (sigma * (1.0 + value * (1.0 - sigma)))
                cot[h, here] = (value * sigma * there).astype(BF16).reshape(2, views, -1)
                top[h, here] = slope.reshape(2, views, -1)
                return (
                    carry[0] + col_sum(slope),
                    carry[1] + col_sum(slope * self.off_mean(OUTPUT, main, lanes)),
                    carry[2] + col_sum(slope * self.off_mean(SHORTCUT, side, lanes)),
                )

            sums = loop(half, out_step, (zero, zero, zero))
            for i in range(3):
                self.top_sum[i : i + 1, lanes] = sums[i]
        self.sum_start(AT_SEVEN, [self.top_sum[i : i + 1, :] for i in range(3)])
        for o in range(rows // 2):
            for p in range(half):
                for h in range(2):
                    lanes = slice(h * LEAF, h * LEAF + LEAF)
                    done = cot[h, o * half + p].astype(F32)
                    self.ca[o, p, :, lanes] = done[0 : self.live_a].astype(BF16)
                    if p < self.cb.shape[1]:
                        self.cb[o, p, :, lanes] = done[self.live_a :].astype(BF16)
        stores = [
            pltpu.make_async_copy(self.ca, self.out_a_to, self.store_sem.at[0]),
            pltpu.make_async_copy(self.cb, self.out_b_to, self.store_sem.at[1]),
        ]
        for copy in stores:
            copy.start()
        self.sum_turn(AT_SEVEN)
        totals = self.sum_finish(AT_SEVEN)
        self.norm_back_ready(OUTPUT, totals[0:1], totals[1:2], part(2048))
        self.norm_back_ready(SHORTCUT, totals[0:1], totals[2:3], part(2048))

        dz6, dzs = self.dz6, self.dzs
        for h in range(2):
            lanes = slice(h * LEAF, h * LEAF + LEAF)

            def top_step(pair):
                here = pl.ds(pair * 2, 2)
                there = pl.ds(pl.multiple_of(pair * 2 * views, 16), 2 * views)
                live = wide(self.half_mask[there, :], LEAF)
                slope = flat(top[h, here])
                dz6[there, lanes] = self.back(OUTPUT, slope, flat(big[h, here]), live, lanes)
                dzs[there, lanes] = self.back(SHORTCUT, slope, flat(big[2 + h, here]), live, lanes)

            loop(half, top_step)

        value = mm_nt(dz6[...], self.w6[...]) * slope_of(self.act(STRIDED, z5[...]))
        self.slope5[...] = value
        self.sum_start(AT_EIGHT, (col_sum(value), col_sum(value * self.off_mean(STRIDED, z5[...]))))

        for name in EXPAND_TWO_PARTS:
            first_lane = GRADS[name][3]

            def grad_expand_two(step):
                m, n = step // 2, lax.rem(step, 2)
                left = h5[:, pl.ds(pl.multiple_of(m * 256, 256), 256)]
                lanes = pl.ds(pl.multiple_of(first_lane + n * 512, 512), 512)
                self.grad_store(name, m, mm_tn(left, dz6[:, lanes]), lanes)

            loop(4, grad_expand_two)
            self.grad_start(name)

        def clear(row):
            big[row] = jnp.zeros(big.shape[1:], F32)

        loop(rows, clear)

        def shortcut_back(n):
            lanes = pl.ds(pl.multiple_of(n * 256, 256), 256)
            value = mm_nt(dzs[...], self.ws[lanes, :]).reshape(rows // 2, half, views, -1)
            for o in range(rows // 2):
                big[2 * o, 0:half, :, lanes] = value[o]

        loop(4, shortcut_back)

        def grad_shortcut_two(m):
            here = pl.ds(pl.multiple_of(m * 256, 256), 256)
            left = jnp.concatenate(
                [flat(feed[2 * o, 0:half, :, here]) for o in range(rows // 2)], axis=0
            )
            for name in SHORTCUT_TWO_PARTS:
                lanes = slice(GRADS[name][3], GRADS[name][3] + GRADS[name][4])
                self.grad_store(name, m, mm_tn(left, dzs[:, lanes]), lanes)

        loop(4, grad_shortcut_two)
        for name in SHORTCUT_TWO_PARTS:
            self.grad_start(name)
        self.grad_steps(0, *EXPAND_TWO_PARTS)
        self.sum_turn(AT_EIGHT)
        totals = self.sum_finish(AT_EIGHT)
        self.norm_back_ready(STRIDED, totals[0:1], totals[1:2], part(512))
        dz5 = self.dz5
        value = self.back(STRIDED, self.slope5[...], z5[...], wide(self.half_mask[...], 512))
        for o in range(rows // 2):
            dz5[o, 0:half] = value[o * half * views : (o + 1) * half * views].reshape(half, views, -1)
        above = self.to_strip(-1, dz5.at[0], dz5.at[rows // 2], 3)

        @pl.when(jnp.logical_not(first))
        def _():
            above.start()

        dh4 = self.dh4
        for i in (1, 2, 0):
            if i == 0:

                @pl.when(jnp.logical_not(last))
                def _():
                    self.to_strip(1, dz5.at[0], dz5.at[rows // 2], 3).wait_recv()

            lead = 1 if i == 0 else 0
            for j in (1, 2, 0):
                tap = (i * 3 + j) * 512
                start = 1 if j == 0 else 0
                given = jnp.concatenate(
                    [flat(dz5[o + lead, start : start + half]) for o in range(rows // 2)], axis=0
                )
                value = mm_nt(given, self.w5[tap : tap + 512, :]).reshape(rows // 2, half, views, -1)
                spot = slice(0, half) if j == 1 else slice(half, 2 * half)
                for o in range(rows // 2):
                    target = 2 * o if i == 1 else 2 * o + 1
                    if j == 0 or i == 0:
                        dh4[target, spot] = dh4[target, spot] + value[o]
                    else:
                        dh4[target, spot] = value[o]

        def slope_four(step, carry):
            row, p = step // 2, lax.rem(step, 2)
            here = pl.ds(p * half, half)
            before = flat(z4[row, here])
            value = flat(dh4[row, here]) * slope_of(self.act(SQUEEZE, before))
            dh4[row, here] = value.reshape(half, views, -1)
            return (
                carry[0] + col_sum(value),
                carry[1] + col_sum(value * self.off_mean(SQUEEZE, before)),
            )

        sums = loop(rows * 2, slope_four, (nothing, nothing))
        self.sum_start(AT_NINE, sums)
        self.sum_turn(AT_NINE)
        self.grad_steps(0, *SHORTCUT_TWO_PARTS)
        self.grad_steps(1, *EXPAND_TWO_PARTS)

        for i, name in enumerate(SPATIAL_TWO_PARTS):

            def grad_spatial_two(step):
                j, m = step // 2, lax.rem(step, 2)
                here = pl.ds(pl.multiple_of(m * 256, 256), 256)
                start = half * ((1 - j) * (2 - j) // 2) + (half + 1) * (j * (j + 1) // 2 - j)
                left = jnp.concatenate(
                    [flat(h4[2 * o + i, pl.ds(start, half), :, here]) for o in range(rows // 2)], axis=0
                )
                right = jnp.concatenate([flat(dz5[o, 0:half]) for o in range(rows // 2)], axis=0)
                self.grad_store(name, m, mm_tn(left, right), row=j * 16)

            loop(6, grad_spatial_two)
            self.grad_start(name)
        totals = self.sum_finish(AT_NINE)
        self.norm_back_ready(SQUEEZE, totals[0:1], totals[1:2], full(512))
        dz4 = self.dz4

        def back_four(step):
            row, p = step // 2, lax.rem(step, 2)
            here = pl.ds(p * half, half)
            value = self.back(
                SQUEEZE, flat(dh4[row, here]), flat(z4[row, here]), wide(flat(mask[row, here]), 512)
            )
            dz4[row, here] = value.reshape(half, views, -1)

        loop(rows * 2, back_four)

        def slope_three(row, carry):
            done = []
            for n in range(2):
                lanes = slice(n * 512, n * 512 + 512)
                before = flat(z3[row, :, :, lanes])
                grad = mm_nt(flat(dz4[row]), self.w4[lanes, :]) + flat(big[row, :, :, lanes])
                point = self.act(WIDENED, before, lanes) + flat(x[row, :, :, lanes]).astype(F32)
                value = grad * slope_of(point)
                big[row, :, :, lanes] = value.reshape(cols, views, -1)
                done.append(
                    (
                        carry[n][0] + col_sum(value),
                        carry[n][1] + col_sum(value * self.off_mean(WIDENED, before, lanes)),
                    )
                )
            return tuple(done)

        sums = loop(rows, slope_three, ((nothing, nothing), (nothing, nothing)))
        sums = [jnp.concatenate([sums[0][i], sums[1][i]], axis=1) for i in range(2)]
        self.sum_start(AT_TEN, sums)
        self.sum_turn(AT_TEN)
        self.grad_steps(0, *SPATIAL_TWO_PARTS)
        self.grad_steps(2, *EXPAND_TWO_PARTS)

        def grad_reduce_two(m):
            here = pl.ds(pl.multiple_of(m * 256, 256), 256)
            left = feed[:, :, :, here].reshape(-1, 256)
            self.grad_store(G_REDUCE_TWO, m, mm_tn(left, dz4[...].reshape(-1, 512)))

        loop(4, grad_reduce_two)
        self.grad_start(G_REDUCE_TWO)
        totals = self.sum_finish(AT_TEN)
        self.norm_back_ready(WIDENED, totals[0:1], totals[1:2], full(1024))
        dz3 = feed

        def back_three(step):
            row, pair = step // half, lax.rem(step, half)
            here = pl.ds(pair * 2, 2)
            live = wide(flat(mask[row, here]), 1024)
            value = self.back(WIDENED, flat(big[row, here]), flat(z3[row, here]), live)
            dz3[row, here] = value.reshape(2, views, -1)

        loop(rows * half, back_three)


        def slope_spatial(row, carry):
            before = flat(z2[row])
            value = mm_nt(flat(dz3[row]), self.w3[...]) * slope_of(self.act(SPATIAL, before))
            dh4[row, :, :, 0:256] = value.reshape(cols, views, -1)
            return (
                carry[0] + col_sum(value),
                carry[1] + col_sum(value * self.off_mean(SPATIAL, before)),
            )

        sums = loop(rows, slope_spatial, (none, none))
        self.sum_start(AT_ELEVEN, sums)
        self.sum_turn(AT_ELEVEN)
        self.grad_step(G_REDUCE_TWO, 0)
        self.grad_steps(1, *SHORTCUT_TWO_PARTS)
        self.grad_steps(3, *EXPAND_TWO_PARTS)

        left = h2[...].reshape(-1, 256)
        g_low = mm_tn(left, dz3[:, :, :, 0:512].reshape(-1, 512))
        g_high = mm_tn(left, dz3[:, :, :, 512:1024].reshape(-1, 512))
        for s in range(SHARDS):
            at = self.place(G_EXPAND_ONE, s) * 16
            piece = jnp.concatenate([g_low[s * 8 : s * 8 + 8], g_high[s * 8 : s * 8 + 8]], axis=0)
            self.grads[EXPAND_ONE][at : at + 16, :] = piece.astype(BF16)
        self.grad_start(G_EXPAND_ONE)
        totals = self.sum_finish(AT_ELEVEN)
        self.norm_back_ready(SPATIAL, totals[0:1], totals[1:2], full(256))
        dz2 = self.dz2

        def back_two(row):
            value = self.back(SPATIAL, flat(dh4[row, :, :, 0:256]), flat(z2[row]), row_mask(row, 256))
            value = value.reshape(cols, views, -1)
            for k in range(cols):
                dz2[row + 1, natural[k] + 1] = value[k]

        back_two(0)
        back_two(rows - 1)
        up = self.to_strip(-1, dz2.at[1], dz2.at[rows + 1], 4)
        down = self.to_strip(1, dz2.at[rows], dz2.at[0], 5)

        @pl.when(jnp.logical_not(first))
        def _():
            up.start()

        @pl.when(jnp.logical_not(last))
        def _():
            down.start()

        loop(rows - 2, lambda i: back_two(i + 1))
        for i in range(3):
            for j in range(3):
                left = h1[i : i + rows, j : j + cols].reshape(-1, 256)
                value = mm_tn(left, dz2[1 : rows + 1, 1 : cols + 1].reshape(-1, 256))
                for s in range(SHARDS):
                    at = self.place(G_SPATIAL_ONE, s) * 144 + (i * 3 + j) * 16
                    piece = value[s * 8 : s * 8 + 8]
                    piece = jnp.concatenate([piece[:, 0:128], piece[:, 128:256]], axis=0)
                    self.grads[SPATIAL_ONE][at : at + 16, :] = piece.astype(BF16)
        self.grad_start(G_SPATIAL_ONE)

        @pl.when(jnp.logical_not(last))
        def _():
            self.to_strip(1, dz2.at[rows], dz2.at[rows + 1], 4).wait_recv()

        @pl.when(jnp.logical_not(first))
        def _():
            self.to_strip(-1, dz2.at[1], dz2.at[0], 5).wait_recv()

        def slope_narrow(row, carry):
            value = 0.0
            for i in range(3):
                for j in range(3):
                    tap = (i * 3 + j) * 256
                    given = flat(dz2[row + 2 - i, 2 - j : 2 - j + cols])
                    value = value + mm_nt(given, self.w2[tap : tap + 256, :])
            value = value.reshape(cols, views, -1)
            value = jnp.concatenate([value[c] for c in natural], axis=0)
            before = flat(z1[row])
            value = value * row_mask(row, 256) * slope_of(self.act(NARROW, before))
            dh4[row, :, :, 0:256] = value.reshape(cols, views, -1)
            return (
                carry[0] + col_sum(value),
                carry[1] + col_sum(value * self.off_mean(NARROW, before)),
            )

        sums = loop(rows, slope_narrow, (none, none))
        self.sum_start(AT_TWELVE, sums)
        self.sum_turn(AT_TWELVE)
        self.grad_step(G_SPATIAL_ONE, 0)
        self.grad_steps(1, *SPATIAL_TWO_PARTS)
        self.grad_steps(2, *SHORTCUT_TWO_PARTS)
        self.grad_step(G_EXPAND_ONE, 0)
        self.grad_step(G_REDUCE_TWO, 1)
        self.grad_steps(4, *EXPAND_TWO_PARTS)
        totals = self.sum_finish(AT_TWELVE)
        self.norm_back_ready(NARROW, totals[0:1], totals[1:2], full(256))
        dz1 = h2

        def back_one(row):
            value = self.back(NARROW, flat(dh4[row, :, :, 0:256]), flat(z1[row]), row_mask(row, 256))
            dz1[row] = value.reshape(cols, views, -1)

        loop(rows, back_one)

        def grad_reduce_one(m):
            here = pl.ds(pl.multiple_of(m * 256, 256), 256)
            left = x[:, :, :, here].reshape(-1, 256)
            self.grad_store(G_REDUCE_ONE, m, mm_tn(left, dz1[...].reshape(-1, 256)))

        loop(4, grad_reduce_one)
        self.grad_start(G_REDUCE_ONE)

        def input_row(row):
            for n in range(2):
                lanes = slice(n * 512, n * 512 + 512)
                value = mm_nt(flat(dz1[row]), self.w1[lanes, :]) + flat(big[row, :, :, lanes])
                value = value.reshape(cols, views, -1)
                for k in range(cols):
                    self.xa[row, natural[k], :, lanes] = value[k, 0 : self.live_a].astype(BF16)
                    if natural[k] < self.xb.shape[1]:
                        self.xb[row, natural[k], :, lanes] = value[k, self.live_a :].astype(BF16)

        loop(rows, input_row)
        for i, pair in enumerate(((self.xa, self.in_a_to), (self.xb, self.in_b_to))):
            copy = pltpu.make_async_copy(*pair, self.store_sem.at[2 + i])
            copy.start()
            stores.append(copy)
        self.grad_step(G_REDUCE_ONE, 0)
        self.grad_step(G_SPATIAL_ONE, 1)
        self.grad_step(G_EXPAND_ONE, 1)
        self.grad_step(G_REDUCE_TWO, 2)
        self.grad_steps(3, *SHORTCUT_TWO_PARTS)
        self.grad_steps(2, *SPATIAL_TWO_PARTS)
        self.grad_step(G_REDUCE_ONE, 1)
        self.grad_step(G_SPATIAL_ONE, 2)
        self.grad_step(G_EXPAND_ONE, 2)
        self.grad_step(G_REDUCE_TWO, 3)
        self.grad_steps(4, *SHORTCUT_TWO_PARTS)
        self.grad_steps(3, *SPATIAL_TWO_PARTS)
        self.grad_step(G_REDUCE_ONE, 2)
        self.grad_step(G_SPATIAL_ONE, 3)
        self.grad_step(G_EXPAND_ONE, 3)
        self.grad_step(G_REDUCE_TWO, 4)
        self.grad_steps(4, *SPATIAL_TWO_PARTS)
        self.grad_step(G_REDUCE_ONE, 3)
        self.grad_steps(4, G_SPATIAL_ONE, G_EXPAND_ONE)
        self.grad_step(G_REDUCE_ONE, 4)

        for copy in stores:
            copy.wait()
        self.sums_sent()
        self.grads_sent()

        @pl.when(jnp.logical_not(first))
        def _():
            self.to_strip(-1, h1.at[1], h1.at[rows + 1], 0).wait_send()
            self.to_strip(-1, dz5.at[0], dz5.at[rows // 2], 3).wait_send()
            self.to_strip(-1, dz2.at[1], dz2.at[rows + 1], 4).wait_send()

        @pl.when(jnp.logical_not(last))
        def _():
            self.to_strip(1, h1.at[rows], h1.at[0], 1).wait_send()
            self.to_strip(1, h4.at[rows], h4.at[0], 2).wait_send()
            self.to_strip(1, dz2.at[rows], dz2.at[0], 5).wait_send()


def settle(*refs):
    half = len(refs) // 2
    for i in range(half):
        refs[half + i][...] = refs[i][...]


def settled(values):
    inside = pl.BlockSpec(memory_space=pltpu.VMEM)
    return pl.pallas_call(
        settle,
        out_shape=[jax.ShapeDtypeStruct(v.shape, v.dtype) for v in values],
        in_specs=[inside] * len(values),
        out_specs=[inside] * len(values),
    )(*values)


def sum_of(pay, near, mid, far, sems):
    return SimpleNamespace(direct=far is None, pay=pay, near=near, mid=mid, far=far, sems=sems)


def both_blocks(given, live_views, weights, gains, biases):
    d_size, r_size = lax.axis_size("dp"), lax.axis_size("rows")
    total = d_size * r_size
    rows, cols, views_a, c_in = given[0].shape
    views_b = given[1].shape[2]
    views = views_a + views_b
    half = cols // 2
    c_mid, c_mid2, c_out = gains[0].shape[1], gains[3].shape[1], gains[5].shape[1]
    pixels = (rows // 2) * half * views
    vmem, dma = pltpu.VMEM, pltpu.SemaphoreType.DMA
    anywhere = pl.BlockSpec(memory_space=pl.ANY)
    inside = pl.BlockSpec(memory_space=pltpu.VMEM)

    def full(lanes, kind):
        return vmem((rows, cols, views, lanes), kind)

    def like(value):
        return vmem(value.shape, value.dtype)

    sums = []
    for count, lanes, straight in SUMS:
        direct = straight and total <= 32
        sums.append(
            dict(
                pay=vmem((count, lanes), F32),
                near=vmem((total if direct else r_size, count, lanes), F32),
                mid=None if direct else vmem((count, lanes), F32),
                far=None if direct else vmem((d_size, count, lanes), F32),
                sems=dma((4,)),
            )
        )
    w = weights
    scratch = dict(
        xa=like(given[0]),
        xb=like(given[1]),
        ca=like(given[2]),
        cb=like(given[3]),
        x=full(c_in, BF16),
        w1=like(w[0]),
        w2=like(w[1]),
        w3=like(w[2]),
        w4=like(w[3]),
        w5=like(w[4]),
        w6=like(w[5]),
        ws=like(w[6]),
        cot=vmem((2, cols, views, LEAF), BF16),
        mask=full(128, F32),
        half_mask=vmem((pixels, 128), F32),
        full_count=vmem((1, 128), F32),
        half_count=vmem((1, 128), F32),
        z1=full(c_mid, F32),
        z2=full(c_mid, F32),
        z3=full(c_in, F32),
        z4=full(c_mid2, F32),
        z5=vmem((pixels, c_mid2), F32),
        h1=vmem((rows + 2, cols + 2, views, c_mid), BF16),
        h2=full(c_mid, BF16),
        feed=full(c_in, BF16),
        h4=vmem((rows + 1, cols + 1, views, c_mid2), BF16),
        h5=vmem((pixels, c_mid2), BF16),
        big=full(c_in, F32),
        top=vmem((2, cols, views, LEAF), F32),
        short_sum=vmem((2, c_out), F32),
        main_sum=vmem((2, c_out), F32),
        top_sum=vmem((3, c_out), F32),
        dz6=vmem((pixels, c_out), BF16),
        dzs=vmem((pixels, c_out), BF16),
        slope5=vmem((pixels, c_mid2), F32),
        dz5=vmem((rows // 2 + 1, half + 1, views, c_mid2), BF16),
        dh4=full(c_mid2, F32),
        dz4=full(c_mid2, BF16),
        dz2=vmem((rows + 2, cols + 2, views, c_mid), BF16),
        g2=vmem((SHARDS * 144, 128), BF16),
        g3=vmem((SHARDS * 16, 512), BF16),
        load_sem=dma((11,)),
        store_sem=dma((4,)),
        halo_send=dma((6,)),
        halo_recv=dma((6,)),
        grad_send=dma((len(GRADS) * BITS,)),
        grad_recv=dma((len(GRADS) * BITS,)),
        coef=[vmem((8, gain.shape[1]), F32) for gain in gains],
        recv=[vmem(((SHARDS - 1) * height, lanes), BF16) for _, height, _, _, lanes, _ in GRADS],
        sums=sums,
    )
    grad_shapes = ((32, 256), (9, 8, 256), (8, 1024), (32, 512), (144, 512), (16, 2048), (32, 2048))
    ins = dict(
        live=live_views,
        xa_in=given[0],
        xb_in=given[1],
        ca_in=given[2],
        cb_in=given[3],
        w1_in=w[0],
        w2_in=w[1],
        w3_in=w[2],
        w4_in=w[3],
        w5_in=w[4],
        w6_in=w[5],
        ws_in=w[6],
        gain=list(gains),
        bias=list(biases),
    )
    shape = jax.ShapeDtypeStruct
    outs = dict(
        out_a_to=shape(given[2].shape, BF16),
        out_b_to=shape(given[3].shape, BF16),
        in_a_to=shape(given[0].shape, BF16),
        in_b_to=shape(given[1].shape, BF16),
        grad_out=[shape(s, F32) for s in grad_shapes],
        grad_gain=[shape(g.shape, F32) for g in gains],
        grad_bias=[shape(g.shape, F32) for g in gains],
    )
    parts = []
    trees = []
    for group in (ins, outs, scratch):
        leaves, tree = jax.tree.flatten(group, is_leaf=lambda v: not isinstance(v, (dict, list, type(None))))
        parts.append(leaves)
        trees.append(tree)
    in_specs = dict(ins)
    for name in ins:
        in_specs[name] = [inside] * len(gains) if isinstance(ins[name], list) else anywhere
    in_specs.update(live=pl.BlockSpec(memory_space=pltpu.SMEM))
    out_specs = {
        name: [inside] * len(outs[name]) if isinstance(outs[name], list) else anywhere for name in outs
    }
    spec_leaves = [
        jax.tree.flatten(group, is_leaf=lambda v: isinstance(v, pl.BlockSpec))[0]
        for group in (in_specs, out_specs)
    ]

    def body(*refs):
        fields = {}
        start = 0
        for leaves, tree in zip(parts, trees):
            fields.update(jax.tree.unflatten(tree, refs[start : start + len(leaves)]))
            start += len(leaves)
        g = SimpleNamespace(**fields)
        fields.update(
            grads=[g.w2, g.g2, g.g3, g.w4, g.w5, g.w6, g.ws],
            sums=[sum_of(**s) for s in g.sums],
        )
        Kernel((d_size, r_size, views_a, views_b), fields).run()

    results = pl.pallas_call(
        body,
        out_shape=parts[1],
        in_specs=spec_leaves[0],
        out_specs=spec_leaves[1],
        scratch_shapes=parts[2],
        compiler_params=pltpu.CompilerParams(
            collective_id=0, has_side_effects=True, vmem_limit_bytes=64 * 2**20 - 65536 * 4
        ),
        cost_estimate=pl.CostEstimate(flops=16 * 10**9, bytes_accessed=30 * 10**6, transcendentals=4 * 10**6),
    )(*parts[0])
    done = SimpleNamespace(**jax.tree.unflatten(trees[1], results))
    plain = settled([done.out_a_to, done.in_a_to, *done.grad_out, *done.grad_gain, *done.grad_bias])
    return plain[0], done.out_b_to, plain[1], done.in_b_to, list(plain[2:9]), plain[9:]


def on_device(input_a, input_b, live_views, *rest):
    weights, params, cotangents = rest[:7], rest[7:21], rest[21:]
    gains = [value.reshape(1, -1) for value in params[0::2]]
    biases = [value.reshape(1, -1) for value in params[1::2]]
    reduce_one, spatial_one, expand_one, reduce_two, spatial_two, expand_two, shortcut_two = weights
    weights = (
        reduce_one,
        spatial_one.transpose(1, 2, 0, 3).reshape(-1, spatial_one.shape[-1]),
        expand_one,
        reduce_two,
        spatial_two.transpose(1, 2, 0, 3).reshape(-1, spatial_two.shape[-1]),
        expand_two,
        shortcut_two,
    )
    given = [value.transpose(0, 2, 1, 3) for value in (input_a, input_b, *cotangents)]
    *moved, grads, norms = both_blocks(given, live_views.T, weights, gains, biases)
    maps = [value.transpose(0, 2, 1, 3) for value in moved]
    grads[1] = grads[1].reshape(3, 3, -1, grads[1].shape[-1]).transpose(2, 0, 1, 3)
    grads[4] = grads[4].reshape(3, 3, -1, grads[4].shape[-1]).transpose(2, 0, 1, 3)
    if lax.axis_size("dp") * lax.axis_size("rows") > SHARDS:
        grads = [lax.psum_scatter(g, "rows", scatter_dimension=0, tiled=True) for g in grads]
    small = []
    for i in range(7):
        small += [norms[i].reshape(-1), norms[7 + i].reshape(-1)]
    return (*maps, *grads, *small)


def solution(mesh):
    split = P("rows", "dp", None, None)
    whole = P()
    shard = P(("dp", "rows"), None)
    shard_4 = P(("dp", "rows"), None, None, None)
    return jax.shard_map(
        on_device,
        mesh=mesh,
        in_specs=(split, split) + (whole,) * 22 + (split, split),
        out_specs=(split,) * 4
        + (shard, shard_4, shard, shard, shard_4, shard, shard)
        + (whole,) * 14,
        check_vma=False,
    )
```

```python
import functools
from types import SimpleNamespace

import jax
import jax.numpy as jnp
from jax import lax
from jax.experimental import pallas as pl
from jax.experimental.pallas import tpu as pltpu
from jax.sharding import PartitionSpec as P

MESH = pl.DeviceIdType.MESH
F32 = jnp.float32
BF16 = jnp.bfloat16

HA = 14
WA = 14
HB = 10
WB = 10

EPS = 1e-05
LEAF = 1024
NARROW, SPATIAL, WIDENED, SQUEEZE, STRIDED, OUTPUT, SHORTCUT = range(7)
Y_FIRST = (0, 1, 2, 3, 4)
X_FIRST = (0, 2, 1, 3, 4)
Z_FIRST = (0, 3, 2, 1, 4)
BITS = 5
SHARDS = 1 << BITS
REDUCE_ONE, SPATIAL_ONE, EXPAND_ONE, REDUCE_TWO, SPATIAL_TWO, EXPAND_TWO, SHORTCUT_TWO = range(7)
(
    G_REDUCE_ONE,
    G_SPATIAL_ONE,
    G_EXPAND_ONE,
    G_REDUCE_TWO,
    G_SPATIAL_TWO_0,
    G_SPATIAL_TWO_1,
    G_SPATIAL_TWO_2,
    G_EXPAND_TWO_0,
    G_EXPAND_TWO_1,
    G_SHORTCUT_TWO_0,
    G_SHORTCUT_TWO_1,
    G_SHORTCUT_TWO_2,
) = range(12)
GRADS = (
    (REDUCE_ONE, 32, 0, 0, 256, Y_FIRST),
    (SPATIAL_ONE, 144, 0, 0, 128, Z_FIRST),
    (EXPAND_ONE, 16, 0, 0, 512, Y_FIRST),
    (REDUCE_TWO, 32, 0, 0, 512, Z_FIRST),
    (SPATIAL_TWO, 48, 0, 0, 512, Y_FIRST),
    (SPATIAL_TWO, 48, 1, 0, 512, X_FIRST),
    (SPATIAL_TWO, 48, 2, 0, 512, Z_FIRST),
    (EXPAND_TWO, 16, 0, 0, 1024, X_FIRST),
    (EXPAND_TWO, 16, 0, 1024, 1024, Z_FIRST),
    (SHORTCUT_TWO, 32, 0, 0, 768, Z_FIRST),
    (SHORTCUT_TWO, 32, 0, 768, 640, Y_FIRST),
    (SHORTCUT_TWO, 32, 0, 1408, 640, X_FIRST),
)
SPATIAL_TWO_PARTS = (G_SPATIAL_TWO_0, G_SPATIAL_TWO_1, G_SPATIAL_TWO_2)
EXPAND_TWO_PARTS = (G_EXPAND_TWO_0, G_EXPAND_TWO_1)
SHORTCUT_TWO_PARTS = (G_SHORTCUT_TWO_0, G_SHORTCUT_TWO_1, G_SHORTCUT_TWO_2)
(
    AT_ONE,
    AT_TWO,
    AT_THREE,
    AT_FOUR,
    AT_FIVE,
    AT_SHORT,
    AT_SIX,
    AT_SEVEN,
    AT_EIGHT,
    AT_NINE,
    AT_TEN,
    AT_ELEVEN,
    AT_TWELVE,
) = range(13)
SUMS = (
    (2, 256, True),
    (2, 256, True),
    (2, 1024, False),
    (2, 512, True),
    (2, 512, True),
    (2, 2048, False),
    (2, 2048, False),
    (1, 6144, False),
    (2, 512, True),
    (2, 512, True),
    (2, 1024, False),
    (2, 256, True),
    (2, 256, True),
)


def mm(left, right):
    return lax.dot_general(left, right, (((1,), (0,)), ((), ())), preferred_element_type=F32)


def mm_nt(left, right):
    return lax.dot_general(left, right, (((1,), (1,)), ((), ())), preferred_element_type=F32)


def mm_tn(left, right):
    return lax.dot_general(left, right, (((0,), (0,)), ((), ())), preferred_element_type=F32)


def sigmoid(value):
    return 0.5 + 0.5 * jnp.tanh(0.5 * value)


def slope_of(value):
    sigma = sigmoid(value)
    return sigma * (1.0 + value * (1.0 - sigma))


def flat(block):
    return block.reshape(-1, block.shape[-1])


def col_sum(value):
    return jnp.sum(value, axis=0, keepdims=True)


def wide(mask, lanes):
    return jnp.concatenate([mask] * (lanes // 128), axis=1)


def loop(count, body, init=None):
    if init is None:

        def plain(step, carry):
            body(step)
            return carry

        return lax.fori_loop(0, count, plain, 0)
    return lax.fori_loop(0, count, body, init)


def bit_of(number, bit):
    return lax.rem(number // (1 << bit), 2)


class Kernel:
    def __init__(self, sizes, refs):
        self.d_size, self.r_size, self.live_a, self.live_b = sizes
        self.total = self.d_size * self.r_size
        self.__dict__.update(refs)
        self.d = lax.axis_index("dp")
        self.r = lax.axis_index("rows")
        self.me = self.d * self.r_size + self.r
        self.low = (self.total // SHARDS).bit_length() - 1
        self.shard = self.me // (1 << self.low)
        self.r_bits = self.r_size.bit_length() - 1


    def device(self, number):
        return (number // self.r_size, lax.rem(number, self.r_size))

    def greet(self):
        barrier = pltpu.get_barrier_semaphore()

        def one(step):
            pl.semaphore_signal(
                barrier,
                inc=1,
                device_id=self.device(lax.rem(self.me + step + 1, self.total)),
                device_id_type=MESH,
            )

        loop(self.total - 1, one)

    def greeted(self):
        pl.semaphore_wait(pltpu.get_barrier_semaphore(), self.total - 1)

    def direct(self, name):
        return self.sums[name].direct

    def sum_start(self, name, vectors):
        s = self.sums[name]
        for i, vector in enumerate(vectors):
            s.pay[i : i + 1, :] = vector
        if s.direct:

            def send(step):
                pltpu.make_async_remote_copy(
                    s.pay,
                    s.near.at[self.me],
                    s.sems.at[0],
                    s.sems.at[1],
                    device_id=self.device(lax.rem(self.me + step + 1, self.total)),
                    device_id_type=MESH,
                ).start()

            loop(self.total - 1, send)
            s.near[self.me] = s.pay[...]
        else:
            for step in range(1, self.r_size):
                pltpu.make_async_remote_copy(
                    s.pay,
                    s.near.at[self.r],
                    s.sems.at[0],
                    s.sems.at[1],
                    device_id=(self.d, lax.rem(self.r + step, self.r_size)),
                    device_id_type=MESH,
                ).start()
            s.near[self.r] = s.pay[...]

    def sum_turn(self, name):
        s = self.sums[name]
        if s.direct:
            return
        several = s.near.at[0 : self.r_size - 1]
        pltpu.make_async_copy(several, several, s.sems.at[1]).wait()
        s.mid[...] = jnp.sum(s.near[...], axis=0)

        def send(step):
            pltpu.make_async_remote_copy(
                s.mid,
                s.far.at[self.d],
                s.sems.at[2],
                s.sems.at[3],
                device_id=(lax.rem(self.d + step + 1, self.d_size), self.r),
                device_id_type=MESH,
            ).start()

        loop(self.d_size - 1, send)
        s.far[self.d] = s.mid[...]

    def sum_finish(self, name):
        s = self.sums[name]
        if s.direct:
            many = s.near.at[0 : self.total - 1]
            pltpu.make_async_copy(many, many, s.sems.at[1]).wait()
            return jnp.sum(s.near[...], axis=0)
        many = s.far.at[0 : self.d_size - 1]
        pltpu.make_async_copy(many, many, s.sems.at[3]).wait()
        return jnp.sum(s.far[...], axis=0)

    def sums_sent(self):
        for s in self.sums:
            if s.direct:
                many = s.near.at[0 : self.total - 1]
                pltpu.make_async_copy(many, many, s.sems.at[0]).wait()
            else:
                several = s.near.at[0 : self.r_size - 1]
                pltpu.make_async_copy(several, several, s.sems.at[0]).wait()
                many = s.far.at[0 : self.d_size - 1]
                pltpu.make_async_copy(many, many, s.sems.at[2]).wait()


    def norm_ready(self, norm, totals, count):
        coef = self.coef[norm]
        mean = totals[0:1] / count
        scale = lax.rsqrt(totals[1:2] / count - mean * mean + EPS)
        factor = scale * self.gain[norm][...]
        coef[0:1, :] = factor
        coef[1:2, :] = self.bias[norm][...] - mean * factor
        coef[2:3, :] = mean
        coef[3:4, :] = scale

    def norm_back_ready(self, norm, first, second, count):
        coef = self.coef[norm]
        factor, mean, scale = coef[0:1, :], coef[2:3, :], coef[3:4, :]
        second = second * scale
        self.grad_gain[norm][...] = second
        self.grad_bias[norm][...] = first
        slant = factor * scale * (second / count)
        coef[4:5, :] = slant
        coef[5:6, :] = factor * (first / count) - mean * slant

    def act(self, norm, value, lanes=slice(None)):
        coef = self.coef[norm]
        return value * coef[0:1, lanes] + coef[1:2, lanes]

    def off_mean(self, norm, value, lanes=slice(None)):
        return value - self.coef[norm][2:3, lanes]

    def back(self, norm, slope, value, mask, lanes=slice(None)):
        coef = self.coef[norm]
        grad = slope * coef[0:1, lanes] - value * coef[4:5, lanes] - coef[5:6, lanes]
        return (grad * mask).astype(BF16)


    def to_strip(self, step, src, dst, slot):
        return pltpu.make_async_remote_copy(
            src,
            dst,
            self.halo_send.at[slot],
            self.halo_recv.at[slot],
            device_id=(self.d, self.r + step),
            device_id_type=MESH,
        )

    def has_strip(self, step):
        return self.r > 0 if step < 0 else self.r < self.r_size - 1

    def edge_send(self, step, value, stage, target, slot):
        count = value.shape[0]
        base = value[0, 0:1].astype(BF16)
        stage[0:count] = (value - base.astype(F32)).astype(BF16)
        stage[count] = jnp.broadcast_to(base.astype(F32), value.shape[1:]).astype(BF16)

        @pl.when(self.has_strip(step))
        def _():
            self.to_strip(step, stage, target, slot).start()

    def edge_sent(self, step, stage, target, slot):
        @pl.when(self.has_strip(step))
        def _():
            self.to_strip(step, stage, target, slot).wait_send()

    def edge_read(self, step, stage, target, slot):
        self.to_strip(-step, stage, target, slot).wait_recv()
        count = target.shape[0] - 1
        return target[0:count].astype(F32) + target[count].astype(F32)[None]


    def place(self, name, shard):
        order = GRADS[name][5]
        if isinstance(shard, int):
            return sum(((shard >> b) & 1) << (BITS - 1 - k) for k, b in enumerate(order))
        where = 0
        for k, b in enumerate(order):
            where = where + bit_of(shard, b) * (1 << (BITS - 1 - k))
        return where

    def halving(self, name, stage):
        order = GRADS[name][5]
        start = 0
        for k in range(stage):
            start = start + bit_of(self.shard, order[k]) * (1 << (BITS - 1 - k))
        half = 1 << (BITS - 1 - stage)
        mine = bit_of(self.shard, order[stage])
        offset = SHARDS - 2 * half
        bit = order[stage] + self.low
        if bit < self.r_bits:
            partner = (self.d, self.r + (1 - 2 * mine) * (1 << bit))
        else:
            partner = (self.d + (1 - 2 * mine) * (1 << (bit - self.r_bits)), self.r)
        return start + mine * half, start + (1 - mine) * half, half, offset, partner

    def grad_copy(self, name, stage):
        array, rows, part, lane, lanes, _ = GRADS[name]
        _, away, half, offset, partner = self.halving(name, stage)
        index = name * BITS + stage
        away = pl.ds(pl.multiple_of((part * SHARDS + away) * rows, 16), half * rows)
        return pltpu.make_async_remote_copy(
            self.grads[array].at[away, lane : lane + lanes],
            self.recv[name].at[pl.ds(offset * rows, half * rows)],
            self.grad_send.at[index],
            self.grad_recv.at[index],
            device_id=partner,
            device_id_type=MESH,
        )

    def grad_start(self, name):
        self.grad_copy(name, 0).start()

    def grad_steps(self, stage, *names):
        for name in names:
            self.grad_step(name, stage)

    def grad_step(self, name, stage):
        array, rows, part, lane, lanes, _ = GRADS[name]
        keep, _, half, offset, _ = self.halving(name, stage)
        keep = part * SHARDS + keep
        self.grad_copy(name, stage).wait_recv()
        own, came = self.grads[array], self.recv[name]
        across = slice(lane, lane + lanes)
        if stage < BITS - 1:
            height = 16
            while height * lanes < 32768 and (half * rows) % (2 * height) == 0:
                height *= 2

            def add(step):
                here = pl.ds(pl.multiple_of(keep * rows + step * height, 16), height)
                there = pl.ds(pl.multiple_of(offset * rows + step * height, 16), height)
                total = own[here, across].astype(F32) + came[there, :].astype(F32)
                own[here, across] = total.astype(BF16)

            loop(half * rows // height, add)
            self.grad_copy(name, stage + 1).start()
            return
        here = pl.ds(pl.multiple_of(keep * rows, 16), rows)
        there = pl.ds(offset * rows, rows)
        out = self.grad_out[array]
        total = own[here, across].astype(F32) + came[there, :].astype(F32)
        if array == SPATIAL_ONE:
            for tap in range(9):
                out[tap, :, 0:128] = total[tap * 16 : tap * 16 + 8]
                out[tap, :, 128:256] = total[tap * 16 + 8 : tap * 16 + 16]
        elif array == EXPAND_ONE:
            out[:, 0:512] = total[0:8]
            out[:, 512:1024] = total[8:16]
        else:
            out[part * rows : part * rows + rows, across] = total

    def grads_sent(self):
        for name in range(len(GRADS)):
            for stage in range(BITS):
                self.grad_copy(name, stage).wait_send()

    def grad_store(self, name, block, value, lanes=slice(None), row=0):
        array, rows, part, _, _, _ = GRADS[name]
        per = 16 if array == SPATIAL_TWO else rows
        count = 256 // per
        base = (part * SHARDS + self.place(name, block * count)) * rows + row
        for s in range(count):
            where = pl.multiple_of(base + self.place(name, s) * rows, 16)
            self.grads[array][pl.ds(where, per), lanes] = value[s * per : (s + 1) * per].astype(BF16)


    def run(self):
        self.greet()
        pairs = dict(
            xa=(self.xa_in, self.xa),
            xb=(self.xb_in, self.xb),
            w1=(self.w1_in, self.w1),
            ca=(self.ca_in, self.ca),
            cb=(self.cb_in, self.cb),
            w2=(self.w2_in, self.w2),
            w3=(self.w3_in, self.w3),
            w4=(self.w4_in, self.w4),
            ws=(self.ws_in, self.ws),
            w5=(self.w5_in, self.w5),
            w6=(self.w6_in, self.w6),
        )
        loads = SimpleNamespace()
        for i, name in enumerate(pairs):
            copy = pltpu.make_async_copy(*pairs[name], self.load_sem.at[i])
            copy.start()
            setattr(loads, name, copy)

        x, z1, z2, z3, z4, z5 = self.x, self.z1, self.z2, self.z3, self.z4, self.z5
        h1, h2, feed, h4, h5 = self.h1, self.h2, self.feed, self.h4, self.h5
        big, mask = self.big, self.mask
        rows, cols, views, _ = x.shape
        half = cols // 2
        natural = [2 * (k % half) + k // half for k in range(cols)]
        zeros = functools.partial(jnp.zeros, dtype=BF16)

        live_a = self.live[0, self.d]
        live_b = self.live[1, self.d]
        all_a = self.live[0, 0]
        all_b = self.live[1, 0]
        for i in range(1, self.d_size):
            all_a = all_a + self.live[0, i]
            all_b = all_b + self.live[1, i]
        line = jnp.zeros((1, 128), jnp.int32)
        line_a = (line + all_a).astype(F32)
        line_b = (line + all_b).astype(F32)
        full_one = HA * WA * line_a + HB * WB * line_b
        half_one = ((HA + 1) // 2) * ((WA + 1) // 2) * line_a + ((HB + 1) // 2) * (
            (WB + 1) // 2
        ) * line_b
        self.full_count[...] = full_one
        self.half_count[...] = half_one

        def full(lanes):
            return wide(self.full_count[...], lanes)

        def part(lanes):
            return wide(self.half_count[...], lanes)

        def mask_of(row):
            place = lax.broadcasted_iota(jnp.int32, (cols, views, 128), 0)
            column = jnp.where(place < half, 2 * place, 2 * (place - half) + 1)
            view = lax.broadcasted_iota(jnp.int32, (cols, views, 128), 1)
            where = self.r * rows + row
            tall_a = jnp.where(where < HA, live_a, 0)
            tall_b = jnp.where(where < HB, live_b, 0)
            in_a = (view < self.live_a) & (view < tall_a)
            in_b = (view >= self.live_a) & (view - self.live_a < tall_b) & (column < WB)
            return jnp.where(in_a | in_b, 1.0, 0.0).astype(F32)

        def make_mask(row):
            mask[row] = mask_of(row)

        loop(rows, make_mask)
        side, side_2 = self.side, self.side_2
        above_a, below_a, above_2, below_2 = (
            self.edge_a.at[0],
            self.edge_a.at[1],
            self.edge_2.at[0],
            self.edge_2.at[1],
        )

        for ref in (h1, self.dz2):
            lanes = ref.shape[-1]
            ref[0] = zeros((cols + 2, views, lanes))
            ref[rows + 1] = zeros((cols + 2, views, lanes))
            for row in range(1, rows + 1):
                ref[row, 0] = zeros((views, lanes))
                ref[row, cols + 1] = zeros((views, lanes))
        h4[0] = zeros(h4.shape[1:])
        for row in range(1, rows + 1):
            h4[row, half] = zeros((views, h4.shape[-1]))
        self.dz5[rows // 2] = zeros(self.dz5.shape[1:])
        for row in range(rows // 2):
            self.dz5[row, half] = zeros((views, self.dz5.shape[-1]))

        def row_mask(row, lanes):
            return wide(flat(mask[row]), lanes)

        none = jnp.zeros((1, 256), F32)

        loads.xa.wait()
        loads.xb.wait()

        def gather_row(row):
            for k in range(cols):
                c = natural[k]
                near = self.xa[row, c].astype(F32)
                if c < self.xb.shape[1]:
                    rest = self.xb[row, c].astype(F32)
                else:
                    rest = jnp.zeros((self.live_b, near.shape[-1]), F32)
                value = jnp.concatenate([near, rest], axis=0)
                x[row, k] = (value * wide(mask[row, k], value.shape[-1])).astype(BF16)

        loop(rows, gather_row)
        loads.w1.wait()

        def reduce_row(row, carry):
            total, square = carry
            value = mm(flat(x[row]), self.w1[...])
            z1[row] = value.reshape(cols, views, -1)
            return (total + col_sum(value), square + col_sum(value * value))

        sums = loop(rows, reduce_row, (none, none))
        self.greeted()
        self.sum_start(AT_ONE, sums)
        self.sum_turn(AT_ONE)
        self.edge_send(-1, z1[0], side.at[0], below_a, 0)
        self.edge_send(1, z1[rows - 1], side.at[1], above_a, 1)
        loads.ca.wait()
        loads.cb.wait()
        for o in range(rows // 2):
            for p in range(half):
                for h in range(2):
                    lanes = slice(h * LEAF, h * LEAF + LEAF)
                    near = self.ca[o, p, :, lanes].astype(F32)
                    if p < self.cb.shape[1]:
                        rest = self.cb[o, p, :, lanes].astype(F32)
                    else:
                        rest = jnp.zeros((self.live_b, LEAF), F32)
                    self.cot[h, o * half + p] = jnp.concatenate([near, rest], axis=0).astype(BF16)
        self.norm_ready(NARROW, self.sum_finish(AT_ONE), full(256))

        def hidden_of(value, live):
            value = self.act(NARROW, value)
            return (value * sigmoid(value) * live).astype(BF16).reshape(cols, views, -1)

        def hidden_one(row):
            value = hidden_of(flat(z1[row]), row_mask(row, 256))
            for k in range(cols):
                h1[row + 1, natural[k] + 1] = value[k]

        loop(rows, hidden_one)

        def hidden_edge(step, source, slot, row):
            @pl.when(self.has_strip(step))
            def _():
                given = flat(self.edge_read(step, side.at[0], source, slot))
                value = hidden_of(given, wide(flat(mask_of(row)), 256))
                for k in range(cols):
                    h1[row + 1, natural[k] + 1] = value[k]

        loads.w2.wait()

        def conv_row(row, carry):
            total, square = carry
            value = 0.0
            for i in range(3):
                for j in range(3):
                    tap = (i * 3 + j) * 256
                    value = value + mm(flat(h1[row + i, j : j + cols]), self.w2[tap : tap + 256, :])
            value = value.reshape(cols, views, -1)
            ordered = jnp.concatenate([value[c] for c in natural], axis=0)
            z2[row] = ordered.reshape(cols, views, -1)
            kept = ordered * row_mask(row, 256)
            return (total + col_sum(kept), square + col_sum(kept * ordered))

        sums = loop(rows - 2, lambda i, carry: conv_row(i + 1, carry), (none, none))

        hidden_edge(-1, above_a, 1, -1)
        hidden_edge(1, below_a, 0, rows)
        sums = conv_row(rows - 1, conv_row(0, sums))
        self.sum_start(AT_TWO, sums)
        self.sum_turn(AT_TWO)
        self.edge_sent(-1, side.at[0], below_a, 0)
        self.edge_sent(1, side.at[1], above_a, 1)
        self.edge_send(-1, z2[0], side.at[0], below_2, 2)
        self.edge_send(1, z2[rows - 1], side.at[1], above_2, 3)
        loads.w3.wait()
        self.norm_ready(SPATIAL, self.sum_finish(AT_TWO), full(256))

        def hidden_two(row):
            value = self.act(SPATIAL, flat(z2[row]))
            value = (value * sigmoid(value) * row_mask(row, 256)).astype(BF16)
            h2[row] = value.reshape(cols, views, -1)

        loop(rows, hidden_two)

        def expand_row(row, carry):
            given = flat(h2[row])
            done = []
            for n in range(2):
                lanes = slice(n * 512, n * 512 + 512)
                value = mm(given, self.w3[:, lanes])
                z3[row, :, :, lanes] = value.reshape(cols, views, -1)
                done.append((carry[n][0] + col_sum(value), carry[n][1] + col_sum(value * value)))
            return tuple(done)

        nothing = jnp.zeros((1, 512), F32)
        sums = loop(rows, expand_row, ((nothing, nothing), (nothing, nothing)))
        sums = [jnp.concatenate([sums[0][i], sums[1][i]], axis=1) for i in range(2)]
        self.sum_start(AT_THREE, sums)
        self.sum_turn(AT_THREE)
        loads.w4.wait()
        loads.ws.wait()
        self.norm_ready(WIDENED, self.sum_finish(AT_THREE), full(1024))

        def feed_step(step):
            row, pair = step // half, lax.rem(step, half)
            here = pl.ds(pair * 2, 2)
            value = self.act(WIDENED, flat(z3[row, here])) + flat(x[row, here]).astype(F32)
            value = value * sigmoid(value) * wide(flat(mask[row, here]), 1024)
            feed[row, here] = value.astype(BF16).reshape(2, views, -1)

        loop(rows * half, feed_step)

        def squeeze_row(row, carry):
            total, square = carry
            value = mm(flat(feed[row]), self.w4[...])
            z4[row] = value.reshape(cols, views, -1)
            return (total + col_sum(value), square + col_sum(value * value))

        sums = loop(rows, squeeze_row, (nothing, nothing))
        self.sum_start(AT_FOUR, sums)
        self.sum_turn(AT_FOUR)
        self.edge_send(1, z4[rows - 1], side_2, self.edge_4, 4)

        def even(ref):
            return jnp.concatenate([flat(ref[2 * o, 0:half]) for o in range(rows // 2)], axis=0)

        for h in range(2):
            sums = []
            for n in range(2):
                lanes = slice(h * LEAF + n * 512, h * LEAF + n * 512 + 512)
                value = mm(even(feed), self.ws[:, lanes])
                big[2 + h, :, :, n * 512 : n * 512 + 512] = value.reshape(cols, views, -1)
                sums.append((col_sum(value), col_sum(value * value)))
            for i in range(2):
                self.short_sum[i : i + 1, h * LEAF : h * LEAF + LEAF] = jnp.concatenate(
                    [sums[0][i], sums[1][i]], axis=1
                )
        self.sum_start(AT_SHORT, [self.short_sum[0:1, :], self.short_sum[1:2, :]])
        self.norm_ready(SQUEEZE, self.sum_finish(AT_FOUR), full(512))

        def hidden_four(row):
            for p in range(2):
                value = self.act(SQUEEZE, flat(z4[row, p * half : p * half + half]))
                value = value * sigmoid(value) * wide(flat(mask[row, p * half : p * half + half]), 512)
                start = p * (half + 1)
                h4[row + 1, start : start + half] = value.astype(BF16).reshape(half, views, -1)

        loop(rows, hidden_four)
        loads.w5.wait()
        starts = (half, 0, half + 1)

        def taken(i, j):
            return jnp.concatenate(
                [flat(h4[2 * o + i, starts[j] : starts[j] + half]) for o in range(rows // 2)], axis=0
            )

        value = 0.0
        for i in (1, 2, 0):
            if i == 0:

                @pl.when(self.has_strip(-1))
                def _():
                    given = self.edge_read(-1, side_2, self.edge_4, 4)
                    live = mask_of(-1)
                    for p in range(2):
                        here = slice(p * half, p * half + half)
                        point = self.act(SQUEEZE, flat(given[here]))
                        point = point * sigmoid(point) * wide(flat(live[here]), 512)
                        start = p * (half + 1)
                        h4[0, start : start + half] = point.astype(BF16).reshape(half, views, -1)

            for j in range(3):
                tap = (i * 3 + j) * 512
                value = value + mm(taken(i, j), self.w5[tap : tap + 512, :])
        z5[...] = value
        half_mask = jnp.concatenate(
            [flat(mask[2 * o, 0:half]) for o in range(rows // 2)], axis=0
        )
        self.half_mask[...] = half_mask
        kept = value * wide(half_mask, 512)
        self.sum_start(AT_FIVE, (col_sum(kept), col_sum(kept * value)))
        self.sum_turn(AT_FIVE)
        self.sum_turn(AT_SHORT)
        self.edge_sent(1, side_2, self.edge_4, 4)
        row_5 = half * views
        self.edge_send(
            -1,
            z5[0:row_5, :].reshape(half, views, -1),
            side_2.at[0 : half + 1],
            self.edge_5,
            5,
        )
        loads.w6.wait()
        self.norm_ready(STRIDED, self.sum_finish(AT_FIVE), part(512))
        value = self.act(STRIDED, z5[...])
        h5[...] = (value * sigmoid(value) * wide(self.half_mask[...], 512)).astype(BF16)

        for h in range(2):
            sums = []
            for n in range(2):
                lanes = slice(h * LEAF + n * 512, h * LEAF + n * 512 + 512)
                value = mm(h5[...], self.w6[:, lanes])
                big[h, :, :, n * 512 : n * 512 + 512] = value.reshape(cols, views, -1)
                sums.append((col_sum(value), col_sum(value * value)))
            for i in range(2):
                self.main_sum[i : i + 1, h * LEAF : h * LEAF + LEAF] = jnp.concatenate(
                    [sums[0][i], sums[1][i]], axis=1
                )
        self.sum_start(AT_SIX, [self.main_sum[0:1, :], self.main_sum[1:2, :]])
        self.norm_ready(SHORTCUT, self.sum_finish(AT_SHORT), part(2048))
        self.sum_turn(AT_SIX)
        self.norm_ready(OUTPUT, self.sum_finish(AT_SIX), part(2048))

        dh4, cot = self.dh4, self.cot
        zero = jnp.zeros((1, LEAF), F32)
        for h in range(2):
            lanes = slice(h * LEAF, h * LEAF + LEAF)

            def out_step(pair, carry):
                here = pl.ds(pair * 2, 2)
                main, side = flat(big[h, here]), flat(big[2 + h, here])
                value = self.act(OUTPUT, main, lanes) + self.act(SHORTCUT, side, lanes)
                there = wide(self.half_mask[pl.ds(pl.multiple_of(pair * 2 * views, 8), 2 * views), :], LEAF)
                sigma = sigmoid(value)
                given = flat(cot[h, here]).astype(F32)
                slope = given * there * (sigma * (1.0 + value * (1.0 - sigma)))
                cot[h, here] = (value * sigma * there).astype(BF16).reshape(2, views, -1)
                for n in range(2):
                    dh4[2 * h + n, here] = slope[:, n * 512 : n * 512 + 512].reshape(2, views, -1)
                return (
                    carry[0] + col_sum(slope),
                    carry[1] + col_sum(slope * self.off_mean(OUTPUT, main, lanes)),
                    carry[2] + col_sum(slope * self.off_mean(SHORTCUT, side, lanes)),
                )

            sums = loop(half, out_step, (zero, zero, zero))
            for i in range(3):
                start = i * 2 * LEAF + h * LEAF
                self.top_sum[:, start : start + LEAF] = sums[i]
        self.sum_start(AT_SEVEN, [self.top_sum[...]])
        for o in range(rows // 2):
            for p in range(half):
                for h in range(2):
                    lanes = slice(h * LEAF, h * LEAF + LEAF)
                    done = cot[h, o * half + p].astype(F32)
                    self.ca[o, p, :, lanes] = done[0 : self.live_a].astype(BF16)
                    if p < self.cb.shape[1]:
                        self.cb[o, p, :, lanes] = done[self.live_a :].astype(BF16)
        stores = [
            pltpu.make_async_copy(self.ca, self.out_a_to, self.store_sem.at[0]),
            pltpu.make_async_copy(self.cb, self.out_b_to, self.store_sem.at[1]),
        ]
        for copy in stores:
            copy.start()
        self.sum_turn(AT_SEVEN)
        totals = self.sum_finish(AT_SEVEN)
        totals = [totals[:, i * 2 * LEAF : (i + 1) * 2 * LEAF] for i in range(3)]
        self.norm_back_ready(OUTPUT, totals[0], totals[1], part(2048))
        self.norm_back_ready(SHORTCUT, totals[0], totals[2], part(2048))

        dz6, dzs = self.dz6, self.dzs
        for h in range(2):
            lanes = slice(h * LEAF, h * LEAF + LEAF)

            def top_step(pair):
                here = pl.ds(pair * 2, 2)
                there = pl.ds(pl.multiple_of(pair * 2 * views, 16), 2 * views)
                live = wide(self.half_mask[there, :], LEAF)
                slope = jnp.concatenate([flat(dh4[2 * h + n, here]) for n in range(2)], axis=1)
                dz6[there, lanes] = self.back(OUTPUT, slope, flat(big[h, here]), live, lanes)
                dzs[there, lanes] = self.back(SHORTCUT, slope, flat(big[2 + h, here]), live, lanes)

            loop(half, top_step)

        value = mm_nt(dz6[...], self.w6[...]) * slope_of(self.act(STRIDED, z5[...]))
        self.slope5[...] = value
        self.sum_start(AT_EIGHT, (col_sum(value), col_sum(value * self.off_mean(STRIDED, z5[...]))))

        self.edge_sent(-1, side_2.at[0 : half + 1], self.edge_5, 5)
        edge_s = self.edge_4.at[0 : half + 1]
        self.edge_send(
            -1,
            self.slope5[0:row_5, :].reshape(half, views, -1),
            side_2.at[0 : half + 1],
            edge_s,
            6,
        )

        for name in EXPAND_TWO_PARTS:
            first_lane = GRADS[name][3]

            def grad_expand_two(step):
                m, n = step // 2, lax.rem(step, 2)
                left = h5[:, pl.ds(pl.multiple_of(m * 256, 256), 256)]
                lanes = pl.ds(pl.multiple_of(first_lane + n * 512, 512), 512)
                self.grad_store(name, m, mm_tn(left, dz6[:, lanes]), lanes)

            loop(4, grad_expand_two)
            self.grad_start(name)

        def clear(row):
            big[row] = jnp.zeros(big.shape[1:], F32)

        loop(rows, clear)

        def shortcut_back(n):
            lanes = pl.ds(pl.multiple_of(n * 256, 256), 256)
            value = mm_nt(dzs[...], self.ws[lanes, :]).reshape(rows // 2, half, views, -1)
            for o in range(rows // 2):
                big[2 * o, 0:half, :, lanes] = value[o]

        loop(4, shortcut_back)

        def grad_shortcut_two(m):
            here = pl.ds(pl.multiple_of(m * 256, 256), 256)
            left = jnp.concatenate(
                [flat(feed[2 * o, 0:half, :, here]) for o in range(rows // 2)], axis=0
            )
            for name in SHORTCUT_TWO_PARTS:
                lanes = slice(GRADS[name][3], GRADS[name][3] + GRADS[name][4])
                self.grad_store(name, m, mm_tn(left, dzs[:, lanes]), lanes)

        loop(4, grad_shortcut_two)
        for name in SHORTCUT_TWO_PARTS:
            self.grad_start(name)
        self.grad_steps(0, *EXPAND_TWO_PARTS)
        self.sum_turn(AT_EIGHT)
        totals = self.sum_finish(AT_EIGHT)
        self.norm_back_ready(STRIDED, totals[0:1], totals[1:2], part(512))
        dz5 = self.dz5
        value = self.back(STRIDED, self.slope5[...], z5[...], wide(self.half_mask[...], 512))
        for o in range(rows // 2):
            dz5[o, 0:half] = value[o * half * views : (o + 1) * half * views].reshape(half, views, -1)
        for i in (1, 2, 0):
            if i == 0:

                @pl.when(self.has_strip(1))
                def _():
                    given = self.edge_read(1, side_2.at[0 : half + 1], edge_s, 6)
                    point = self.edge_read(1, side_2.at[0 : half + 1], self.edge_5, 5)
                    live = wide(flat(mask_of(rows)[0:half]), 512)
                    point = self.back(STRIDED, flat(given), flat(point), live)
                    dz5[rows // 2, 0:half] = point.reshape(half, views, -1)

            lead = 1 if i == 0 else 0
            for j in (1, 2, 0):
                tap = (i * 3 + j) * 512
                start = 1 if j == 0 else 0
                given = jnp.concatenate(
                    [flat(dz5[o + lead, start : start + half]) for o in range(rows // 2)], axis=0
                )
                value = mm_nt(given, self.w5[tap : tap + 512, :]).reshape(rows // 2, half, views, -1)
                spot = slice(0, half) if j == 1 else slice(half, 2 * half)
                for o in range(rows // 2):
                    target = 2 * o if i == 1 else 2 * o + 1
                    if j == 0 or i == 0:
                        dh4[target, spot] = dh4[target, spot] + value[o]
                    else:
                        dh4[target, spot] = value[o]

        def slope_four(step, carry):
            row, p = step // 2, lax.rem(step, 2)
            here = pl.ds(p * half, half)
            before = flat(z4[row, here])
            value = flat(dh4[row, here]) * slope_of(self.act(SQUEEZE, before))
            dh4[row, here] = value.reshape(half, views, -1)
            return (
                carry[0] + col_sum(value),
                carry[1] + col_sum(value * self.off_mean(SQUEEZE, before)),
            )

        sums = loop(rows * 2, slope_four, (nothing, nothing))
        self.sum_start(AT_NINE, sums)
        self.sum_turn(AT_NINE)
        self.grad_steps(0, *SHORTCUT_TWO_PARTS)
        self.grad_steps(1, *EXPAND_TWO_PARTS)

        for i, name in enumerate(SPATIAL_TWO_PARTS):

            def grad_spatial_two(step):
                j, m = step // 2, lax.rem(step, 2)
                here = pl.ds(pl.multiple_of(m * 256, 256), 256)
                start = half * ((1 - j) * (2 - j) // 2) + (half + 1) * (j * (j + 1) // 2 - j)
                left = jnp.concatenate(
                    [flat(h4[2 * o + i, pl.ds(start, half), :, here]) for o in range(rows // 2)], axis=0
                )
                right = jnp.concatenate([flat(dz5[o, 0:half]) for o in range(rows // 2)], axis=0)
                self.grad_store(name, m, mm_tn(left, right), row=j * 16)

            loop(6, grad_spatial_two)
            self.grad_start(name)
        totals = self.sum_finish(AT_NINE)
        self.norm_back_ready(SQUEEZE, totals[0:1], totals[1:2], full(512))
        dz4 = self.dz4

        def back_four(step):
            row, p = step // 2, lax.rem(step, 2)
            here = pl.ds(p * half, half)
            value = self.back(
                SQUEEZE, flat(dh4[row, here]), flat(z4[row, here]), wide(flat(mask[row, here]), 512)
            )
            dz4[row, here] = value.reshape(half, views, -1)

        loop(rows * 2, back_four)

        def slope_three(row, carry):
            done = []
            for n in range(2):
                lanes = slice(n * 512, n * 512 + 512)
                before = flat(z3[row, :, :, lanes])
                grad = mm_nt(flat(dz4[row]), self.w4[lanes, :]) + flat(big[row, :, :, lanes])
                point = self.act(WIDENED, before, lanes) + flat(x[row, :, :, lanes]).astype(F32)
                value = grad * slope_of(point)
                big[row, :, :, lanes] = value.reshape(cols, views, -1)
                done.append(
                    (
                        carry[n][0] + col_sum(value),
                        carry[n][1] + col_sum(value * self.off_mean(WIDENED, before, lanes)),
                    )
                )
            return tuple(done)

        sums = loop(rows, slope_three, ((nothing, nothing), (nothing, nothing)))
        sums = [jnp.concatenate([sums[0][i], sums[1][i]], axis=1) for i in range(2)]
        self.sum_start(AT_TEN, sums)

        def grad_reduce_two(m):
            here = pl.ds(pl.multiple_of(m * 256, 256), 256)
            left = feed[:, :, :, here].reshape(-1, 256)
            self.grad_store(G_REDUCE_TWO, m, mm_tn(left, dz4[...].reshape(-1, 512)))

        loop(4, grad_reduce_two)
        self.grad_start(G_REDUCE_TWO)
        self.sum_turn(AT_TEN)
        self.grad_steps(0, *SPATIAL_TWO_PARTS)
        self.grad_steps(2, *EXPAND_TWO_PARTS)
        totals = self.sum_finish(AT_TEN)
        self.norm_back_ready(WIDENED, totals[0:1], totals[1:2], full(1024))
        dz3 = feed

        def back_three(step):
            row, pair = step // half, lax.rem(step, half)
            here = pl.ds(pair * 2, 2)
            live = wide(flat(mask[row, here]), 1024)
            value = self.back(WIDENED, flat(big[row, here]), flat(z3[row, here]), live)
            dz3[row, here] = value.reshape(2, views, -1)

        loop(rows * half, back_three)


        def slope_spatial(row, carry):
            before = flat(z2[row])
            value = mm_nt(flat(dz3[row]), self.w3[...]) * slope_of(self.act(SPATIAL, before))
            dh4[row, :, :, 0:256] = value.reshape(cols, views, -1)
            return (
                carry[0] + col_sum(value),
                carry[1] + col_sum(value * self.off_mean(SPATIAL, before)),
            )

        sums = loop(rows, slope_spatial, (none, none))
        self.sum_start(AT_ELEVEN, sums)
        self.sum_turn(AT_ELEVEN)
        self.edge_sent(-1, side.at[0], below_2, 2)
        self.edge_sent(1, side.at[1], above_2, 3)
        self.edge_send(-1, dh4[0, :, :, 0:256], side.at[0], below_a, 7)
        self.edge_send(1, dh4[rows - 1, :, :, 0:256], side.at[1], above_a, 8)
        self.grad_step(G_REDUCE_TWO, 0)
        self.grad_steps(1, *SHORTCUT_TWO_PARTS)
        self.grad_steps(3, *EXPAND_TWO_PARTS)

        left = h2[...].reshape(-1, 256)
        g_low = mm_tn(left, dz3[:, :, :, 0:512].reshape(-1, 512))
        g_high = mm_tn(left, dz3[:, :, :, 512:1024].reshape(-1, 512))
        for s in range(SHARDS):
            at = self.place(G_EXPAND_ONE, s) * 16
            piece = jnp.concatenate([g_low[s * 8 : s * 8 + 8], g_high[s * 8 : s * 8 + 8]], axis=0)
            self.grads[EXPAND_ONE][at : at + 16, :] = piece.astype(BF16)
        self.grad_start(G_EXPAND_ONE)
        totals = self.sum_finish(AT_ELEVEN)
        self.norm_back_ready(SPATIAL, totals[0:1], totals[1:2], full(256))
        dz2 = self.dz2

        def back_two(row):
            value = self.back(SPATIAL, flat(dh4[row, :, :, 0:256]), flat(z2[row]), row_mask(row, 256))
            value = value.reshape(cols, views, -1)
            for k in range(cols):
                dz2[row + 1, natural[k] + 1] = value[k]

        loop(rows, back_two)
        for i in range(3):
            for j in range(3):
                left = h1[i : i + rows, j : j + cols].reshape(-1, 256)
                value = mm_tn(left, dz2[1 : rows + 1, 1 : cols + 1].reshape(-1, 256))
                for s in range(SHARDS):
                    at = self.place(G_SPATIAL_ONE, s) * 144 + (i * 3 + j) * 16
                    piece = value[s * 8 : s * 8 + 8]
                    piece = jnp.concatenate([piece[:, 0:128], piece[:, 128:256]], axis=0)
                    self.grads[SPATIAL_ONE][at : at + 16, :] = piece.astype(BF16)
        self.grad_start(G_SPATIAL_ONE)

        def edge_two(step, slope_from, slope_slot, value_from, value_slot, row):
            @pl.when(self.has_strip(step))
            def _():
                given = flat(self.edge_read(step, side.at[0], slope_from, slope_slot))
                point = flat(self.edge_read(step, side.at[0], value_from, value_slot))
                value = self.back(SPATIAL, given, point, wide(flat(mask_of(row)), 256))
                value = value.reshape(cols, views, -1)
                for k in range(cols):
                    dz2[row + 1, natural[k] + 1] = value[k]

        edge_two(-1, above_a, 8, above_2, 3, -1)
        edge_two(1, below_a, 7, below_2, 2, rows)

        def slope_narrow(row, carry):
            value = 0.0
            for i in range(3):
                for j in range(3):
                    tap = (i * 3 + j) * 256
                    given = flat(dz2[row + 2 - i, 2 - j : 2 - j + cols])
                    value = value + mm_nt(given, self.w2[tap : tap + 256, :])
            value = value.reshape(cols, views, -1)
            value = jnp.concatenate([value[c] for c in natural], axis=0)
            before = flat(z1[row])
            value = value * row_mask(row, 256) * slope_of(self.act(NARROW, before))
            dh4[row, :, :, 0:256] = value.reshape(cols, views, -1)
            return (
                carry[0] + col_sum(value),
                carry[1] + col_sum(value * self.off_mean(NARROW, before)),
            )

        sums = loop(rows, slope_narrow, (none, none))
        self.sum_start(AT_TWELVE, sums)
        self.sum_turn(AT_TWELVE)
        self.grad_step(G_SPATIAL_ONE, 0)
        self.grad_steps(1, *SPATIAL_TWO_PARTS)
        self.grad_steps(2, *SHORTCUT_TWO_PARTS)
        self.grad_step(G_EXPAND_ONE, 0)
        self.grad_step(G_REDUCE_TWO, 1)
        self.grad_steps(4, *EXPAND_TWO_PARTS)
        totals = self.sum_finish(AT_TWELVE)
        self.norm_back_ready(NARROW, totals[0:1], totals[1:2], full(256))
        dz1 = h2

        def back_one(row):
            value = self.back(NARROW, flat(dh4[row, :, :, 0:256]), flat(z1[row]), row_mask(row, 256))
            dz1[row] = value.reshape(cols, views, -1)

        loop(rows, back_one)

        def grad_reduce_one(m):
            here = pl.ds(pl.multiple_of(m * 256, 256), 256)
            left = x[:, :, :, here].reshape(-1, 256)
            self.grad_store(G_REDUCE_ONE, m, mm_tn(left, dz1[...].reshape(-1, 256)))

        loop(4, grad_reduce_one)
        self.grad_start(G_REDUCE_ONE)

        def input_row(row):
            for n in range(2):
                lanes = slice(n * 512, n * 512 + 512)
                value = mm_nt(flat(dz1[row]), self.w1[lanes, :]) + flat(big[row, :, :, lanes])
                value = value.reshape(cols, views, -1)
                for k in range(cols):
                    self.xa[row, natural[k], :, lanes] = value[k, 0 : self.live_a].astype(BF16)
                    if natural[k] < self.xb.shape[1]:
                        self.xb[row, natural[k], :, lanes] = value[k, self.live_a :].astype(BF16)

        loop(rows, input_row)
        for i, pair in enumerate(((self.xa, self.in_a_to), (self.xb, self.in_b_to))):
            copy = pltpu.make_async_copy(*pair, self.store_sem.at[2 + i])
            copy.start()
            stores.append(copy)
        self.grad_step(G_REDUCE_ONE, 0)
        self.grad_step(G_SPATIAL_ONE, 1)
        self.grad_step(G_EXPAND_ONE, 1)
        self.grad_step(G_REDUCE_TWO, 2)
        self.grad_steps(3, *SHORTCUT_TWO_PARTS)
        self.grad_steps(2, *SPATIAL_TWO_PARTS)
        self.grad_step(G_REDUCE_ONE, 1)
        self.grad_step(G_SPATIAL_ONE, 2)
        self.grad_step(G_EXPAND_ONE, 2)
        self.grad_step(G_REDUCE_TWO, 3)
        self.grad_steps(4, *SHORTCUT_TWO_PARTS)
        self.grad_steps(3, *SPATIAL_TWO_PARTS)
        self.grad_step(G_REDUCE_ONE, 2)
        self.grad_step(G_SPATIAL_ONE, 3)
        self.grad_step(G_EXPAND_ONE, 3)
        self.grad_step(G_REDUCE_TWO, 4)
        self.grad_steps(4, *SPATIAL_TWO_PARTS)
        self.grad_step(G_REDUCE_ONE, 3)
        self.grad_steps(4, G_SPATIAL_ONE, G_EXPAND_ONE)
        self.grad_step(G_REDUCE_ONE, 4)

        for copy in stores:
            copy.wait()
        self.sums_sent()
        self.grads_sent()

        self.edge_sent(-1, side_2.at[0 : half + 1], edge_s, 6)
        self.edge_sent(-1, side.at[0], below_a, 7)
        self.edge_sent(1, side.at[1], above_a, 8)


def settle(*refs):
    half = len(refs) // 2
    for i in range(half):
        refs[half + i][...] = refs[i][...]


def settled(values):
    inside = pl.BlockSpec(memory_space=pltpu.VMEM)
    return pl.pallas_call(
        settle,
        out_shape=[jax.ShapeDtypeStruct(v.shape, v.dtype) for v in values],
        in_specs=[inside] * len(values),
        out_specs=[inside] * len(values),
    )(*values)


def sum_of(pay, near, mid, far, sems):
    return SimpleNamespace(direct=far is None, pay=pay, near=near, mid=mid, far=far, sems=sems)


def both_blocks(given, live_views, weights, gains, biases):
    d_size, r_size = lax.axis_size("dp"), lax.axis_size("rows")
    total = d_size * r_size
    rows, cols, views_a, c_in = given[0].shape
    views_b = given[1].shape[2]
    views = views_a + views_b
    half = cols // 2
    c_mid, c_mid2, c_out = gains[0].shape[1], gains[3].shape[1], gains[5].shape[1]
    pixels = (rows // 2) * half * views
    vmem, dma = pltpu.VMEM, pltpu.SemaphoreType.DMA
    anywhere = pl.BlockSpec(memory_space=pl.ANY)
    inside = pl.BlockSpec(memory_space=pltpu.VMEM)

    def full(lanes, kind):
        return vmem((rows, cols, views, lanes), kind)

    def like(value):
        return vmem(value.shape, value.dtype)

    sums = []
    for count, lanes, straight in SUMS:
        direct = straight and total <= 32
        sums.append(
            dict(
                pay=vmem((count, lanes), F32),
                near=vmem((total if direct else r_size, count, lanes), F32),
                mid=None if direct else vmem((count, lanes), F32),
                far=None if direct else vmem((d_size, count, lanes), F32),
                sems=dma((4,)),
            )
        )
    w = weights
    scratch = dict(
        xa=like(given[0]),
        xb=like(given[1]),
        ca=like(given[2]),
        cb=like(given[3]),
        x=full(c_in, BF16),
        w1=like(w[0]),
        w2=like(w[1]),
        w3=like(w[2]),
        w4=like(w[3]),
        w5=like(w[4]),
        w6=like(w[5]),
        ws=like(w[6]),
        cot=vmem((2, cols, views, LEAF), BF16),
        mask=full(128, F32),
        half_mask=vmem((pixels, 128), F32),
        full_count=vmem((1, 128), F32),
        half_count=vmem((1, 128), F32),
        z1=full(c_mid, F32),
        z2=full(c_mid, F32),
        z3=full(c_in, F32),
        z4=full(c_mid2, F32),
        z5=vmem((pixels, c_mid2), F32),
        h1=vmem((rows + 2, cols + 2, views, c_mid), BF16),
        h2=full(c_mid, BF16),
        feed=full(c_in, BF16),
        h4=vmem((rows + 1, cols + 1, views, c_mid2), BF16),
        h5=vmem((pixels, c_mid2), BF16),
        big=full(c_in, F32),
        short_sum=vmem((2, c_out), F32),
        main_sum=vmem((2, c_out), F32),
        top_sum=vmem((1, 3 * c_out), F32),
        dz6=vmem((pixels, c_out), BF16),
        dzs=vmem((pixels, c_out), BF16),
        slope5=vmem((pixels, c_mid2), F32),
        dz5=vmem((rows // 2 + 1, half + 1, views, c_mid2), BF16),
        dh4=full(c_mid2, F32),
        dz4=full(c_mid2, BF16),
        dz2=vmem((rows + 2, cols + 2, views, c_mid), BF16),
        g2=vmem((SHARDS * 144, 128), BF16),
        g3=vmem((SHARDS * 16, 512), BF16),
        load_sem=dma((11,)),
        store_sem=dma((4,)),
        side=vmem((2, cols + 1, views, c_mid), BF16),
        edge_a=vmem((2, cols + 1, views, c_mid), BF16),
        edge_2=vmem((2, cols + 1, views, c_mid), BF16),
        side_2=vmem((cols + 1, views, c_mid2), BF16),
        edge_4=vmem((cols + 1, views, c_mid2), BF16),
        edge_5=vmem((half + 1, views, c_mid2), BF16),
        halo_send=dma((9,)),
        halo_recv=dma((9,)),
        grad_send=dma((len(GRADS) * BITS,)),
        grad_recv=dma((len(GRADS) * BITS,)),
        coef=[vmem((8, gain.shape[1]), F32) for gain in gains],
        recv=[vmem(((SHARDS - 1) * height, lanes), BF16) for _, height, _, _, lanes, _ in GRADS],
        sums=sums,
    )
    grad_shapes = ((32, 256), (9, 8, 256), (8, 1024), (32, 512), (144, 512), (16, 2048), (32, 2048))
    ins = dict(
        live=live_views,
        xa_in=given[0],
        xb_in=given[1],
        ca_in=given[2],
        cb_in=given[3],
        w1_in=w[0],
        w2_in=w[1],
        w3_in=w[2],
        w4_in=w[3],
        w5_in=w[4],
        w6_in=w[5],
        ws_in=w[6],
        gain=list(gains),
        bias=list(biases),
    )
    shape = jax.ShapeDtypeStruct
    outs = dict(
        out_a_to=shape(given[2].shape, BF16),
        out_b_to=shape(given[3].shape, BF16),
        in_a_to=shape(given[0].shape, BF16),
        in_b_to=shape(given[1].shape, BF16),
        grad_out=[shape(s, F32) for s in grad_shapes],
        grad_gain=[shape(g.shape, F32) for g in gains],
        grad_bias=[shape(g.shape, F32) for g in gains],
    )
    parts = []
    trees = []
    for group in (ins, outs, scratch):
        leaves, tree = jax.tree.flatten(group, is_leaf=lambda v: not isinstance(v, (dict, list, type(None))))
        parts.append(leaves)
        trees.append(tree)
    in_specs = dict(ins)
    for name in ins:
        in_specs[name] = [inside] * len(gains) if isinstance(ins[name], list) else anywhere
    in_specs.update(live=pl.BlockSpec(memory_space=pltpu.SMEM))
    out_specs = {
        name: [inside] * len(outs[name]) if isinstance(outs[name], list) else anywhere for name in outs
    }
    spec_leaves = [
        jax.tree.flatten(group, is_leaf=lambda v: isinstance(v, pl.BlockSpec))[0]
        for group in (in_specs, out_specs)
    ]

    def body(*refs):
        fields = {}
        start = 0
        for leaves, tree in zip(parts, trees):
            fields.update(jax.tree.unflatten(tree, refs[start : start + len(leaves)]))
            start += len(leaves)
        g = SimpleNamespace(**fields)
        fields.update(
            grads=[g.w2, g.g2, g.g3, g.w4, g.w5, g.w6, g.ws],
            sums=[sum_of(**s) for s in g.sums],
        )
        Kernel((d_size, r_size, views_a, views_b), fields).run()

    results = pl.pallas_call(
        body,
        out_shape=parts[1],
        in_specs=spec_leaves[0],
        out_specs=spec_leaves[1],
        scratch_shapes=parts[2],
        compiler_params=pltpu.CompilerParams(
            collective_id=0, has_side_effects=True, vmem_limit_bytes=64 * 2**20 - 65536 * 4
        ),
        cost_estimate=pl.CostEstimate(flops=16 * 10**9, bytes_accessed=30 * 10**6, transcendentals=4 * 10**6),
    )(*parts[0])
    done = SimpleNamespace(**jax.tree.unflatten(trees[1], results))
    plain = settled([done.out_a_to, done.in_a_to, *done.grad_out, *done.grad_gain, *done.grad_bias])
    return plain[0], done.out_b_to, plain[1], done.in_b_to, list(plain[2:9]), plain[9:]


def on_device(input_a, input_b, live_views, *rest):
    weights, params, cotangents = rest[:7], rest[7:21], rest[21:]
    gains = [value.reshape(1, -1) for value in params[0::2]]
    biases = [value.reshape(1, -1) for value in params[1::2]]
    reduce_one, spatial_one, expand_one, reduce_two, spatial_two, expand_two, shortcut_two = weights
    weights = (
        reduce_one,
        spatial_one.transpose(1, 2, 0, 3).reshape(-1, spatial_one.shape[-1]),
        expand_one,
        reduce_two,
        spatial_two.transpose(1, 2, 0, 3).reshape(-1, spatial_two.shape[-1]),
        expand_two,
        shortcut_two,
    )
    given = [value.transpose(0, 2, 1, 3) for value in (input_a, input_b, *cotangents)]
    *moved, grads, norms = both_blocks(given, live_views.T, weights, gains, biases)
    maps = [value.transpose(0, 2, 1, 3) for value in moved]
    grads[1] = grads[1].reshape(3, 3, -1, grads[1].shape[-1]).transpose(2, 0, 1, 3)
    grads[4] = grads[4].reshape(3, 3, -1, grads[4].shape[-1]).transpose(2, 0, 1, 3)
    if lax.axis_size("dp") * lax.axis_size("rows") > SHARDS:
        grads = [lax.psum_scatter(g, "rows", scatter_dimension=0, tiled=True) for g in grads]
    small = []
    for i in range(7):
        small += [norms[i].reshape(-1), norms[7 + i].reshape(-1)]
    return (*maps, *grads, *small)


def solution(mesh):
    split = P("rows", "dp", None, None)
    whole = P()
    shard = P(("dp", "rows"), None)
    shard_4 = P(("dp", "rows"), None, None, None)
    return jax.shard_map(
        on_device,
        mesh=mesh,
        in_specs=(split, split) + (whole,) * 22 + (split, split),
        out_specs=(split,) * 4
        + (shard, shard_4, shard, shard, shard_4, shard, shard)
        + (whole,) * 14,
        check_vma=False,
    )
```

```python
import functools
from types import SimpleNamespace

import jax
import jax.numpy as jnp
from jax import lax
from jax.experimental import pallas as pl
from jax.experimental.pallas import tpu as pltpu
from jax.sharding import PartitionSpec as P

MESH = pl.DeviceIdType.MESH
F32 = jnp.float32
BF16 = jnp.bfloat16

HA = 14
WA = 14
HB = 10
WB = 10

EPS = 1e-05
LEAF = 1024
NARROW, SPATIAL, WIDENED, SQUEEZE, STRIDED, OUTPUT, SHORTCUT = range(7)
Y_FIRST = (0, 1, 2, 3, 4)
X_FIRST = (0, 2, 1, 3, 4)
Z_FIRST = (0, 3, 2, 1, 4)
BITS = 5
SHARDS = 1 << BITS
REDUCE_ONE, SPATIAL_ONE, EXPAND_ONE, REDUCE_TWO, SPATIAL_TWO, EXPAND_TWO, SHORTCUT_TWO = range(7)
(
    G_REDUCE_ONE,
    G_SPATIAL_ONE,
    G_EXPAND_ONE,
    G_REDUCE_TWO,
    G_SPATIAL_TWO_0,
    G_SPATIAL_TWO_1,
    G_SPATIAL_TWO_2,
    G_EXPAND_TWO_0,
    G_EXPAND_TWO_1,
    G_SHORTCUT_TWO_0,
    G_SHORTCUT_TWO_1,
    G_SHORTCUT_TWO_2,
) = range(12)
GRADS = (
    (REDUCE_ONE, 32, 0, 0, 256, Y_FIRST),
    (SPATIAL_ONE, 144, 0, 0, 128, Z_FIRST),
    (EXPAND_ONE, 16, 0, 0, 512, Y_FIRST),
    (REDUCE_TWO, 32, 0, 0, 512, Z_FIRST),
    (SPATIAL_TWO, 48, 0, 0, 512, Y_FIRST),
    (SPATIAL_TWO, 48, 1, 0, 512, X_FIRST),
    (SPATIAL_TWO, 48, 2, 0, 512, Z_FIRST),
    (EXPAND_TWO, 16, 0, 0, 1024, X_FIRST),
    (EXPAND_TWO, 16, 0, 1024, 1024, Z_FIRST),
    (SHORTCUT_TWO, 32, 0, 0, 768, Z_FIRST),
    (SHORTCUT_TWO, 32, 0, 768, 640, Y_FIRST),
    (SHORTCUT_TWO, 32, 0, 1408, 640, X_FIRST),
)
SLOTS = (
    ((7, 0), (8, 0),),
    (),
    ((9, 0), (10, 0), (11, 0), (7, 1), (8, 1),),
    (),
    (),
    (),
    ((4, 0), (5, 0), (6, 0), (7, 2), (8, 2),),
    (),
    ((3, 0), (9, 1), (10, 1), (11, 1), (7, 3), (8, 3),),
    (),
    ((4, 1), (5, 1), (6, 1),),
    (),
    ((1, 0), (9, 2), (10, 2), (11, 2), (2, 0), (3, 1), (7, 4), (8, 4),),
    (),
    ((0, 0), (9, 3), (10, 3), (11, 3), (3, 2), (4, 2), (5, 2), (6, 2), (1, 1), (2, 1), (0, 1), (9, 4), (10, 4), (11, 4), (3, 3), (4, 3), (5, 3), (6, 3), (1, 2), (2, 2), (0, 2), (3, 4), (4, 4), (5, 4), (6, 4), (1, 3), (2, 3), (0, 3), (1, 4), (2, 4), (0, 4),),
)
SPATIAL_TWO_PARTS = (G_SPATIAL_TWO_0, G_SPATIAL_TWO_1, G_SPATIAL_TWO_2)
EXPAND_TWO_PARTS = (G_EXPAND_TWO_0, G_EXPAND_TWO_1)
SHORTCUT_TWO_PARTS = (G_SHORTCUT_TWO_0, G_SHORTCUT_TWO_1, G_SHORTCUT_TWO_2)
(
    AT_ONE,
    AT_TWO,
    AT_THREE,
    AT_FOUR,
    AT_FIVE,
    AT_SHORT,
    AT_SIX,
    AT_SEVEN,
    AT_EIGHT,
    AT_NINE,
    AT_TEN,
    AT_ELEVEN,
    AT_TWELVE,
) = range(13)
SUMS = (
    (2, 256, True),
    (2, 256, True),
    (2, 1024, False),
    (2, 512, True),
    (2, 512, True),
    (2, 2048, False),
    (2, 2048, False),
    (1, 6144, False),
    (2, 512, True),
    (2, 512, True),
    (2, 1024, False),
    (2, 256, True),
    (2, 256, True),
)


def mm(left, right):
    return lax.dot_general(left, right, (((1,), (0,)), ((), ())), preferred_element_type=F32)


def mm_nt(left, right):
    return lax.dot_general(left, right, (((1,), (1,)), ((), ())), preferred_element_type=F32)


def mm_tn(left, right):
    return lax.dot_general(left, right, (((0,), (0,)), ((), ())), preferred_element_type=F32)


def sigmoid(value):
    return 0.5 + 0.5 * jnp.tanh(0.5 * value)


def slope_of(value):
    sigma = sigmoid(value)
    return sigma * (1.0 + value * (1.0 - sigma))


def flat(block):
    return block.reshape(-1, block.shape[-1])


def col_sum(value):
    return jnp.sum(value, axis=0, keepdims=True)


def wide(mask, lanes):
    return jnp.concatenate([mask] * (lanes // 128), axis=1)


def loop(count, body, init=None):
    if init is None:

        def plain(step, carry):
            body(step)
            return carry

        return lax.fori_loop(0, count, plain, 0)
    return lax.fori_loop(0, count, body, init)


def bit_of(number, bit):
    return lax.rem(number // (1 << bit), 2)


class Kernel:
    def __init__(self, sizes, refs):
        self.d_size, self.r_size, self.live_a, self.live_b = sizes
        self.total = self.d_size * self.r_size
        self.__dict__.update(refs)
        self.d = lax.axis_index("dp")
        self.r = lax.axis_index("rows")
        self.me = self.d * self.r_size + self.r
        self.low = (self.total // SHARDS).bit_length() - 1
        self.shard = self.me // (1 << self.low)
        self.r_bits = self.r_size.bit_length() - 1


    def device(self, number):
        return (number // self.r_size, lax.rem(number, self.r_size))

    def greet(self):
        barrier = pltpu.get_barrier_semaphore()

        def one(step):
            pl.semaphore_signal(
                barrier,
                inc=1,
                device_id=self.device(lax.rem(self.me + step + 1, self.total)),
                device_id_type=MESH,
            )

        loop(self.total - 1, one)

    def greeted(self):
        pl.semaphore_wait(pltpu.get_barrier_semaphore(), self.total - 1)

    def direct(self, name):
        return self.sums[name].direct

    def sum_start(self, name, vectors):
        s = self.sums[name]
        for i, vector in enumerate(vectors):
            s.pay[i : i + 1, :] = vector
        if s.direct:

            def send(step):
                pltpu.make_async_remote_copy(
                    s.pay,
                    s.near.at[self.me],
                    s.sems.at[0],
                    s.sems.at[1],
                    device_id=self.device(lax.rem(self.me + step + 1, self.total)),
                    device_id_type=MESH,
                ).start()

            loop(self.total - 1, send)
            s.near[self.me] = s.pay[...]
        else:
            for step in range(1, self.r_size):
                pltpu.make_async_remote_copy(
                    s.pay,
                    s.near.at[self.r],
                    s.sems.at[0],
                    s.sems.at[1],
                    device_id=(self.d, lax.rem(self.r + step, self.r_size)),
                    device_id_type=MESH,
                ).start()
            s.near[self.r] = s.pay[...]

    def sum_turn(self, name):
        s = self.sums[name]
        if s.direct:
            return
        several = s.near.at[0 : self.r_size - 1]
        pltpu.make_async_copy(several, several, s.sems.at[1]).wait()
        s.mid[...] = jnp.sum(s.near[...], axis=0)

        def send(step):
            pltpu.make_async_remote_copy(
                s.mid,
                s.far.at[self.d],
                s.sems.at[2],
                s.sems.at[3],
                device_id=(lax.rem(self.d + step + 1, self.d_size), self.r),
                device_id_type=MESH,
            ).start()

        loop(self.d_size - 1, send)
        s.far[self.d] = s.mid[...]

    def sum_finish(self, name):
        s = self.sums[name]
        if s.direct:
            many = s.near.at[0 : self.total - 1]
            pltpu.make_async_copy(many, many, s.sems.at[1]).wait()
            return jnp.sum(s.near[...], axis=0)
        many = s.far.at[0 : self.d_size - 1]
        pltpu.make_async_copy(many, many, s.sems.at[3]).wait()
        return jnp.sum(s.far[...], axis=0)

    def sums_sent(self):
        for s in self.sums:
            if s.direct:
                many = s.near.at[0 : self.total - 1]
                pltpu.make_async_copy(many, many, s.sems.at[0]).wait()
            else:
                several = s.near.at[0 : self.r_size - 1]
                pltpu.make_async_copy(several, several, s.sems.at[0]).wait()
                many = s.far.at[0 : self.d_size - 1]
                pltpu.make_async_copy(many, many, s.sems.at[2]).wait()


    def norm_ready(self, norm, totals, count):
        coef = self.coef[norm]
        mean = totals[0:1] / count
        scale = lax.rsqrt(totals[1:2] / count - mean * mean + EPS)
        factor = scale * self.gain[norm][...]
        coef[0:1, :] = factor
        coef[1:2, :] = self.bias[norm][...] - mean * factor
        coef[2:3, :] = mean
        coef[3:4, :] = scale

    def norm_back_ready(self, norm, first, second, count):
        coef = self.coef[norm]
        factor, mean, scale = coef[0:1, :], coef[2:3, :], coef[3:4, :]
        second = second * scale
        self.grad_gain[norm][...] = second
        self.grad_bias[norm][...] = first
        slant = factor * scale * (second / count)
        coef[4:5, :] = slant
        coef[5:6, :] = factor * (first / count) - mean * slant

    def act(self, norm, value, lanes=slice(None)):
        coef = self.coef[norm]
        return value * coef[0:1, lanes] + coef[1:2, lanes]

    def off_mean(self, norm, value, lanes=slice(None)):
        return value - self.coef[norm][2:3, lanes]

    def back(self, norm, slope, value, mask, lanes=slice(None)):
        coef = self.coef[norm]
        grad = slope * coef[0:1, lanes] - value * coef[4:5, lanes] - coef[5:6, lanes]
        return (grad * mask).astype(BF16)


    def to_strip(self, step, src, dst, slot):
        return pltpu.make_async_remote_copy(
            src,
            dst,
            self.halo_send.at[slot],
            self.halo_recv.at[slot],
            device_id=(self.d, self.r + step),
            device_id_type=MESH,
        )

    def has_strip(self, step):
        return self.r > 0 if step < 0 else self.r < self.r_size - 1

    def edge_send(self, step, value, stage, target, slot):
        count = value.shape[0]
        base = value[0, 0:1].astype(BF16)
        stage[0:count] = (value - base.astype(F32)).astype(BF16)
        stage[count] = jnp.broadcast_to(base.astype(F32), value.shape[1:]).astype(BF16)

        @pl.when(self.has_strip(step))
        def _():
            self.to_strip(step, stage, target, slot).start()

    def edge_sent(self, step, stage, target, slot):
        @pl.when(self.has_strip(step))
        def _():
            self.to_strip(step, stage, target, slot).wait_send()

    def edge_read(self, step, stage, target, slot):
        self.to_strip(-step, stage, target, slot).wait_recv()
        count = target.shape[0] - 1
        return target[0:count].astype(F32) + target[count].astype(F32)[None]


    def place(self, name, shard):
        order = GRADS[name][5]
        if isinstance(shard, int):
            return sum(((shard >> b) & 1) << (BITS - 1 - k) for k, b in enumerate(order))
        where = 0
        for k, b in enumerate(order):
            where = where + bit_of(shard, b) * (1 << (BITS - 1 - k))
        return where

    def halving(self, name, stage):
        order = GRADS[name][5]
        start = 0
        for k in range(stage):
            start = start + bit_of(self.shard, order[k]) * (1 << (BITS - 1 - k))
        half = 1 << (BITS - 1 - stage)
        mine = bit_of(self.shard, order[stage])
        offset = SHARDS - 2 * half
        bit = order[stage] + self.low
        if bit < self.r_bits:
            partner = (self.d, self.r + (1 - 2 * mine) * (1 << bit))
        else:
            partner = (self.d + (1 - 2 * mine) * (1 << (bit - self.r_bits)), self.r)
        return start + mine * half, start + (1 - mine) * half, half, offset, partner

    def grad_copy(self, name, stage):
        array, rows, part, lane, lanes, _ = GRADS[name]
        _, away, half, offset, partner = self.halving(name, stage)
        index = name * BITS + stage
        away = pl.ds(pl.multiple_of((part * SHARDS + away) * rows, 16), half * rows)
        return pltpu.make_async_remote_copy(
            self.grads[array].at[away, lane : lane + lanes],
            self.recv[name].at[pl.ds(offset * rows, half * rows)],
            self.grad_send.at[index],
            self.grad_recv.at[index],
            device_id=partner,
            device_id_type=MESH,
        )

    def grad_start(self, name):
        self.grad_copy(name, 0).start()

    def grad_slot(self, slot):
        for name, stage in SLOTS[slot]:
            self.grad_step(name, stage)

    def grad_step(self, name, stage):
        array, rows, part, lane, lanes, _ = GRADS[name]
        keep, _, half, offset, _ = self.halving(name, stage)
        keep = part * SHARDS + keep
        self.grad_copy(name, stage).wait_recv()
        own, came = self.grads[array], self.recv[name]
        across = slice(lane, lane + lanes)
        if stage < BITS - 1:
            height = 16
            while height * lanes < 65536 and (half * rows) % (2 * height) == 0:
                height *= 2

            def add(step):
                here = pl.ds(pl.multiple_of(keep * rows + step * height, 16), height)
                there = pl.ds(pl.multiple_of(offset * rows + step * height, 16), height)
                own[here, across] = own[here, across] + came[there, :]

            loop(half * rows // height, add)
            self.grad_copy(name, stage + 1).start()
            return
        here = pl.ds(pl.multiple_of(keep * rows, 16), rows)
        there = pl.ds(offset * rows, rows)
        out = self.grad_out[array]
        total = own[here, across].astype(F32) + came[there, :].astype(F32)
        if array == SPATIAL_ONE:
            for tap in range(9):
                out[tap, :, 0:128] = total[tap * 16 : tap * 16 + 8]
                out[tap, :, 128:256] = total[tap * 16 + 8 : tap * 16 + 16]
        elif array == EXPAND_ONE:
            out[:, 0:512] = total[0:8]
            out[:, 512:1024] = total[8:16]
        else:
            out[part * rows : part * rows + rows, across] = total

    def grads_sent(self):
        for name in range(len(GRADS)):
            for stage in range(BITS):
                self.grad_copy(name, stage).wait_send()

    def grad_store(self, name, block, value, lanes=slice(None), row=0):
        array, rows, part, _, _, _ = GRADS[name]
        per = 16 if array == SPATIAL_TWO else rows
        count = 256 // per
        base = (part * SHARDS + self.place(name, block * count)) * rows + row
        for s in range(count):
            where = pl.multiple_of(base + self.place(name, s) * rows, 16)
            self.grads[array][pl.ds(where, per), lanes] = value[s * per : (s + 1) * per].astype(BF16)


    def run(self):
        self.greet()
        pairs = dict(
            xa=(self.xa_in, self.xa),
            xb=(self.xb_in, self.xb),
            w1=(self.w1_in, self.w1),
            ca=(self.ca_in, self.ca),
            cb=(self.cb_in, self.cb),
            w2=(self.w2_in, self.w2),
            w3=(self.w3_in, self.w3),
            w4=(self.w4_in, self.w4),
            ws=(self.ws_in, self.ws),
            w5=(self.w5_in, self.w5),
            w6=(self.w6_in, self.w6),
        )
        loads = SimpleNamespace()
        for i, name in enumerate(pairs):
            copy = pltpu.make_async_copy(*pairs[name], self.load_sem.at[i])
            copy.start()
            setattr(loads, name, copy)

        x, z1, z2, z3, z4, z5 = self.x, self.z1, self.z2, self.z3, self.z4, self.z5
        h1, h2, feed, h4, h5 = self.h1, self.h2, self.feed, self.h4, self.h5
        big, mask = self.big, self.mask
        rows, cols, views, _ = x.shape
        half = cols // 2
        natural = [2 * (k % half) + k // half for k in range(cols)]
        zeros = functools.partial(jnp.zeros, dtype=BF16)

        live_a = self.live[0, self.d]
        live_b = self.live[1, self.d]
        all_a = self.live[0, 0]
        all_b = self.live[1, 0]
        for i in range(1, self.d_size):
            all_a = all_a + self.live[0, i]
            all_b = all_b + self.live[1, i]
        line = jnp.zeros((1, 128), jnp.int32)
        line_a = (line + all_a).astype(F32)
        line_b = (line + all_b).astype(F32)
        full_one = HA * WA * line_a + HB * WB * line_b
        half_one = ((HA + 1) // 2) * ((WA + 1) // 2) * line_a + ((HB + 1) // 2) * (
            (WB + 1) // 2
        ) * line_b
        self.full_count[...] = full_one
        self.half_count[...] = half_one

        def full(lanes):
            return wide(self.full_count[...], lanes)

        def part(lanes):
            return wide(self.half_count[...], lanes)

        def mask_of(row):
            place = lax.broadcasted_iota(jnp.int32, (cols, views, 128), 0)
            column = jnp.where(place < half, 2 * place, 2 * (place - half) + 1)
            view = lax.broadcasted_iota(jnp.int32, (cols, views, 128), 1)
            where = self.r * rows + row
            tall_a = jnp.where(where < HA, live_a, 0)
            tall_b = jnp.where(where < HB, live_b, 0)
            in_a = (view < self.live_a) & (view < tall_a)
            in_b = (view >= self.live_a) & (view - self.live_a < tall_b) & (column < WB)
            return jnp.where(in_a | in_b, 1.0, 0.0).astype(F32)

        def make_mask(row):
            mask[row] = mask_of(row)

        loop(rows, make_mask)
        side, side_2 = self.side, self.side_2
        above_a, below_a, above_2, below_2 = (
            self.edge_a.at[0],
            self.edge_a.at[1],
            self.edge_2.at[0],
            self.edge_2.at[1],
        )

        for ref in (h1, self.dz2):
            lanes = ref.shape[-1]
            ref[0] = zeros((cols + 2, views, lanes))
            ref[rows + 1] = zeros((cols + 2, views, lanes))
            for row in range(1, rows + 1):
                ref[row, 0] = zeros((views, lanes))
                ref[row, cols + 1] = zeros((views, lanes))
        h4[0] = zeros(h4.shape[1:])
        for row in range(1, rows + 1):
            h4[row, half] = zeros((views, h4.shape[-1]))
        self.dz5[rows // 2] = zeros(self.dz5.shape[1:])
        for row in range(rows // 2):
            self.dz5[row, half] = zeros((views, self.dz5.shape[-1]))

        def row_mask(row, lanes):
            return wide(flat(mask[row]), lanes)

        none = jnp.zeros((1, 256), F32)

        loads.xa.wait()
        loads.xb.wait()

        def gather_row(row):
            for k in range(cols):
                c = natural[k]
                near = self.xa[row, c].astype(F32)
                if c < self.xb.shape[1]:
                    rest = self.xb[row, c].astype(F32)
                else:
                    rest = jnp.zeros((self.live_b, near.shape[-1]), F32)
                value = jnp.concatenate([near, rest], axis=0)
                x[row, k] = (value * wide(mask[row, k], value.shape[-1])).astype(BF16)

        loop(rows, gather_row)
        loads.w1.wait()

        def reduce_row(row, carry):
            total, square = carry
            value = mm(flat(x[row]), self.w1[...])
            z1[row] = value.reshape(cols, views, -1)
            return (total + col_sum(value), square + col_sum(value * value))

        sums = loop(rows, reduce_row, (none, none))
        self.greeted()
        self.sum_start(AT_ONE, sums)
        self.sum_turn(AT_ONE)
        self.edge_send(-1, z1[0], side.at[0], below_a, 0)
        self.edge_send(1, z1[rows - 1], side.at[1], above_a, 1)
        loads.ca.wait()
        loads.cb.wait()
        for o in range(rows // 2):
            for p in range(half):
                for h in range(2):
                    lanes = slice(h * LEAF, h * LEAF + LEAF)
                    near = self.ca[o, p, :, lanes].astype(F32)
                    if p < self.cb.shape[1]:
                        rest = self.cb[o, p, :, lanes].astype(F32)
                    else:
                        rest = jnp.zeros((self.live_b, LEAF), F32)
                    self.cot[h, o * half + p] = jnp.concatenate([near, rest], axis=0).astype(BF16)
        self.norm_ready(NARROW, self.sum_finish(AT_ONE), full(256))

        def hidden_of(value, live):
            value = self.act(NARROW, value)
            return (value * sigmoid(value) * live).astype(BF16).reshape(cols, views, -1)

        def hidden_one(row):
            value = hidden_of(flat(z1[row]), row_mask(row, 256))
            for k in range(cols):
                h1[row + 1, natural[k] + 1] = value[k]

        loop(rows, hidden_one)

        def hidden_edge(step, source, slot, row):
            @pl.when(self.has_strip(step))
            def _():
                given = flat(self.edge_read(step, side.at[0], source, slot))
                value = hidden_of(given, wide(flat(mask_of(row)), 256))
                for k in range(cols):
                    h1[row + 1, natural[k] + 1] = value[k]

        loads.w2.wait()

        def conv_row(row, carry):
            total, square = carry
            value = 0.0
            for i in range(3):
                for j in range(3):
                    tap = (i * 3 + j) * 256
                    value = value + mm(flat(h1[row + i, j : j + cols]), self.w2[tap : tap + 256, :])
            value = value.reshape(cols, views, -1)
            ordered = jnp.concatenate([value[c] for c in natural], axis=0)
            z2[row] = ordered.reshape(cols, views, -1)
            kept = ordered * row_mask(row, 256)
            return (total + col_sum(kept), square + col_sum(kept * ordered))

        sums = loop(rows - 2, lambda i, carry: conv_row(i + 1, carry), (none, none))

        hidden_edge(-1, above_a, 1, -1)
        hidden_edge(1, below_a, 0, rows)
        sums = conv_row(rows - 1, conv_row(0, sums))
        self.sum_start(AT_TWO, sums)
        self.sum_turn(AT_TWO)
        self.edge_sent(-1, side.at[0], below_a, 0)
        self.edge_sent(1, side.at[1], above_a, 1)
        self.edge_send(-1, z2[0], side.at[0], below_2, 2)
        self.edge_send(1, z2[rows - 1], side.at[1], above_2, 3)
        loads.w3.wait()
        self.norm_ready(SPATIAL, self.sum_finish(AT_TWO), full(256))

        def hidden_two(row):
            value = self.act(SPATIAL, flat(z2[row]))
            value = (value * sigmoid(value) * row_mask(row, 256)).astype(BF16)
            h2[row] = value.reshape(cols, views, -1)

        loop(rows, hidden_two)

        def expand_row(row, carry):
            given = flat(h2[row])
            done = []
            for n in range(2):
                lanes = slice(n * 512, n * 512 + 512)
                value = mm(given, self.w3[:, lanes])
                z3[row, :, :, lanes] = value.reshape(cols, views, -1)
                done.append((carry[n][0] + col_sum(value), carry[n][1] + col_sum(value * value)))
            return tuple(done)

        nothing = jnp.zeros((1, 512), F32)
        sums = loop(rows, expand_row, ((nothing, nothing), (nothing, nothing)))
        sums = [jnp.concatenate([sums[0][i], sums[1][i]], axis=1) for i in range(2)]
        self.sum_start(AT_THREE, sums)
        self.sum_turn(AT_THREE)
        loads.w4.wait()
        loads.ws.wait()
        self.norm_ready(WIDENED, self.sum_finish(AT_THREE), full(1024))

        def feed_step(step):
            row, pair = step // half, lax.rem(step, half)
            here = pl.ds(pair * 2, 2)
            value = self.act(WIDENED, flat(z3[row, here])) + flat(x[row, here]).astype(F32)
            value = value * sigmoid(value) * wide(flat(mask[row, here]), 1024)
            feed[row, here] = value.astype(BF16).reshape(2, views, -1)

        loop(rows * half, feed_step)

        def squeeze_row(row, carry):
            total, square = carry
            value = mm(flat(feed[row]), self.w4[...])
            z4[row] = value.reshape(cols, views, -1)
            return (total + col_sum(value), square + col_sum(value * value))

        sums = loop(rows, squeeze_row, (nothing, nothing))
        self.sum_start(AT_FOUR, sums)
        self.sum_turn(AT_FOUR)
        self.edge_send(1, z4[rows - 1], side_2, self.edge_4, 4)

        def even(ref):
            return jnp.concatenate([flat(ref[2 * o, 0:half]) for o in range(rows // 2)], axis=0)

        for h in range(2):
            sums = []
            for n in range(2):
                lanes = slice(h * LEAF + n * 512, h * LEAF + n * 512 + 512)
                value = mm(even(feed), self.ws[:, lanes])
                big[2 + h, :, :, n * 512 : n * 512 + 512] = value.reshape(cols, views, -1)
                sums.append((col_sum(value), col_sum(value * value)))
            for i in range(2):
                self.short_sum[i : i + 1, h * LEAF : h * LEAF + LEAF] = jnp.concatenate(
                    [sums[0][i], sums[1][i]], axis=1
                )
        self.sum_start(AT_SHORT, [self.short_sum[0:1, :], self.short_sum[1:2, :]])
        self.norm_ready(SQUEEZE, self.sum_finish(AT_FOUR), full(512))

        def hidden_four(row):
            for p in range(2):
                value = self.act(SQUEEZE, flat(z4[row, p * half : p * half + half]))
                value = value * sigmoid(value) * wide(flat(mask[row, p * half : p * half + half]), 512)
                start = p * (half + 1)
                h4[row + 1, start : start + half] = value.astype(BF16).reshape(half, views, -1)

        loop(rows, hidden_four)
        loads.w5.wait()
        starts = (half, 0, half + 1)

        def taken(i, j):
            return jnp.concatenate(
                [flat(h4[2 * o + i, starts[j] : starts[j] + half]) for o in range(rows // 2)], axis=0
            )

        value = 0.0
        for i in (1, 2, 0):
            if i == 0:

                @pl.when(self.has_strip(-1))
                def _():
                    given = self.edge_read(-1, side_2, self.edge_4, 4)
                    live = mask_of(-1)
                    for p in range(2):
                        here = slice(p * half, p * half + half)
                        point = self.act(SQUEEZE, flat(given[here]))
                        point = point * sigmoid(point) * wide(flat(live[here]), 512)
                        start = p * (half + 1)
                        h4[0, start : start + half] = point.astype(BF16).reshape(half, views, -1)

            for j in range(3):
                tap = (i * 3 + j) * 512
                value = value + mm(taken(i, j), self.w5[tap : tap + 512, :])
        z5[...] = value
        half_mask = jnp.concatenate(
            [flat(mask[2 * o, 0:half]) for o in range(rows // 2)], axis=0
        )
        self.half_mask[...] = half_mask
        kept = value * wide(half_mask, 512)
        self.sum_start(AT_FIVE, (col_sum(kept), col_sum(kept * value)))
        self.sum_turn(AT_FIVE)
        self.sum_turn(AT_SHORT)
        self.edge_sent(1, side_2, self.edge_4, 4)
        row_5 = half * views
        self.edge_send(
            -1,
            z5[0:row_5, :].reshape(half, views, -1),
            side_2.at[0 : half + 1],
            self.edge_5,
            5,
        )
        loads.w6.wait()
        self.norm_ready(STRIDED, self.sum_finish(AT_FIVE), part(512))
        value = self.act(STRIDED, z5[...])
        h5[...] = (value * sigmoid(value) * wide(self.half_mask[...], 512)).astype(BF16)

        for h in range(2):
            sums = []
            for n in range(2):
                lanes = slice(h * LEAF + n * 512, h * LEAF + n * 512 + 512)
                value = mm(h5[...], self.w6[:, lanes])
                big[h, :, :, n * 512 : n * 512 + 512] = value.reshape(cols, views, -1)
                sums.append((col_sum(value), col_sum(value * value)))
            for i in range(2):
                self.main_sum[i : i + 1, h * LEAF : h * LEAF + LEAF] = jnp.concatenate(
                    [sums[0][i], sums[1][i]], axis=1
                )
        self.sum_start(AT_SIX, [self.main_sum[0:1, :], self.main_sum[1:2, :]])
        self.norm_ready(SHORTCUT, self.sum_finish(AT_SHORT), part(2048))
        self.sum_turn(AT_SIX)
        self.norm_ready(OUTPUT, self.sum_finish(AT_SIX), part(2048))

        dh4, cot = self.dh4, self.cot
        zero = jnp.zeros((1, LEAF), F32)
        for h in range(2):
            lanes = slice(h * LEAF, h * LEAF + LEAF)

            def out_step(pair, carry):
                here = pl.ds(pair * 2, 2)
                main, side = flat(big[h, here]), flat(big[2 + h, here])
                value = self.act(OUTPUT, main, lanes) + self.act(SHORTCUT, side, lanes)
                there = wide(self.half_mask[pl.ds(pl.multiple_of(pair * 2 * views, 8), 2 * views), :], LEAF)
                sigma = sigmoid(value)
                given = flat(cot[h, here]).astype(F32)
                slope = given * there * (sigma * (1.0 + value * (1.0 - sigma)))
                cot[h, here] = (value * sigma * there).astype(BF16).reshape(2, views, -1)
                for n in range(2):
                    dh4[2 * h + n, here] = slope[:, n * 512 : n * 512 + 512].reshape(2, views, -1)
                return (
                    carry[0] + col_sum(slope),
                    carry[1] + col_sum(slope * self.off_mean(OUTPUT, main, lanes)),
                    carry[2] + col_sum(slope * self.off_mean(SHORTCUT, side, lanes)),
                )

            sums = loop(half, out_step, (zero, zero, zero))
            for i in range(3):
                start = i * 2 * LEAF + h * LEAF
                self.top_sum[:, start : start + LEAF] = sums[i]
        self.sum_start(AT_SEVEN, [self.top_sum[...]])
        for o in range(rows // 2):
            for p in range(half):
                for h in range(2):
                    lanes = slice(h * LEAF, h * LEAF + LEAF)
                    done = cot[h, o * half + p].astype(F32)
                    self.ca[o, p, :, lanes] = done[0 : self.live_a].astype(BF16)
                    if p < self.cb.shape[1]:
                        self.cb[o, p, :, lanes] = done[self.live_a :].astype(BF16)
        stores = [
            pltpu.make_async_copy(self.ca, self.out_a_to, self.store_sem.at[0]),
            pltpu.make_async_copy(self.cb, self.out_b_to, self.store_sem.at[1]),
        ]
        for copy in stores:
            copy.start()
        self.sum_turn(AT_SEVEN)
        totals = self.sum_finish(AT_SEVEN)
        totals = [totals[:, i * 2 * LEAF : (i + 1) * 2 * LEAF] for i in range(3)]
        self.norm_back_ready(OUTPUT, totals[0], totals[1], part(2048))
        self.norm_back_ready(SHORTCUT, totals[0], totals[2], part(2048))

        dz6, dzs = self.dz6, self.dzs
        for h in range(2):
            lanes = slice(h * LEAF, h * LEAF + LEAF)

            def top_step(pair):
                here = pl.ds(pair * 2, 2)
                there = pl.ds(pl.multiple_of(pair * 2 * views, 16), 2 * views)
                live = wide(self.half_mask[there, :], LEAF)
                slope = jnp.concatenate([flat(dh4[2 * h + n, here]) for n in range(2)], axis=1)
                dz6[there, lanes] = self.back(OUTPUT, slope, flat(big[h, here]), live, lanes)
                dzs[there, lanes] = self.back(SHORTCUT, slope, flat(big[2 + h, here]), live, lanes)

            loop(half, top_step)

        value = mm_nt(dz6[...], self.w6[...]) * slope_of(self.act(STRIDED, z5[...]))
        self.slope5[...] = value
        self.sum_start(AT_EIGHT, (col_sum(value), col_sum(value * self.off_mean(STRIDED, z5[...]))))

        self.edge_sent(-1, side_2.at[0 : half + 1], self.edge_5, 5)
        edge_s = self.edge_4.at[0 : half + 1]
        self.edge_send(
            -1,
            self.slope5[0:row_5, :].reshape(half, views, -1),
            side_2.at[0 : half + 1],
            edge_s,
            6,
        )

        for name in EXPAND_TWO_PARTS:
            first_lane = GRADS[name][3]

            def grad_expand_two(step):
                m, n = step // 2, lax.rem(step, 2)
                left = h5[:, pl.ds(pl.multiple_of(m * 256, 256), 256)]
                lanes = pl.ds(pl.multiple_of(first_lane + n * 512, 512), 512)
                self.grad_store(name, m, mm_tn(left, dz6[:, lanes]), lanes)

            loop(4, grad_expand_two)
            self.grad_start(name)

        def clear(row):
            big[row] = jnp.zeros(big.shape[1:], F32)

        loop(rows, clear)

        def shortcut_back(n):
            lanes = pl.ds(pl.multiple_of(n * 256, 256), 256)
            value = mm_nt(dzs[...], self.ws[lanes, :]).reshape(rows // 2, half, views, -1)
            for o in range(rows // 2):
                big[2 * o, 0:half, :, lanes] = value[o]

        loop(4, shortcut_back)

        def grad_shortcut_two(m):
            here = pl.ds(pl.multiple_of(m * 256, 256), 256)
            left = jnp.concatenate(
                [flat(feed[2 * o, 0:half, :, here]) for o in range(rows // 2)], axis=0
            )
            for name in SHORTCUT_TWO_PARTS:
                lanes = slice(GRADS[name][3], GRADS[name][3] + GRADS[name][4])
                self.grad_store(name, m, mm_tn(left, dzs[:, lanes]), lanes)

        loop(4, grad_shortcut_two)
        for name in SHORTCUT_TWO_PARTS:
            self.grad_start(name)
        self.grad_slot(0)
        self.sum_turn(AT_EIGHT)
        totals = self.sum_finish(AT_EIGHT)
        self.norm_back_ready(STRIDED, totals[0:1], totals[1:2], part(512))
        dz5 = self.dz5
        value = self.back(STRIDED, self.slope5[...], z5[...], wide(self.half_mask[...], 512))
        for o in range(rows // 2):
            dz5[o, 0:half] = value[o * half * views : (o + 1) * half * views].reshape(half, views, -1)
        self.grad_slot(1)
        for i in (1, 2, 0):
            if i == 0:

                @pl.when(self.has_strip(1))
                def _():
                    given = self.edge_read(1, side_2.at[0 : half + 1], edge_s, 6)
                    point = self.edge_read(1, side_2.at[0 : half + 1], self.edge_5, 5)
                    live = wide(flat(mask_of(rows)[0:half]), 512)
                    point = self.back(STRIDED, flat(given), flat(point), live)
                    dz5[rows // 2, 0:half] = point.reshape(half, views, -1)

            lead = 1 if i == 0 else 0
            for j in (1, 2, 0):
                tap = (i * 3 + j) * 512
                start = 1 if j == 0 else 0
                given = jnp.concatenate(
                    [flat(dz5[o + lead, start : start + half]) for o in range(rows // 2)], axis=0
                )
                value = mm_nt(given, self.w5[tap : tap + 512, :]).reshape(rows // 2, half, views, -1)
                spot = slice(0, half) if j == 1 else slice(half, 2 * half)
                for o in range(rows // 2):
                    target = 2 * o if i == 1 else 2 * o + 1
                    if j == 0 or i == 0:
                        dh4[target, spot] = dh4[target, spot] + value[o]
                    else:
                        dh4[target, spot] = value[o]

        def slope_four(step, carry):
            row, p = step // 2, lax.rem(step, 2)
            here = pl.ds(p * half, half)
            before = flat(z4[row, here])
            value = flat(dh4[row, here]) * slope_of(self.act(SQUEEZE, before))
            dh4[row, here] = value.reshape(half, views, -1)
            return (
                carry[0] + col_sum(value),
                carry[1] + col_sum(value * self.off_mean(SQUEEZE, before)),
            )

        sums = loop(rows * 2, slope_four, (nothing, nothing))
        self.sum_start(AT_NINE, sums)
        self.sum_turn(AT_NINE)
        self.grad_slot(2)

        for i, name in enumerate(SPATIAL_TWO_PARTS):

            def grad_spatial_two(step):
                j, m = step // 2, lax.rem(step, 2)
                here = pl.ds(pl.multiple_of(m * 256, 256), 256)
                start = half * ((1 - j) * (2 - j) // 2) + (half + 1) * (j * (j + 1) // 2 - j)
                left = jnp.concatenate(
                    [flat(h4[2 * o + i, pl.ds(start, half), :, here]) for o in range(rows // 2)], axis=0
                )
                right = jnp.concatenate([flat(dz5[o, 0:half]) for o in range(rows // 2)], axis=0)
                self.grad_store(name, m, mm_tn(left, right), row=j * 16)

            loop(6, grad_spatial_two)
            self.grad_start(name)
        self.grad_slot(3)
        totals = self.sum_finish(AT_NINE)
        self.norm_back_ready(SQUEEZE, totals[0:1], totals[1:2], full(512))
        dz4 = self.dz4

        def back_four(step):
            row, p = step // 2, lax.rem(step, 2)
            here = pl.ds(p * half, half)
            value = self.back(
                SQUEEZE, flat(dh4[row, here]), flat(z4[row, here]), wide(flat(mask[row, here]), 512)
            )
            dz4[row, here] = value.reshape(half, views, -1)

        loop(rows * 2, back_four)
        self.grad_slot(4)

        def slope_three(row, carry):
            done = []
            for n in range(2):
                lanes = slice(n * 512, n * 512 + 512)
                before = flat(z3[row, :, :, lanes])
                grad = mm_nt(flat(dz4[row]), self.w4[lanes, :]) + flat(big[row, :, :, lanes])
                point = self.act(WIDENED, before, lanes) + flat(x[row, :, :, lanes]).astype(F32)
                value = grad * slope_of(point)
                big[row, :, :, lanes] = value.reshape(cols, views, -1)
                done.append(
                    (
                        carry[n][0] + col_sum(value),
                        carry[n][1] + col_sum(value * self.off_mean(WIDENED, before, lanes)),
                    )
                )
            return tuple(done)

        sums = loop(rows, slope_three, ((nothing, nothing), (nothing, nothing)))
        sums = [jnp.concatenate([sums[0][i], sums[1][i]], axis=1) for i in range(2)]
        self.sum_start(AT_TEN, sums)
        self.grad_slot(5)

        def grad_reduce_two(m):
            here = pl.ds(pl.multiple_of(m * 256, 256), 256)
            left = feed[:, :, :, here].reshape(-1, 256)
            self.grad_store(G_REDUCE_TWO, m, mm_tn(left, dz4[...].reshape(-1, 512)))

        loop(4, grad_reduce_two)
        self.grad_start(G_REDUCE_TWO)
        self.sum_turn(AT_TEN)
        self.grad_slot(6)
        totals = self.sum_finish(AT_TEN)
        self.norm_back_ready(WIDENED, totals[0:1], totals[1:2], full(1024))
        dz3 = feed

        def back_three(step):
            row, pair = step // half, lax.rem(step, half)
            here = pl.ds(pair * 2, 2)
            live = wide(flat(mask[row, here]), 1024)
            value = self.back(WIDENED, flat(big[row, here]), flat(z3[row, here]), live)
            dz3[row, here] = value.reshape(2, views, -1)

        loop(rows * half, back_three)
        self.grad_slot(7)


        def slope_spatial(row, carry):
            before = flat(z2[row])
            value = mm_nt(flat(dz3[row]), self.w3[...]) * slope_of(self.act(SPATIAL, before))
            dh4[row, :, :, 0:256] = value.reshape(cols, views, -1)
            return (
                carry[0] + col_sum(value),
                carry[1] + col_sum(value * self.off_mean(SPATIAL, before)),
            )

        sums = loop(rows, slope_spatial, (none, none))
        self.sum_start(AT_ELEVEN, sums)
        self.sum_turn(AT_ELEVEN)
        self.edge_sent(-1, side.at[0], below_2, 2)
        self.edge_sent(1, side.at[1], above_2, 3)
        self.edge_send(-1, dh4[0, :, :, 0:256], side.at[0], below_a, 7)
        self.edge_send(1, dh4[rows - 1, :, :, 0:256], side.at[1], above_a, 8)
        self.grad_slot(8)

        left = h2[...].reshape(-1, 256)
        g_low = mm_tn(left, dz3[:, :, :, 0:512].reshape(-1, 512))
        g_high = mm_tn(left, dz3[:, :, :, 512:1024].reshape(-1, 512))
        for s in range(SHARDS):
            at = self.place(G_EXPAND_ONE, s) * 16
            piece = jnp.concatenate([g_low[s * 8 : s * 8 + 8], g_high[s * 8 : s * 8 + 8]], axis=0)
            self.grads[EXPAND_ONE][at : at + 16, :] = piece.astype(BF16)
        self.grad_start(G_EXPAND_ONE)
        self.grad_slot(9)
        totals = self.sum_finish(AT_ELEVEN)
        self.norm_back_ready(SPATIAL, totals[0:1], totals[1:2], full(256))
        dz2 = self.dz2

        def back_two(row):
            value = self.back(SPATIAL, flat(dh4[row, :, :, 0:256]), flat(z2[row]), row_mask(row, 256))
            value = value.reshape(cols, views, -1)
            for k in range(cols):
                dz2[row + 1, natural[k] + 1] = value[k]

        loop(rows, back_two)
        self.grad_slot(10)
        for i in range(3):
            for j in range(3):
                left = h1[i : i + rows, j : j + cols].reshape(-1, 256)
                value = mm_tn(left, dz2[1 : rows + 1, 1 : cols + 1].reshape(-1, 256))
                for s in range(SHARDS):
                    at = self.place(G_SPATIAL_ONE, s) * 144 + (i * 3 + j) * 16
                    piece = value[s * 8 : s * 8 + 8]
                    piece = jnp.concatenate([piece[:, 0:128], piece[:, 128:256]], axis=0)
                    self.grads[SPATIAL_ONE][at : at + 16, :] = piece.astype(BF16)
        self.grad_start(G_SPATIAL_ONE)
        self.grad_slot(11)

        def edge_two(step, slope_from, slope_slot, value_from, value_slot, row):
            @pl.when(self.has_strip(step))
            def _():
                given = flat(self.edge_read(step, side.at[0], slope_from, slope_slot))
                point = flat(self.edge_read(step, side.at[0], value_from, value_slot))
                value = self.back(SPATIAL, given, point, wide(flat(mask_of(row)), 256))
                value = value.reshape(cols, views, -1)
                for k in range(cols):
                    dz2[row + 1, natural[k] + 1] = value[k]

        edge_two(-1, above_a, 8, above_2, 3, -1)
        edge_two(1, below_a, 7, below_2, 2, rows)

        def slope_narrow(row, carry):
            value = 0.0
            for i in range(3):
                for j in range(3):
                    tap = (i * 3 + j) * 256
                    given = flat(dz2[row + 2 - i, 2 - j : 2 - j + cols])
                    value = value + mm_nt(given, self.w2[tap : tap + 256, :])
            value = value.reshape(cols, views, -1)
            value = jnp.concatenate([value[c] for c in natural], axis=0)
            before = flat(z1[row])
            value = value * row_mask(row, 256) * slope_of(self.act(NARROW, before))
            dh4[row, :, :, 0:256] = value.reshape(cols, views, -1)
            return (
                carry[0] + col_sum(value),
                carry[1] + col_sum(value * self.off_mean(NARROW, before)),
            )

        sums = loop(rows, slope_narrow, (none, none))
        self.sum_start(AT_TWELVE, sums)
        self.sum_turn(AT_TWELVE)
        self.grad_slot(12)
        totals = self.sum_finish(AT_TWELVE)
        self.norm_back_ready(NARROW, totals[0:1], totals[1:2], full(256))
        dz1 = h2

        def back_one(row):
            value = self.back(NARROW, flat(dh4[row, :, :, 0:256]), flat(z1[row]), row_mask(row, 256))
            dz1[row] = value.reshape(cols, views, -1)

        loop(rows, back_one)

        def grad_reduce_one(m):
            here = pl.ds(pl.multiple_of(m * 256, 256), 256)
            left = x[:, :, :, here].reshape(-1, 256)
            self.grad_store(G_REDUCE_ONE, m, mm_tn(left, dz1[...].reshape(-1, 256)))

        loop(4, grad_reduce_one)
        self.grad_start(G_REDUCE_ONE)
        self.grad_slot(13)

        def input_row(row):
            for n in range(2):
                lanes = slice(n * 512, n * 512 + 512)
                value = mm_nt(flat(dz1[row]), self.w1[lanes, :]) + flat(big[row, :, :, lanes])
                value = value.reshape(cols, views, -1)
                for k in range(cols):
                    self.xa[row, natural[k], :, lanes] = value[k, 0 : self.live_a].astype(BF16)
                    if natural[k] < self.xb.shape[1]:
                        self.xb[row, natural[k], :, lanes] = value[k, self.live_a :].astype(BF16)

        loop(rows, input_row)
        for i, pair in enumerate(((self.xa, self.in_a_to), (self.xb, self.in_b_to))):
            copy = pltpu.make_async_copy(*pair, self.store_sem.at[2 + i])
            copy.start()
            stores.append(copy)

        self.grad_slot(14)
        for copy in stores:
            copy.wait()
        self.sums_sent()
        self.grads_sent()

        self.edge_sent(-1, side_2.at[0 : half + 1], edge_s, 6)
        self.edge_sent(-1, side.at[0], below_a, 7)
        self.edge_sent(1, side.at[1], above_a, 8)


def settle(*refs):
    half = len(refs) // 2
    for i in range(half):
        refs[half + i][...] = refs[i][...]


def settled(values):
    inside = pl.BlockSpec(memory_space=pltpu.VMEM)
    return pl.pallas_call(
        settle,
        out_shape=[jax.ShapeDtypeStruct(v.shape, v.dtype) for v in values],
        in_specs=[inside] * len(values),
        out_specs=[inside] * len(values),
    )(*values)


def sum_of(pay, near, mid, far, sems):
    return SimpleNamespace(direct=far is None, pay=pay, near=near, mid=mid, far=far, sems=sems)


def both_blocks(given, live_views, weights, gains, biases):
    d_size, r_size = lax.axis_size("dp"), lax.axis_size("rows")
    total = d_size * r_size
    rows, cols, views_a, c_in = given[0].shape
    views_b = given[1].shape[2]
    views = views_a + views_b
    half = cols // 2
    c_mid, c_mid2, c_out = gains[0].shape[1], gains[3].shape[1], gains[5].shape[1]
    pixels = (rows // 2) * half * views
    vmem, dma = pltpu.VMEM, pltpu.SemaphoreType.DMA
    anywhere = pl.BlockSpec(memory_space=pl.ANY)
    inside = pl.BlockSpec(memory_space=pltpu.VMEM)

    def full(lanes, kind):
        return vmem((rows, cols, views, lanes), kind)

    def like(value):
        return vmem(value.shape, value.dtype)

    sums = []
    for count, lanes, straight in SUMS:
        direct = straight and total <= 32
        sums.append(
            dict(
                pay=vmem((count, lanes), F32),
                near=vmem((total if direct else r_size, count, lanes), F32),
                mid=None if direct else vmem((count, lanes), F32),
                far=None if direct else vmem((d_size, count, lanes), F32),
                sems=dma((4,)),
            )
        )
    w = weights
    scratch = dict(
        xa=like(given[0]),
        xb=like(given[1]),
        ca=like(given[2]),
        cb=like(given[3]),
        x=full(c_in, BF16),
        w1=like(w[0]),
        w2=like(w[1]),
        w3=like(w[2]),
        w4=like(w[3]),
        w5=like(w[4]),
        w6=like(w[5]),
        ws=like(w[6]),
        cot=vmem((2, cols, views, LEAF), BF16),
        mask=full(128, F32),
        half_mask=vmem((pixels, 128), F32),
        full_count=vmem((1, 128), F32),
        half_count=vmem((1, 128), F32),
        z1=full(c_mid, F32),
        z2=full(c_mid, F32),
        z3=full(c_in, F32),
        z4=full(c_mid2, F32),
        z5=vmem((pixels, c_mid2), F32),
        h1=vmem((rows + 2, cols + 2, views, c_mid), BF16),
        h2=full(c_mid, BF16),
        feed=full(c_in, BF16),
        h4=vmem((rows + 1, cols + 1, views, c_mid2), BF16),
        h5=vmem((pixels, c_mid2), BF16),
        big=full(c_in, F32),
        short_sum=vmem((2, c_out), F32),
        main_sum=vmem((2, c_out), F32),
        top_sum=vmem((1, 3 * c_out), F32),
        dz6=vmem((pixels, c_out), BF16),
        dzs=vmem((pixels, c_out), BF16),
        slope5=vmem((pixels, c_mid2), F32),
        dz5=vmem((rows // 2 + 1, half + 1, views, c_mid2), BF16),
        dh4=full(c_mid2, F32),
        dz4=full(c_mid2, BF16),
        dz2=vmem((rows + 2, cols + 2, views, c_mid), BF16),
        g2=vmem((SHARDS * 144, 128), BF16),
        g3=vmem((SHARDS * 16, 512), BF16),
        load_sem=dma((11,)),
        store_sem=dma((4,)),
        side=vmem((2, cols + 1, views, c_mid), BF16),
        edge_a=vmem((2, cols + 1, views, c_mid), BF16),
        edge_2=vmem((2, cols + 1, views, c_mid), BF16),
        side_2=vmem((cols + 1, views, c_mid2), BF16),
        edge_4=vmem((cols + 1, views, c_mid2), BF16),
        edge_5=vmem((half + 1, views, c_mid2), BF16),
        halo_send=dma((9,)),
        halo_recv=dma((9,)),
        grad_send=dma((len(GRADS) * BITS,)),
        grad_recv=dma((len(GRADS) * BITS,)),
        coef=[vmem((8, gain.shape[1]), F32) for gain in gains],
        recv=[vmem(((SHARDS - 1) * height, lanes), BF16) for _, height, _, _, lanes, _ in GRADS],
        sums=sums,
    )
    grad_shapes = ((32, 256), (9, 8, 256), (8, 1024), (32, 512), (144, 512), (16, 2048), (32, 2048))
    ins = dict(
        live=live_views,
        xa_in=given[0],
        xb_in=given[1],
        ca_in=given[2],
        cb_in=given[3],
        w1_in=w[0],
        w2_in=w[1],
        w3_in=w[2],
        w4_in=w[3],
        w5_in=w[4],
        w6_in=w[5],
        ws_in=w[6],
        gain=list(gains),
        bias=list(biases),
    )
    shape = jax.ShapeDtypeStruct
    outs = dict(
        out_a_to=shape(given[2].shape, BF16),
        out_b_to=shape(given[3].shape, BF16),
        in_a_to=shape(given[0].shape, BF16),
        in_b_to=shape(given[1].shape, BF16),
        grad_out=[shape(s, F32) for s in grad_shapes],
        grad_gain=[shape(g.shape, F32) for g in gains],
        grad_bias=[shape(g.shape, F32) for g in gains],
    )
    parts = []
    trees = []
    for group in (ins, outs, scratch):
        leaves, tree = jax.tree.flatten(group, is_leaf=lambda v: not isinstance(v, (dict, list, type(None))))
        parts.append(leaves)
        trees.append(tree)
    in_specs = dict(ins)
    for name in ins:
        in_specs[name] = [inside] * len(gains) if isinstance(ins[name], list) else anywhere
    in_specs.update(live=pl.BlockSpec(memory_space=pltpu.SMEM))
    out_specs = {
        name: [inside] * len(outs[name]) if isinstance(outs[name], list) else anywhere for name in outs
    }
    spec_leaves = [
        jax.tree.flatten(group, is_leaf=lambda v: isinstance(v, pl.BlockSpec))[0]
        for group in (in_specs, out_specs)
    ]

    def body(*refs):
        fields = {}
        start = 0
        for leaves, tree in zip(parts, trees):
            fields.update(jax.tree.unflatten(tree, refs[start : start + len(leaves)]))
            start += len(leaves)
        g = SimpleNamespace(**fields)
        fields.update(
            grads=[g.w2, g.g2, g.g3, g.w4, g.w5, g.w6, g.ws],
            sums=[sum_of(**s) for s in g.sums],
        )
        Kernel((d_size, r_size, views_a, views_b), fields).run()

    results = pl.pallas_call(
        body,
        out_shape=parts[1],
        in_specs=spec_leaves[0],
        out_specs=spec_leaves[1],
        scratch_shapes=parts[2],
        compiler_params=pltpu.CompilerParams(
            collective_id=0, has_side_effects=True, vmem_limit_bytes=64 * 2**20 - 65536 * 4
        ),
        cost_estimate=pl.CostEstimate(flops=16 * 10**9, bytes_accessed=30 * 10**6, transcendentals=4 * 10**6),
    )(*parts[0])
    done = SimpleNamespace(**jax.tree.unflatten(trees[1], results))
    plain = settled([done.out_a_to, done.in_a_to, *done.grad_out, *done.grad_gain, *done.grad_bias])
    return plain[0], done.out_b_to, plain[1], done.in_b_to, list(plain[2:9]), plain[9:]


def on_device(input_a, input_b, live_views, *rest):
    weights, params, cotangents = rest[:7], rest[7:21], rest[21:]
    gains = [value.reshape(1, -1) for value in params[0::2]]
    biases = [value.reshape(1, -1) for value in params[1::2]]
    reduce_one, spatial_one, expand_one, reduce_two, spatial_two, expand_two, shortcut_two = weights
    weights = (
        reduce_one,
        spatial_one.transpose(1, 2, 0, 3).reshape(-1, spatial_one.shape[-1]),
        expand_one,
        reduce_two,
        spatial_two.transpose(1, 2, 0, 3).reshape(-1, spatial_two.shape[-1]),
        expand_two,
        shortcut_two,
    )
    given = [value.transpose(0, 2, 1, 3) for value in (input_a, input_b, *cotangents)]
    *moved, grads, norms = both_blocks(given, live_views.T, weights, gains, biases)
    maps = [value.transpose(0, 2, 1, 3) for value in moved]
    grads[1] = grads[1].reshape(3, 3, -1, grads[1].shape[-1]).transpose(2, 0, 1, 3)
    grads[4] = grads[4].reshape(3, 3, -1, grads[4].shape[-1]).transpose(2, 0, 1, 3)
    if lax.axis_size("dp") * lax.axis_size("rows") > SHARDS:
        grads = [lax.psum_scatter(g, "rows", scatter_dimension=0, tiled=True) for g in grads]
    small = []
    for i in range(7):
        small += [norms[i].reshape(-1), norms[7 + i].reshape(-1)]
    return (*maps, *grads, *small)


def solution(mesh):
    split = P("rows", "dp", None, None)
    whole = P()
    shard = P(("dp", "rows"), None)
    shard_4 = P(("dp", "rows"), None, None, None)
    return jax.shard_map(
        on_device,
        mesh=mesh,
        in_specs=(split, split) + (whole,) * 22 + (split, split),
        out_specs=(split,) * 4
        + (shard, shard_4, shard, shard, shard_4, shard, shard)
        + (whole,) * 14,
        check_vma=False,
    )
```

```python
import functools
from types import SimpleNamespace

import jax
import jax.numpy as jnp
from jax import lax
from jax.experimental import pallas as pl
from jax.experimental.pallas import tpu as pltpu
from jax.sharding import PartitionSpec as P

MESH = pl.DeviceIdType.MESH
F32 = jnp.float32
BF16 = jnp.bfloat16

HA = 14
WA = 14
HB = 10
WB = 10

EPS = 1e-05
LEAF = 1024
NARROW, SPATIAL, WIDENED, SQUEEZE, STRIDED, OUTPUT, SHORTCUT = range(7)
Y_FIRST = (0, 1, 2, 3, 4)
X_FIRST = (0, 2, 1, 3, 4)
Z_FIRST = (0, 3, 2, 1, 4)
BITS = 5
SHARDS = 1 << BITS
REDUCE_ONE, SPATIAL_ONE, EXPAND_ONE, REDUCE_TWO, SPATIAL_TWO, EXPAND_TWO, SHORTCUT_TWO = range(7)
(
    G_REDUCE_ONE,
    G_SPATIAL_ONE,
    G_EXPAND_ONE,
    G_REDUCE_TWO,
    G_SPATIAL_TWO_0,
    G_SPATIAL_TWO_1,
    G_SPATIAL_TWO_2,
    G_EXPAND_TWO_0,
    G_EXPAND_TWO_1,
    G_SHORTCUT_TWO_0,
    G_SHORTCUT_TWO_1,
    G_SHORTCUT_TWO_2,
) = range(12)
GRADS = (
    (REDUCE_ONE, 32, 0, 0, 256, Y_FIRST),
    (SPATIAL_ONE, 144, 0, 0, 128, Z_FIRST),
    (EXPAND_ONE, 16, 0, 0, 512, Y_FIRST),
    (REDUCE_TWO, 32, 0, 0, 512, Z_FIRST),
    (SPATIAL_TWO, 48, 0, 0, 512, Y_FIRST),
    (SPATIAL_TWO, 48, 1, 0, 512, X_FIRST),
    (SPATIAL_TWO, 48, 2, 0, 512, Z_FIRST),
    (EXPAND_TWO, 16, 0, 0, 1024, X_FIRST),
    (EXPAND_TWO, 16, 0, 1024, 1024, Z_FIRST),
    (SHORTCUT_TWO, 32, 0, 0, 768, Z_FIRST),
    (SHORTCUT_TWO, 32, 0, 768, 640, Y_FIRST),
    (SHORTCUT_TWO, 32, 0, 1408, 640, X_FIRST),
)
SLOTS = (
    ((7, 0), (8, 0),),
    (),
    ((9, 0), (10, 0), (11, 0), (7, 1), (8, 1),),
    (),
    (),
    (),
    ((4, 0), (5, 0), (6, 0), (7, 2), (8, 2),),
    (),
    ((3, 0), (9, 1), (10, 1), (11, 1), (7, 3), (8, 3),),
    (),
    ((4, 1), (5, 1), (6, 1),),
    (),
    ((1, 0), (9, 2), (10, 2), (11, 2), (2, 0), (3, 1), (7, 4), (8, 4),),
    (),
    ((0, 0), (9, 3), (10, 3), (11, 3), (3, 2), (4, 2), (5, 2), (6, 2), (1, 1), (2, 1), (0, 1), (9, 4), (10, 4), (11, 4), (3, 3), (4, 3), (5, 3), (6, 3), (1, 2), (2, 2), (0, 2), (3, 4), (4, 4), (5, 4), (6, 4), (1, 3), (2, 3), (0, 3), (1, 4), (2, 4), (0, 4),),
)
SPATIAL_TWO_PARTS = (G_SPATIAL_TWO_0, G_SPATIAL_TWO_1, G_SPATIAL_TWO_2)
EXPAND_TWO_PARTS = (G_EXPAND_TWO_0, G_EXPAND_TWO_1)
SHORTCUT_TWO_PARTS = (G_SHORTCUT_TWO_0, G_SHORTCUT_TWO_1, G_SHORTCUT_TWO_2)
(
    AT_ONE,
    AT_TWO,
    AT_THREE,
    AT_FOUR,
    AT_FIVE,
    AT_SHORT,
    AT_SIX,
    AT_SEVEN,
    AT_EIGHT,
    AT_NINE,
    AT_TEN,
    AT_ELEVEN,
    AT_TWELVE,
) = range(13)
SUMS = (
    (2, 256, True),
    (2, 256, True),
    (2, 1024, False),
    (2, 512, True),
    (2, 512, True),
    (2, 2048, False),
    (2, 2048, False),
    (1, 6144, False),
    (2, 512, True),
    (2, 512, True),
    (2, 1024, False),
    (2, 256, True),
    (2, 256, True),
)


def mm(left, right):
    return lax.dot_general(left, right, (((1,), (0,)), ((), ())), preferred_element_type=F32)


def mm_nt(left, right):
    return lax.dot_general(left, right, (((1,), (1,)), ((), ())), preferred_element_type=F32)


def mm_tn(left, right):
    return lax.dot_general(left, right, (((0,), (0,)), ((), ())), preferred_element_type=F32)


def sigmoid(value):
    return 0.5 + 0.5 * jnp.tanh(0.5 * value)


def slope_of(value):
    sigma = sigmoid(value)
    return sigma * (1.0 + value * (1.0 - sigma))


def flat(block):
    return block.reshape(-1, block.shape[-1])


def col_sum(value):
    return jnp.sum(value, axis=0, keepdims=True)


def wide(mask, lanes):
    return jnp.concatenate([mask] * (lanes // 128), axis=1)


def loop(count, body, init=None):
    if init is None:

        def plain(step, carry):
            body(step)
            return carry

        return lax.fori_loop(0, count, plain, 0)
    return lax.fori_loop(0, count, body, init)


def bit_of(number, bit):
    return lax.rem(number // (1 << bit), 2)


class Kernel:
    def __init__(self, sizes, refs):
        self.d_size, self.r_size, self.live_a, self.live_b = sizes
        self.total = self.d_size * self.r_size
        self.__dict__.update(refs)
        self.d = lax.axis_index("dp")
        self.r = lax.axis_index("rows")
        self.me = self.d * self.r_size + self.r
        self.low = (self.total // SHARDS).bit_length() - 1
        self.shard = self.me // (1 << self.low)
        self.r_bits = self.r_size.bit_length() - 1


    def device(self, number):
        return (number // self.r_size, lax.rem(number, self.r_size))

    def greet(self):
        barrier = pltpu.get_barrier_semaphore()

        def one(step):
            pl.semaphore_signal(
                barrier,
                inc=1,
                device_id=self.device(lax.rem(self.me + step + 1, self.total)),
                device_id_type=MESH,
            )

        loop(self.total - 1, one)

    def greeted(self):
        pl.semaphore_wait(pltpu.get_barrier_semaphore(), self.total - 1)

    def direct(self, name):
        return self.sums[name].direct

    def sum_start(self, name, vectors):
        s = self.sums[name]
        for i, vector in enumerate(vectors):
            s.pay[i : i + 1, :] = vector
        if s.direct:

            def send(step):
                pltpu.make_async_remote_copy(
                    s.pay,
                    s.near.at[self.me],
                    s.sems.at[0],
                    s.sems.at[1],
                    device_id=self.device(lax.rem(self.me + step + 1, self.total)),
                    device_id_type=MESH,
                ).start()

            loop(self.total - 1, send)
            s.near[self.me] = s.pay[...]
        else:
            for step in range(1, self.r_size):
                pltpu.make_async_remote_copy(
                    s.pay,
                    s.near.at[self.r],
                    s.sems.at[0],
                    s.sems.at[1],
                    device_id=(self.d, lax.rem(self.r + step, self.r_size)),
                    device_id_type=MESH,
                ).start()
            s.near[self.r] = s.pay[...]

    def sum_turn(self, name):
        s = self.sums[name]
        if s.direct:
            return
        several = s.near.at[0 : self.r_size - 1]
        pltpu.make_async_copy(several, several, s.sems.at[1]).wait()
        s.mid[...] = jnp.sum(s.near[...], axis=0)

        def send(step):
            pltpu.make_async_remote_copy(
                s.mid,
                s.far.at[self.d],
                s.sems.at[2],
                s.sems.at[3],
                device_id=(lax.rem(self.d + step + 1, self.d_size), self.r),
                device_id_type=MESH,
            ).start()

        loop(self.d_size - 1, send)
        s.far[self.d] = s.mid[...]

    def sum_finish(self, name):
        s = self.sums[name]
        if s.direct:
            many = s.near.at[0 : self.total - 1]
            pltpu.make_async_copy(many, many, s.sems.at[1]).wait()
            return jnp.sum(s.near[...], axis=0)
        many = s.far.at[0 : self.d_size - 1]
        pltpu.make_async_copy(many, many, s.sems.at[3]).wait()
        return jnp.sum(s.far[...], axis=0)

    def sums_sent(self):
        for s in self.sums:
            if s.direct:
                many = s.near.at[0 : self.total - 1]
                pltpu.make_async_copy(many, many, s.sems.at[0]).wait()
            else:
                several = s.near.at[0 : self.r_size - 1]
                pltpu.make_async_copy(several, several, s.sems.at[0]).wait()
                many = s.far.at[0 : self.d_size - 1]
                pltpu.make_async_copy(many, many, s.sems.at[2]).wait()


    def norm_ready(self, norm, totals, count):
        coef = self.coef[norm]
        mean = totals[0:1] / count
        scale = lax.rsqrt(totals[1:2] / count - mean * mean + EPS)
        factor = scale * self.gain[norm][...]
        coef[0:1, :] = factor
        coef[1:2, :] = self.bias[norm][...] - mean * factor
        coef[2:3, :] = mean
        coef[3:4, :] = scale

    def norm_back_ready(self, norm, first, second, count):
        coef = self.coef[norm]
        factor, mean, scale = coef[0:1, :], coef[2:3, :], coef[3:4, :]
        second = second * scale
        self.grad_gain[norm][...] = second
        self.grad_bias[norm][...] = first
        slant = factor * scale * (second / count)
        coef[4:5, :] = slant
        coef[5:6, :] = factor * (first / count) - mean * slant

    def act(self, norm, value, lanes=slice(None)):
        coef = self.coef[norm]
        return value * coef[0:1, lanes] + coef[1:2, lanes]

    def off_mean(self, norm, value, lanes=slice(None)):
        return value - self.coef[norm][2:3, lanes]

    def back(self, norm, slope, value, mask, lanes=slice(None)):
        coef = self.coef[norm]
        grad = slope * coef[0:1, lanes] - value * coef[4:5, lanes] - coef[5:6, lanes]
        return (grad * mask).astype(BF16)


    def to_strip(self, step, src, dst, slot):
        return pltpu.make_async_remote_copy(
            src,
            dst,
            self.halo_send.at[slot],
            self.halo_recv.at[slot],
            device_id=(self.d, self.r + step),
            device_id_type=MESH,
        )

    def has_strip(self, step):
        return self.r > 0 if step < 0 else self.r < self.r_size - 1

    def edge_send(self, step, value, stage, target, slot):
        count = value.shape[0]
        base = value[0, 0:1].astype(BF16)
        stage[0:count] = (value - base.astype(F32)).astype(BF16)
        stage[count] = jnp.broadcast_to(base.astype(F32), value.shape[1:]).astype(BF16)

        @pl.when(self.has_strip(step))
        def _():
            self.to_strip(step, stage, target, slot).start()

    def edge_sent(self, step, stage, target, slot):
        @pl.when(self.has_strip(step))
        def _():
            self.to_strip(step, stage, target, slot).wait_send()

    def edge_read(self, step, stage, target, slot):
        self.to_strip(-step, stage, target, slot).wait_recv()
        count = target.shape[0] - 1
        return target[0:count].astype(F32) + target[count].astype(F32)[None]


    def place(self, name, shard):
        order = GRADS[name][5]
        if isinstance(shard, int):
            return sum(((shard >> b) & 1) << (BITS - 1 - k) for k, b in enumerate(order))
        where = 0
        for k, b in enumerate(order):
            where = where + bit_of(shard, b) * (1 << (BITS - 1 - k))
        return where

    def halving(self, name, stage):
        order = GRADS[name][5]
        start = 0
        for k in range(stage):
            start = start + bit_of(self.shard, order[k]) * (1 << (BITS - 1 - k))
        half = 1 << (BITS - 1 - stage)
        mine = bit_of(self.shard, order[stage])
        offset = SHARDS - 2 * half
        bit = order[stage] + self.low
        if bit < self.r_bits:
            partner = (self.d, self.r + (1 - 2 * mine) * (1 << bit))
        else:
            partner = (self.d + (1 - 2 * mine) * (1 << (bit - self.r_bits)), self.r)
        return start + mine * half, start + (1 - mine) * half, half, offset, partner

    def grad_copy(self, name, stage):
        array, rows, part, lane, lanes, _ = GRADS[name]
        _, away, half, offset, partner = self.halving(name, stage)
        index = name * BITS + stage
        away = pl.ds(pl.multiple_of((part * SHARDS + away) * rows, 16), half * rows)
        return pltpu.make_async_remote_copy(
            self.grads[array].at[away, lane : lane + lanes],
            self.recv[name].at[pl.ds(offset * rows, half * rows)],
            self.grad_send.at[index],
            self.grad_recv.at[index],
            device_id=partner,
            device_id_type=MESH,
        )

    def grad_start(self, name):
        self.grad_copy(name, 0).start()

    def grad_slot(self, slot):
        for name, stage in SLOTS[slot]:
            self.grad_step(name, stage)

    def grad_step(self, name, stage):
        array, rows, part, lane, lanes, _ = GRADS[name]
        keep, _, half, offset, _ = self.halving(name, stage)
        keep = part * SHARDS + keep
        self.grad_copy(name, stage).wait_recv()
        own, came = self.grads[array], self.recv[name]
        across = slice(lane, lane + lanes)
        if stage < BITS - 1:
            height = 16
            while height * lanes < 65536 and (half * rows) % (2 * height) == 0:
                height *= 2

            def add(step):
                here = pl.ds(pl.multiple_of(keep * rows + step * height, 16), height)
                there = pl.ds(pl.multiple_of(offset * rows + step * height, 16), height)
                own[here, across] = own[here, across] + came[there, :]

            loop(half * rows // height, add)
            self.grad_copy(name, stage + 1).start()
            return
        here = pl.ds(pl.multiple_of(keep * rows, 16), rows)
        there = pl.ds(offset * rows, rows)
        out = self.grad_out[array]
        total = own[here, across].astype(F32) + came[there, :].astype(F32)
        if array == SPATIAL_ONE:
            for tap in range(9):
                out[tap, :, 0:128] = total[tap * 16 : tap * 16 + 8]
                out[tap, :, 128:256] = total[tap * 16 + 8 : tap * 16 + 16]
        elif array == EXPAND_ONE:
            out[:, 0:512] = total[0:8]
            out[:, 512:1024] = total[8:16]
        else:
            out[part * rows : part * rows + rows, across] = total

    def grads_sent(self):
        for name in range(len(GRADS)):
            for stage in range(BITS):
                self.grad_copy(name, stage).wait_send()

    def grad_store(self, name, block, value, lanes=slice(None), row=0):
        array, rows, part, _, _, _ = GRADS[name]
        per = 16 if array == SPATIAL_TWO else rows
        count = 256 // per
        base = (part * SHARDS + self.place(name, block * count)) * rows + row
        for s in range(count):
            where = pl.multiple_of(base + self.place(name, s) * rows, 16)
            self.grads[array][pl.ds(where, per), lanes] = value[s * per : (s + 1) * per].astype(BF16)


    def run(self):
        self.greet()
        pairs = dict(
            xa=(self.xa_in, self.xa),
            xb=(self.xb_in, self.xb),
            w1=(self.w1_in, self.w1),
            ca=(self.ca_in, self.ca),
            cb=(self.cb_in, self.cb),
            w2=(self.w2_in, self.w2),
            w3=(self.w3_in, self.w3),
            w4=(self.w4_in, self.w4),
            ws=(self.ws_in, self.ws),
            w5=(self.w5_in, self.w5),
            w6=(self.w6_in, self.w6),
        )
        loads = SimpleNamespace()
        for i, name in enumerate(pairs):
            copy = pltpu.make_async_copy(*pairs[name], self.load_sem.at[i])
            copy.start()
            setattr(loads, name, copy)

        x, z1, z2, z3, z4, z5 = self.x, self.z1, self.z2, self.z3, self.z4, self.z5
        h1, h2, feed, h4, h5 = self.h1, self.h2, self.feed, self.h4, self.h5
        big, mask = self.big, self.mask
        rows, cols, views, _ = x.shape
        half = cols // 2
        natural = [2 * (k % half) + k // half for k in range(cols)]
        zeros = functools.partial(jnp.zeros, dtype=BF16)

        live_a = self.live[0, self.d]
        live_b = self.live[1, self.d]
        all_a = self.live[0, 0]
        all_b = self.live[1, 0]
        for i in range(1, self.d_size):
            all_a = all_a + self.live[0, i]
            all_b = all_b + self.live[1, i]
        line = jnp.zeros((1, 128), jnp.int32)
        line_a = (line + all_a).astype(F32)
        line_b = (line + all_b).astype(F32)
        full_one = HA * WA * line_a + HB * WB * line_b
        half_one = ((HA + 1) // 2) * ((WA + 1) // 2) * line_a + ((HB + 1) // 2) * (
            (WB + 1) // 2
        ) * line_b
        self.full_count[...] = full_one
        self.half_count[...] = half_one

        def full(lanes):
            return wide(self.full_count[...], lanes)

        def part(lanes):
            return wide(self.half_count[...], lanes)

        def mask_of(row):
            place = lax.broadcasted_iota(jnp.int32, (cols, views, 128), 0)
            column = jnp.where(place < half, 2 * place, 2 * (place - half) + 1)
            view = lax.broadcasted_iota(jnp.int32, (cols, views, 128), 1)
            where = self.r * rows + row
            tall_a = jnp.where(where < HA, live_a, 0)
            tall_b = jnp.where(where < HB, live_b, 0)
            in_a = (view < self.live_a) & (view < tall_a)
            in_b = (view >= self.live_a) & (view - self.live_a < tall_b) & (column < WB)
            return jnp.where(in_a | in_b, 1.0, 0.0).astype(F32)

        def make_mask(row):
            mask[row] = mask_of(row)

        loop(rows, make_mask)
        side, side_2 = self.side, self.side_2
        above_a, below_a, above_2, below_2 = (
            self.edge_a.at[0],
            self.edge_a.at[1],
            self.edge_2.at[0],
            self.edge_2.at[1],
        )

        for ref in (h1, self.dz2):
            lanes = ref.shape[-1]
            ref[0] = zeros((cols + 2, views, lanes))
            ref[rows + 1] = zeros((cols + 2, views, lanes))
            for row in range(1, rows + 1):
                ref[row, 0] = zeros((views, lanes))
                ref[row, cols + 1] = zeros((views, lanes))
        h4[0] = zeros(h4.shape[1:])
        for row in range(1, rows + 1):
            h4[row, half] = zeros((views, h4.shape[-1]))
        self.dz5[rows // 2] = zeros(self.dz5.shape[1:])
        for row in range(rows // 2):
            self.dz5[row, half] = zeros((views, self.dz5.shape[-1]))

        def row_mask(row, lanes):
            return wide(flat(mask[row]), lanes)

        none = jnp.zeros((1, 256), F32)

        loads.xa.wait()
        loads.xb.wait()

        def gather_row(row):
            for k in range(cols):
                c = natural[k]
                near = self.xa[row, c].astype(F32)
                if c < self.xb.shape[1]:
                    rest = self.xb[row, c].astype(F32)
                else:
                    rest = jnp.zeros((self.live_b, near.shape[-1]), F32)
                value = jnp.concatenate([near, rest], axis=0)
                x[row, k] = (value * wide(mask[row, k], value.shape[-1])).astype(BF16)

        loop(rows, gather_row)
        loads.w1.wait()

        def reduce_row(row, carry):
            total, square = carry
            value = mm(flat(x[row]), self.w1[...])
            z1[row] = value.reshape(cols, views, -1)
            return (total + col_sum(value), square + col_sum(value * value))

        sums = loop(rows, reduce_row, (none, none))
        self.greeted()
        self.sum_start(AT_ONE, sums)
        self.sum_turn(AT_ONE)
        self.edge_send(-1, z1[0], side.at[0], below_a, 0)
        self.edge_send(1, z1[rows - 1], side.at[1], above_a, 1)
        loads.ca.wait()
        loads.cb.wait()
        for o in range(rows // 2):
            for p in range(half):
                for h in range(2):
                    lanes = slice(h * LEAF, h * LEAF + LEAF)
                    near = self.ca[o, p, :, lanes].astype(F32)
                    if p < self.cb.shape[1]:
                        rest = self.cb[o, p, :, lanes].astype(F32)
                    else:
                        rest = jnp.zeros((self.live_b, LEAF), F32)
                    self.cot[h, o * half + p] = jnp.concatenate([near, rest], axis=0).astype(BF16)
        self.norm_ready(NARROW, self.sum_finish(AT_ONE), full(256))

        def hidden_of(value, live):
            value = self.act(NARROW, value)
            return (value * sigmoid(value) * live).astype(BF16).reshape(cols, views, -1)

        def hidden_one(row):
            value = hidden_of(flat(z1[row]), row_mask(row, 256))
            for k in range(cols):
                h1[row + 1, natural[k] + 1] = value[k]

        loop(rows, hidden_one)

        def hidden_edge(step, source, slot, row):
            @pl.when(self.has_strip(step))
            def _():
                given = flat(self.edge_read(step, side.at[0], source, slot))
                value = hidden_of(given, wide(flat(mask_of(row)), 256))
                for k in range(cols):
                    h1[row + 1, natural[k] + 1] = value[k]

        loads.w2.wait()

        def conv_row(row, carry):
            total, square = carry
            value = 0.0
            for i in range(3):
                for j in range(3):
                    tap = (i * 3 + j) * 256
                    value = value + mm(flat(h1[row + i, j : j + cols]), self.w2[tap : tap + 256, :])
            value = value.reshape(cols, views, -1)
            ordered = jnp.concatenate([value[c] for c in natural], axis=0)
            z2[row] = ordered.reshape(cols, views, -1)
            kept = ordered * row_mask(row, 256)
            return (total + col_sum(kept), square + col_sum(kept * ordered))

        sums = loop(rows - 2, lambda i, carry: conv_row(i + 1, carry), (none, none))

        hidden_edge(-1, above_a, 1, -1)
        hidden_edge(1, below_a, 0, rows)
        sums = conv_row(rows - 1, conv_row(0, sums))
        self.sum_start(AT_TWO, sums)
        self.sum_turn(AT_TWO)
        self.edge_sent(-1, side.at[0], below_a, 0)
        self.edge_sent(1, side.at[1], above_a, 1)
        self.edge_send(-1, z2[0], side.at[0], below_2, 2)
        self.edge_send(1, z2[rows - 1], side.at[1], above_2, 3)
        loads.w3.wait()
        self.norm_ready(SPATIAL, self.sum_finish(AT_TWO), full(256))

        def hidden_two(row):
            value = self.act(SPATIAL, flat(z2[row]))
            value = (value * sigmoid(value) * row_mask(row, 256)).astype(BF16)
            h2[row] = value.reshape(cols, views, -1)

        loop(rows, hidden_two)

        def expand_row(row, carry):
            given = flat(h2[row])
            done = []
            for n in range(2):
                lanes = slice(n * 512, n * 512 + 512)
                value = mm(given, self.w3[:, lanes])
                z3[row, :, :, lanes] = value.reshape(cols, views, -1)
                done.append((carry[n][0] + col_sum(value), carry[n][1] + col_sum(value * value)))
            return tuple(done)

        nothing = jnp.zeros((1, 512), F32)
        sums = loop(rows, expand_row, ((nothing, nothing), (nothing, nothing)))
        sums = [jnp.concatenate([sums[0][i], sums[1][i]], axis=1) for i in range(2)]
        self.sum_start(AT_THREE, sums)
        self.sum_turn(AT_THREE)
        loads.w4.wait()
        loads.ws.wait()
        self.norm_ready(WIDENED, self.sum_finish(AT_THREE), full(1024))

        def feed_step(step):
            row, pair = step // half, lax.rem(step, half)
            here = pl.ds(pair * 2, 2)
            value = self.act(WIDENED, flat(z3[row, here])) + flat(x[row, here]).astype(F32)
            value = value * sigmoid(value) * wide(flat(mask[row, here]), 1024)
            feed[row, here] = value.astype(BF16).reshape(2, views, -1)

        loop(rows * half, feed_step)

        def squeeze_row(row, carry):
            total, square = carry
            value = mm(flat(feed[row]), self.w4[...])
            z4[row] = value.reshape(cols, views, -1)
            return (total + col_sum(value), square + col_sum(value * value))

        sums = loop(rows, squeeze_row, (nothing, nothing))
        self.sum_start(AT_FOUR, sums)
        self.sum_turn(AT_FOUR)
        self.edge_send(1, z4[rows - 1], side_2, self.edge_4, 4)

        def even(ref):
            return jnp.concatenate([flat(ref[2 * o, 0:half]) for o in range(rows // 2)], axis=0)

        for h in range(2):
            sums = []
            for n in range(2):
                lanes = slice(h * LEAF + n * 512, h * LEAF + n * 512 + 512)
                value = mm(even(feed), self.ws[:, lanes])
                big[2 + h, :, :, n * 512 : n * 512 + 512] = value.reshape(cols, views, -1)
                sums.append((col_sum(value), col_sum(value * value)))
            for i in range(2):
                self.short_sum[i : i + 1, h * LEAF : h * LEAF + LEAF] = jnp.concatenate(
                    [sums[0][i], sums[1][i]], axis=1
                )
        self.sum_start(AT_SHORT, [self.short_sum[0:1, :], self.short_sum[1:2, :]])
        self.norm_ready(SQUEEZE, self.sum_finish(AT_FOUR), full(512))

        def hidden_four(row):
            for p in range(2):
                value = self.act(SQUEEZE, flat(z4[row, p * half : p * half + half]))
                value = value * sigmoid(value) * wide(flat(mask[row, p * half : p * half + half]), 512)
                start = p * (half + 1)
                h4[row + 1, start : start + half] = value.astype(BF16).reshape(half, views, -1)

        loop(rows, hidden_four)
        loads.w5.wait()
        starts = (half, 0, half + 1)

        def taken(i, j):
            return jnp.concatenate(
                [flat(h4[2 * o + i, starts[j] : starts[j] + half]) for o in range(rows // 2)], axis=0
            )

        value = 0.0
        for i in (1, 2, 0):
            if i == 0:

                @pl.when(self.has_strip(-1))
                def _():
                    given = self.edge_read(-1, side_2, self.edge_4, 4)
                    live = mask_of(-1)
                    for p in range(2):
                        here = slice(p * half, p * half + half)
                        point = self.act(SQUEEZE, flat(given[here]))
                        point = point * sigmoid(point) * wide(flat(live[here]), 512)
                        start = p * (half + 1)
                        h4[0, start : start + half] = point.astype(BF16).reshape(half, views, -1)

            for j in range(3):
                tap = (i * 3 + j) * 512
                value = value + mm(taken(i, j), self.w5[tap : tap + 512, :])
        z5[...] = value
        half_mask = jnp.concatenate(
            [flat(mask[2 * o, 0:half]) for o in range(rows // 2)], axis=0
        )
        self.half_mask[...] = half_mask
        kept = value * wide(half_mask, 512)
        self.sum_start(AT_FIVE, (col_sum(kept), col_sum(kept * value)))
        self.sum_turn(AT_FIVE)
        self.sum_turn(AT_SHORT)
        self.edge_sent(1, side_2, self.edge_4, 4)
        row_5 = half * views
        self.edge_send(
            -1,
            z5[0:row_5, :].reshape(half, views, -1),
            side_2.at[0 : half + 1],
            self.edge_5,
            5,
        )
        loads.w6.wait()
        self.norm_ready(STRIDED, self.sum_finish(AT_FIVE), part(512))
        value = self.act(STRIDED, z5[...])
        h5[...] = (value * sigmoid(value) * wide(self.half_mask[...], 512)).astype(BF16)

        for h in range(2):
            sums = []
            for n in range(2):
                lanes = slice(h * LEAF + n * 512, h * LEAF + n * 512 + 512)
                value = mm(h5[...], self.w6[:, lanes])
                big[h, :, :, n * 512 : n * 512 + 512] = value.reshape(cols, views, -1)
                sums.append((col_sum(value), col_sum(value * value)))
            for i in range(2):
                self.main_sum[i : i + 1, h * LEAF : h * LEAF + LEAF] = jnp.concatenate(
                    [sums[0][i], sums[1][i]], axis=1
                )
        self.sum_start(AT_SIX, [self.main_sum[0:1, :], self.main_sum[1:2, :]])
        self.norm_ready(SHORTCUT, self.sum_finish(AT_SHORT), part(2048))
        self.sum_turn(AT_SIX)
        self.norm_ready(OUTPUT, self.sum_finish(AT_SIX), part(2048))

        dh4, cot = self.dh4, self.cot
        zero = jnp.zeros((1, LEAF), F32)
        for h in range(2):
            lanes = slice(h * LEAF, h * LEAF + LEAF)

            def out_step(pair, carry):
                here = pl.ds(pair * 2, 2)
                main, side = flat(big[h, here]), flat(big[2 + h, here])
                value = self.act(OUTPUT, main, lanes) + self.act(SHORTCUT, side, lanes)
                there = wide(self.half_mask[pl.ds(pl.multiple_of(pair * 2 * views, 8), 2 * views), :], LEAF)
                sigma = sigmoid(value)
                given = flat(cot[h, here]).astype(F32)
                slope = given * there * (sigma * (1.0 + value * (1.0 - sigma)))
                cot[h, here] = (value * sigma * there).astype(BF16).reshape(2, views, -1)
                for n in range(2):
                    dh4[2 * h + n, here] = slope[:, n * 512 : n * 512 + 512].reshape(2, views, -1)
                return (
                    carry[0] + col_sum(slope),
                    carry[1] + col_sum(slope * self.off_mean(OUTPUT, main, lanes)),
                    carry[2] + col_sum(slope * self.off_mean(SHORTCUT, side, lanes)),
                )

            sums = loop(half, out_step, (zero, zero, zero))
            for i in range(3):
                start = i * 2 * LEAF + h * LEAF
                self.top_sum[:, start : start + LEAF] = sums[i]
        self.sum_start(AT_SEVEN, [self.top_sum[...]])
        for o in range(rows // 2):
            for p in range(half):
                for h in range(2):
                    lanes = slice(h * LEAF, h * LEAF + LEAF)
                    done = cot[h, o * half + p].astype(F32)
                    self.ca[o, p, :, lanes] = done[0 : self.live_a].astype(BF16)
                    if p < self.cb.shape[1]:
                        self.cb[o, p, :, lanes] = done[self.live_a :].astype(BF16)
        stores = [
            pltpu.make_async_copy(self.ca, self.out_a_to, self.store_sem.at[0]),
            pltpu.make_async_copy(self.cb, self.out_b_to, self.store_sem.at[1]),
        ]
        for copy in stores:
            copy.start()
        self.sum_turn(AT_SEVEN)
        totals = self.sum_finish(AT_SEVEN)
        totals = [totals[:, i * 2 * LEAF : (i + 1) * 2 * LEAF] for i in range(3)]
        self.norm_back_ready(OUTPUT, totals[0], totals[1], part(2048))
        self.norm_back_ready(SHORTCUT, totals[0], totals[2], part(2048))

        dz6, dzs = self.dz6, self.dzs
        for h in range(2):
            lanes = slice(h * LEAF, h * LEAF + LEAF)

            def top_step(pair):
                here = pl.ds(pair * 2, 2)
                there = pl.ds(pl.multiple_of(pair * 2 * views, 16), 2 * views)
                live = wide(self.half_mask[there, :], LEAF)
                slope = jnp.concatenate([flat(dh4[2 * h + n, here]) for n in range(2)], axis=1)
                dz6[there, lanes] = self.back(OUTPUT, slope, flat(big[h, here]), live, lanes)
                dzs[there, lanes] = self.back(SHORTCUT, slope, flat(big[2 + h, here]), live, lanes)

            loop(half, top_step)

        value = mm_nt(dz6[...], self.w6[...]) * slope_of(self.act(STRIDED, z5[...]))
        self.slope5[...] = value
        self.sum_start(AT_EIGHT, (col_sum(value), col_sum(value * self.off_mean(STRIDED, z5[...]))))

        self.edge_sent(-1, side_2.at[0 : half + 1], self.edge_5, 5)
        edge_s = self.edge_4.at[0 : half + 1]
        self.edge_send(
            -1,
            self.slope5[0:row_5, :].reshape(half, views, -1),
            side_2.at[0 : half + 1],
            edge_s,
            6,
        )

        for name in EXPAND_TWO_PARTS:
            first_lane = GRADS[name][3]

            def grad_expand_two(step):
                m, n = step // 2, lax.rem(step, 2)
                left = h5[:, pl.ds(pl.multiple_of(m * 256, 256), 256)]
                lanes = pl.ds(pl.multiple_of(first_lane + n * 512, 512), 512)
                self.grad_store(name, m, mm_tn(left, dz6[:, lanes]), lanes)

            loop(4, grad_expand_two)
            self.grad_start(name)

        def shortcut_back(n):
            lanes = pl.ds(pl.multiple_of(n * 256, 256), 256)
            value = mm_nt(dzs[...], self.ws[lanes, :]).reshape(rows // 2, half, views, -1)
            for o in range(rows // 2):
                big[2 * o, 0:half, :, lanes] = value[o]

        loop(4, shortcut_back)

        def grad_shortcut_two(m):
            here = pl.ds(pl.multiple_of(m * 256, 256), 256)
            left = jnp.concatenate(
                [flat(feed[2 * o, 0:half, :, here]) for o in range(rows // 2)], axis=0
            )
            for name in SHORTCUT_TWO_PARTS:
                lanes = slice(GRADS[name][3], GRADS[name][3] + GRADS[name][4])
                self.grad_store(name, m, mm_tn(left, dzs[:, lanes]), lanes)

        loop(4, grad_shortcut_two)
        for name in SHORTCUT_TWO_PARTS:
            self.grad_start(name)
        self.grad_slot(0)
        self.sum_turn(AT_EIGHT)
        totals = self.sum_finish(AT_EIGHT)
        self.norm_back_ready(STRIDED, totals[0:1], totals[1:2], part(512))
        dz5 = self.dz5
        value = self.back(STRIDED, self.slope5[...], z5[...], wide(self.half_mask[...], 512))
        for o in range(rows // 2):
            dz5[o, 0:half] = value[o * half * views : (o + 1) * half * views].reshape(half, views, -1)
        self.grad_slot(1)
        for i in (1, 2, 0):
            if i == 0:

                @pl.when(self.has_strip(1))
                def _():
                    given = self.edge_read(1, side_2.at[0 : half + 1], edge_s, 6)
                    point = self.edge_read(1, side_2.at[0 : half + 1], self.edge_5, 5)
                    live = wide(flat(mask_of(rows)[0:half]), 512)
                    point = self.back(STRIDED, flat(given), flat(point), live)
                    dz5[rows // 2, 0:half] = point.reshape(half, views, -1)

            lead = 1 if i == 0 else 0
            for j in (1, 2, 0):
                tap = (i * 3 + j) * 512
                start = 1 if j == 0 else 0
                given = jnp.concatenate(
                    [flat(dz5[o + lead, start : start + half]) for o in range(rows // 2)], axis=0
                )
                value = mm_nt(given, self.w5[tap : tap + 512, :]).reshape(rows // 2, half, views, -1)
                spot = slice(0, half) if j == 1 else slice(half, 2 * half)
                for o in range(rows // 2):
                    target = 2 * o if i == 1 else 2 * o + 1
                    if j == 0 or i == 0:
                        dh4[target, spot] = dh4[target, spot] + value[o]
                    else:
                        dh4[target, spot] = value[o]

        def slope_four(step, carry):
            row, p = step // 2, lax.rem(step, 2)
            here = pl.ds(p * half, half)
            before = flat(z4[row, here])
            value = flat(dh4[row, here]) * slope_of(self.act(SQUEEZE, before))
            dh4[row, here] = value.reshape(half, views, -1)
            return (
                carry[0] + col_sum(value),
                carry[1] + col_sum(value * self.off_mean(SQUEEZE, before)),
            )

        sums = loop(rows * 2, slope_four, (nothing, nothing))
        self.sum_start(AT_NINE, sums)
        self.sum_turn(AT_NINE)
        self.grad_slot(2)

        for i, name in enumerate(SPATIAL_TWO_PARTS):

            def grad_spatial_two(step):
                j, m = step // 2, lax.rem(step, 2)
                here = pl.ds(pl.multiple_of(m * 256, 256), 256)
                start = half * ((1 - j) * (2 - j) // 2) + (half + 1) * (j * (j + 1) // 2 - j)
                left = jnp.concatenate(
                    [flat(h4[2 * o + i, pl.ds(start, half), :, here]) for o in range(rows // 2)], axis=0
                )
                right = jnp.concatenate([flat(dz5[o, 0:half]) for o in range(rows // 2)], axis=0)
                self.grad_store(name, m, mm_tn(left, right), row=j * 16)

            loop(6, grad_spatial_two)
            self.grad_start(name)
        self.grad_slot(3)
        totals = self.sum_finish(AT_NINE)
        self.norm_back_ready(SQUEEZE, totals[0:1], totals[1:2], full(512))
        dz4 = self.dz4

        def back_four(step):
            row, p = step // 2, lax.rem(step, 2)
            here = pl.ds(p * half, half)
            value = self.back(
                SQUEEZE, flat(dh4[row, here]), flat(z4[row, here]), wide(flat(mask[row, here]), 512)
            )
            dz4[row, here] = value.reshape(half, views, -1)

        loop(rows * 2, back_four)
        self.grad_slot(4)

        def slope_three(row, carry, even):
            done = []
            for n in range(2):
                lanes = slice(n * 512, n * 512 + 512)
                before = flat(z3[row, :, :, lanes])
                grad = mm_nt(flat(dz4[row]), self.w4[lanes, :])
                if even:
                    count = half * views
                    more = flat(big[row, 0:half, :, lanes])
                    grad = jnp.concatenate([grad[:count] + more, grad[count:]], axis=0)
                point = self.act(WIDENED, before, lanes) + flat(x[row, :, :, lanes]).astype(F32)
                value = grad * slope_of(point)
                big[row, :, :, lanes] = value.reshape(cols, views, -1)
                done.append(
                    (
                        carry[n][0] + col_sum(value),
                        carry[n][1] + col_sum(value * self.off_mean(WIDENED, before, lanes)),
                    )
                )
            return tuple(done)

        def slope_pair(o, carry):
            return slope_three(2 * o + 1, slope_three(2 * o, carry, True), False)

        sums = loop(rows // 2, slope_pair, ((nothing, nothing), (nothing, nothing)))
        sums = [jnp.concatenate([sums[0][i], sums[1][i]], axis=1) for i in range(2)]
        self.sum_start(AT_TEN, sums)
        self.grad_slot(5)

        def grad_reduce_two(m):
            here = pl.ds(pl.multiple_of(m * 256, 256), 256)
            left = feed[:, :, :, here].reshape(-1, 256)
            self.grad_store(G_REDUCE_TWO, m, mm_tn(left, dz4[...].reshape(-1, 512)))

        loop(4, grad_reduce_two)
        self.grad_start(G_REDUCE_TWO)
        self.sum_turn(AT_TEN)
        self.grad_slot(6)
        totals = self.sum_finish(AT_TEN)
        self.norm_back_ready(WIDENED, totals[0:1], totals[1:2], full(1024))
        dz3 = feed

        def back_three(step):
            row, pair = step // half, lax.rem(step, half)
            here = pl.ds(pair * 2, 2)
            live = wide(flat(mask[row, here]), 1024)
            value = self.back(WIDENED, flat(big[row, here]), flat(z3[row, here]), live)
            dz3[row, here] = value.reshape(2, views, -1)

        loop(rows * half, back_three)
        self.grad_slot(7)


        def slope_spatial(row, carry):
            before = flat(z2[row])
            value = mm_nt(flat(dz3[row]), self.w3[...]) * slope_of(self.act(SPATIAL, before))
            dh4[row, :, :, 0:256] = value.reshape(cols, views, -1)
            return (
                carry[0] + col_sum(value),
                carry[1] + col_sum(value * self.off_mean(SPATIAL, before)),
            )

        sums = loop(rows, slope_spatial, (none, none))
        self.sum_start(AT_ELEVEN, sums)
        self.sum_turn(AT_ELEVEN)
        self.edge_sent(-1, side.at[0], below_2, 2)
        self.edge_sent(1, side.at[1], above_2, 3)
        self.edge_send(-1, dh4[0, :, :, 0:256], side.at[0], below_a, 7)
        self.edge_send(1, dh4[rows - 1, :, :, 0:256], side.at[1], above_a, 8)
        self.grad_slot(8)

        left = h2[...].reshape(-1, 256)
        g_low = mm_tn(left, dz3[:, :, :, 0:512].reshape(-1, 512))
        g_high = mm_tn(left, dz3[:, :, :, 512:1024].reshape(-1, 512))
        for s in range(SHARDS):
            at = self.place(G_EXPAND_ONE, s) * 16
            piece = jnp.concatenate([g_low[s * 8 : s * 8 + 8], g_high[s * 8 : s * 8 + 8]], axis=0)
            self.grads[EXPAND_ONE][at : at + 16, :] = piece.astype(BF16)
        self.grad_start(G_EXPAND_ONE)
        self.grad_slot(9)
        totals = self.sum_finish(AT_ELEVEN)
        self.norm_back_ready(SPATIAL, totals[0:1], totals[1:2], full(256))
        dz2 = self.dz2

        def back_two(row):
            value = self.back(SPATIAL, flat(dh4[row, :, :, 0:256]), flat(z2[row]), row_mask(row, 256))
            value = value.reshape(cols, views, -1)
            for k in range(cols):
                dz2[row + 1, natural[k] + 1] = value[k]

        loop(rows, back_two)
        self.grad_slot(10)
        for i in range(3):
            for j in range(3):
                left = h1[i : i + rows, j : j + cols].reshape(-1, 256)
                value = mm_tn(left, dz2[1 : rows + 1, 1 : cols + 1].reshape(-1, 256))
                for s in range(SHARDS):
                    at = self.place(G_SPATIAL_ONE, s) * 144 + (i * 3 + j) * 16
                    piece = value[s * 8 : s * 8 + 8]
                    piece = jnp.concatenate([piece[:, 0:128], piece[:, 128:256]], axis=0)
                    self.grads[SPATIAL_ONE][at : at + 16, :] = piece.astype(BF16)
        self.grad_start(G_SPATIAL_ONE)
        self.grad_slot(11)

        def edge_two(step, slope_from, slope_slot, value_from, value_slot, row):
            @pl.when(self.has_strip(step))
            def _():
                given = flat(self.edge_read(step, side.at[0], slope_from, slope_slot))
                point = flat(self.edge_read(step, side.at[0], value_from, value_slot))
                value = self.back(SPATIAL, given, point, wide(flat(mask_of(row)), 256))
                value = value.reshape(cols, views, -1)
                for k in range(cols):
                    dz2[row + 1, natural[k] + 1] = value[k]

        edge_two(-1, above_a, 8, above_2, 3, -1)
        edge_two(1, below_a, 7, below_2, 2, rows)

        def slope_narrow(row, carry):
            value = 0.0
            for i in range(3):
                for j in range(3):
                    tap = (i * 3 + j) * 256
                    given = flat(dz2[row + 2 - i, 2 - j : 2 - j + cols])
                    value = value + mm_nt(given, self.w2[tap : tap + 256, :])
            value = value.reshape(cols, views, -1)
            value = jnp.concatenate([value[c] for c in natural], axis=0)
            before = flat(z1[row])
            value = value * row_mask(row, 256) * slope_of(self.act(NARROW, before))
            dh4[row, :, :, 0:256] = value.reshape(cols, views, -1)
            return (
                carry[0] + col_sum(value),
                carry[1] + col_sum(value * self.off_mean(NARROW, before)),
            )

        sums = loop(rows, slope_narrow, (none, none))
        self.sum_start(AT_TWELVE, sums)
        self.sum_turn(AT_TWELVE)
        self.grad_slot(12)
        totals = self.sum_finish(AT_TWELVE)
        self.norm_back_ready(NARROW, totals[0:1], totals[1:2], full(256))
        dz1 = h2

        def back_one(row):
            value = self.back(NARROW, flat(dh4[row, :, :, 0:256]), flat(z1[row]), row_mask(row, 256))
            dz1[row] = value.reshape(cols, views, -1)

        loop(rows, back_one)

        def grad_reduce_one(m):
            here = pl.ds(pl.multiple_of(m * 256, 256), 256)
            left = x[:, :, :, here].reshape(-1, 256)
            self.grad_store(G_REDUCE_ONE, m, mm_tn(left, dz1[...].reshape(-1, 256)))

        loop(4, grad_reduce_one)
        self.grad_start(G_REDUCE_ONE)
        self.grad_slot(13)

        def input_row(row):
            for n in range(2):
                lanes = slice(n * 512, n * 512 + 512)
                value = mm_nt(flat(dz1[row]), self.w1[lanes, :]) + flat(big[row, :, :, lanes])
                value = value.reshape(cols, views, -1)
                for k in range(cols):
                    self.xa[row, natural[k], :, lanes] = value[k, 0 : self.live_a].astype(BF16)
                    if natural[k] < self.xb.shape[1]:
                        self.xb[row, natural[k], :, lanes] = value[k, self.live_a :].astype(BF16)

        loop(rows, input_row)
        for i, pair in enumerate(((self.xa, self.in_a_to), (self.xb, self.in_b_to))):
            copy = pltpu.make_async_copy(*pair, self.store_sem.at[2 + i])
            copy.start()
            stores.append(copy)

        self.grad_slot(14)
        for copy in stores:
            copy.wait()
        self.sums_sent()
        self.grads_sent()

        self.edge_sent(-1, side_2.at[0 : half + 1], edge_s, 6)
        self.edge_sent(-1, side.at[0], below_a, 7)
        self.edge_sent(1, side.at[1], above_a, 8)


def settle(*refs):
    half = len(refs) // 2
    for i in range(half):
        refs[half + i][...] = refs[i][...]


def settled(values):
    inside = pl.BlockSpec(memory_space=pltpu.VMEM)
    return pl.pallas_call(
        settle,
        out_shape=[jax.ShapeDtypeStruct(v.shape, v.dtype) for v in values],
        in_specs=[inside] * len(values),
        out_specs=[inside] * len(values),
    )(*values)


def sum_of(pay, near, mid, far, sems):
    return SimpleNamespace(direct=far is None, pay=pay, near=near, mid=mid, far=far, sems=sems)


def both_blocks(given, live_views, weights, gains, biases):
    d_size, r_size = lax.axis_size("dp"), lax.axis_size("rows")
    total = d_size * r_size
    rows, cols, views_a, c_in = given[0].shape
    views_b = given[1].shape[2]
    views = views_a + views_b
    half = cols // 2
    c_mid, c_mid2, c_out = gains[0].shape[1], gains[3].shape[1], gains[5].shape[1]
    pixels = (rows // 2) * half * views
    vmem, dma = pltpu.VMEM, pltpu.SemaphoreType.DMA
    anywhere = pl.BlockSpec(memory_space=pl.ANY)
    inside = pl.BlockSpec(memory_space=pltpu.VMEM)

    def full(lanes, kind):
        return vmem((rows, cols, views, lanes), kind)

    def like(value):
        return vmem(value.shape, value.dtype)

    sums = []
    for count, lanes, straight in SUMS:
        direct = straight and total <= 32
        sums.append(
            dict(
                pay=vmem((count, lanes), F32),
                near=vmem((total if direct else r_size, count, lanes), F32),
                mid=None if direct else vmem((count, lanes), F32),
                far=None if direct else vmem((d_size, count, lanes), F32),
                sems=dma((4,)),
            )
        )
    w = weights
    scratch = dict(
        xa=like(given[0]),
        xb=like(given[1]),
        ca=like(given[2]),
        cb=like(given[3]),
        x=full(c_in, BF16),
        w1=like(w[0]),
        w2=like(w[1]),
        w3=like(w[2]),
        w4=like(w[3]),
        w5=like(w[4]),
        w6=like(w[5]),
        ws=like(w[6]),
        cot=vmem((2, cols, views, LEAF), BF16),
        mask=full(128, F32),
        half_mask=vmem((pixels, 128), F32),
        full_count=vmem((1, 128), F32),
        half_count=vmem((1, 128), F32),
        z1=full(c_mid, F32),
        z2=full(c_mid, F32),
        z3=full(c_in, F32),
        z4=full(c_mid2, F32),
        z5=vmem((pixels, c_mid2), F32),
        h1=vmem((rows + 2, cols + 2, views, c_mid), BF16),
        h2=full(c_mid, BF16),
        feed=full(c_in, BF16),
        h4=vmem((rows + 1, cols + 1, views, c_mid2), BF16),
        h5=vmem((pixels, c_mid2), BF16),
        big=full(c_in, F32),
        short_sum=vmem((2, c_out), F32),
        main_sum=vmem((2, c_out), F32),
        top_sum=vmem((1, 3 * c_out), F32),
        dz6=vmem((pixels, c_out), BF16),
        dzs=vmem((pixels, c_out), BF16),
        slope5=vmem((pixels, c_mid2), F32),
        dz5=vmem((rows // 2 + 1, half + 1, views, c_mid2), BF16),
        dh4=full(c_mid2, F32),
        dz4=full(c_mid2, BF16),
        dz2=vmem((rows + 2, cols + 2, views, c_mid), BF16),
        g2=vmem((SHARDS * 144, 128), BF16),
        g3=vmem((SHARDS * 16, 512), BF16),
        load_sem=dma((11,)),
        store_sem=dma((4,)),
        side=vmem((2, cols + 1, views, c_mid), BF16),
        edge_a=vmem((2, cols + 1, views, c_mid), BF16),
        edge_2=vmem((2, cols + 1, views, c_mid), BF16),
        side_2=vmem((cols + 1, views, c_mid2), BF16),
        edge_4=vmem((cols + 1, views, c_mid2), BF16),
        edge_5=vmem((half + 1, views, c_mid2), BF16),
        halo_send=dma((9,)),
        halo_recv=dma((9,)),
        grad_send=dma((len(GRADS) * BITS,)),
        grad_recv=dma((len(GRADS) * BITS,)),
        coef=[vmem((8, gain.shape[1]), F32) for gain in gains],
        recv=[vmem(((SHARDS - 1) * height, lanes), BF16) for _, height, _, _, lanes, _ in GRADS],
        sums=sums,
    )
    grad_shapes = ((32, 256), (9, 8, 256), (8, 1024), (32, 512), (144, 512), (16, 2048), (32, 2048))
    ins = dict(
        live=live_views,
        xa_in=given[0],
        xb_in=given[1],
        ca_in=given[2],
        cb_in=given[3],
        w1_in=w[0],
        w2_in=w[1],
        w3_in=w[2],
        w4_in=w[3],
        w5_in=w[4],
        w6_in=w[5],
        ws_in=w[6],
        gain=list(gains),
        bias=list(biases),
    )
    shape = jax.ShapeDtypeStruct
    outs = dict(
        out_a_to=shape(given[2].shape, BF16),
        out_b_to=shape(given[3].shape, BF16),
        in_a_to=shape(given[0].shape, BF16),
        in_b_to=shape(given[1].shape, BF16),
        grad_out=[shape(s, F32) for s in grad_shapes],
        grad_gain=[shape(g.shape, F32) for g in gains],
        grad_bias=[shape(g.shape, F32) for g in gains],
    )
    parts = []
    trees = []
    for group in (ins, outs, scratch):
        leaves, tree = jax.tree.flatten(group, is_leaf=lambda v: not isinstance(v, (dict, list, type(None))))
        parts.append(leaves)
        trees.append(tree)
    in_specs = dict(ins)
    for name in ins:
        in_specs[name] = [inside] * len(gains) if isinstance(ins[name], list) else anywhere
    in_specs.update(live=pl.BlockSpec(memory_space=pltpu.SMEM))
    out_specs = {
        name: [inside] * len(outs[name]) if isinstance(outs[name], list) else anywhere for name in outs
    }
    spec_leaves = [
        jax.tree.flatten(group, is_leaf=lambda v: isinstance(v, pl.BlockSpec))[0]
        for group in (in_specs, out_specs)
    ]

    def body(*refs):
        fields = {}
        start = 0
        for leaves, tree in zip(parts, trees):
            fields.update(jax.tree.unflatten(tree, refs[start : start + len(leaves)]))
            start += len(leaves)
        g = SimpleNamespace(**fields)
        fields.update(
            grads=[g.w2, g.g2, g.g3, g.w4, g.w5, g.w6, g.ws],
            sums=[sum_of(**s) for s in g.sums],
        )
        Kernel((d_size, r_size, views_a, views_b), fields).run()

    results = pl.pallas_call(
        body,
        out_shape=parts[1],
        in_specs=spec_leaves[0],
        out_specs=spec_leaves[1],
        scratch_shapes=parts[2],
        compiler_params=pltpu.CompilerParams(
            collective_id=0, has_side_effects=True, vmem_limit_bytes=64 * 2**20 - 65536 * 4
        ),
        cost_estimate=pl.CostEstimate(flops=16 * 10**9, bytes_accessed=30 * 10**6, transcendentals=4 * 10**6),
    )(*parts[0])
    done = SimpleNamespace(**jax.tree.unflatten(trees[1], results))
    plain = settled([done.out_a_to, done.in_a_to, *done.grad_out, *done.grad_gain, *done.grad_bias])
    return plain[0], done.out_b_to, plain[1], done.in_b_to, list(plain[2:9]), plain[9:]


def on_device(input_a, input_b, live_views, *rest):
    weights, params, cotangents = rest[:7], rest[7:21], rest[21:]
    gains = [value.reshape(1, -1) for value in params[0::2]]
    biases = [value.reshape(1, -1) for value in params[1::2]]
    reduce_one, spatial_one, expand_one, reduce_two, spatial_two, expand_two, shortcut_two = weights
    weights = (
        reduce_one,
        spatial_one.transpose(1, 2, 0, 3).reshape(-1, spatial_one.shape[-1]),
        expand_one,
        reduce_two,
        spatial_two.transpose(1, 2, 0, 3).reshape(-1, spatial_two.shape[-1]),
        expand_two,
        shortcut_two,
    )
    given = [value.transpose(0, 2, 1, 3) for value in (input_a, input_b, *cotangents)]
    *moved, grads, norms = both_blocks(given, live_views.T, weights, gains, biases)
    maps = [value.transpose(0, 2, 1, 3) for value in moved]
    grads[1] = grads[1].reshape(3, 3, -1, grads[1].shape[-1]).transpose(2, 0, 1, 3)
    grads[4] = grads[4].reshape(3, 3, -1, grads[4].shape[-1]).transpose(2, 0, 1, 3)
    if lax.axis_size("dp") * lax.axis_size("rows") > SHARDS:
        grads = [lax.psum_scatter(g, "rows", scatter_dimension=0, tiled=True) for g in grads]
    small = []
    for i in range(7):
        small += [norms[i].reshape(-1), norms[7 + i].reshape(-1)]
    return (*maps, *grads, *small)


def solution(mesh):
    split = P("rows", "dp", None, None)
    whole = P()
    shard = P(("dp", "rows"), None)
    shard_4 = P(("dp", "rows"), None, None, None)
    return jax.shard_map(
        on_device,
        mesh=mesh,
        in_specs=(split, split) + (whole,) * 22 + (split, split),
        out_specs=(split,) * 4
        + (shard, shard_4, shard, shard, shard_4, shard, shard)
        + (whole,) * 14,
        check_vma=False,
    )
```

```python
import functools
from types import SimpleNamespace

import jax
import jax.numpy as jnp
from jax import lax
from jax.experimental import pallas as pl
from jax.experimental.pallas import tpu as pltpu
from jax.sharding import PartitionSpec as P

MESH = pl.DeviceIdType.MESH
F32 = jnp.float32
BF16 = jnp.bfloat16

HA = 14
WA = 14
HB = 10
WB = 10

EPS = 1e-05
LEAF = 1024
NARROW, SPATIAL, WIDENED, SQUEEZE, STRIDED, OUTPUT, SHORTCUT = range(7)
Y_FIRST = (0, 1, 2, 3, 4)
X_FIRST = (0, 2, 1, 3, 4)
Z_FIRST = (0, 3, 2, 1, 4)
BITS = 5
SHARDS = 1 << BITS
REDUCE_ONE, SPATIAL_ONE, EXPAND_ONE, REDUCE_TWO, SPATIAL_TWO, EXPAND_TWO, SHORTCUT_TWO = range(7)
(
    G_REDUCE_ONE,
    G_SPATIAL_ONE,
    G_EXPAND_ONE,
    G_REDUCE_TWO,
    G_SPATIAL_TWO_0,
    G_SPATIAL_TWO_1,
    G_SPATIAL_TWO_2,
    G_EXPAND_TWO_0,
    G_EXPAND_TWO_1,
    G_SHORTCUT_TWO_0,
    G_SHORTCUT_TWO_1,
    G_SHORTCUT_TWO_2,
) = range(12)
GRADS = (
    (REDUCE_ONE, 32, 0, 0, 256, Y_FIRST),
    (SPATIAL_ONE, 144, 0, 0, 128, Z_FIRST),
    (EXPAND_ONE, 16, 0, 0, 512, Y_FIRST),
    (REDUCE_TWO, 32, 0, 0, 512, Z_FIRST),
    (SPATIAL_TWO, 48, 0, 0, 512, Y_FIRST),
    (SPATIAL_TWO, 48, 1, 0, 512, X_FIRST),
    (SPATIAL_TWO, 48, 2, 0, 512, Z_FIRST),
    (EXPAND_TWO, 16, 0, 0, 1024, X_FIRST),
    (EXPAND_TWO, 16, 0, 1024, 1024, Z_FIRST),
    (SHORTCUT_TWO, 32, 0, 0, 768, Z_FIRST),
    (SHORTCUT_TWO, 32, 0, 768, 640, Y_FIRST),
    (SHORTCUT_TWO, 32, 0, 1408, 640, X_FIRST),
)
SLOTS = (
    ((7, 0), (8, 0),),
    (),
    ((9, 0), (10, 0), (11, 0), (7, 1), (8, 1),),
    (),
    (),
    (),
    ((4, 0), (5, 0), (6, 0), (7, 2), (8, 2),),
    (),
    ((3, 0), (9, 1), (10, 1), (11, 1), (7, 3), (8, 3),),
    (),
    ((4, 1), (5, 1), (6, 1),),
    (),
    ((1, 0), (9, 2), (10, 2), (11, 2), (2, 0), (3, 1), (7, 4), (8, 4),),
    (),
    ((0, 0), (9, 3), (10, 3), (11, 3), (3, 2), (4, 2), (5, 2), (6, 2), (1, 1), (2, 1), (0, 1), (9, 4), (10, 4), (11, 4), (3, 3), (4, 3), (5, 3), (6, 3), (1, 2), (2, 2), (0, 2), (3, 4), (4, 4), (5, 4), (6, 4), (1, 3), (2, 3), (0, 3), (1, 4), (2, 4), (0, 4),),
)
SPATIAL_TWO_PARTS = (G_SPATIAL_TWO_0, G_SPATIAL_TWO_1, G_SPATIAL_TWO_2)
EXPAND_TWO_PARTS = (G_EXPAND_TWO_0, G_EXPAND_TWO_1)
SHORTCUT_TWO_PARTS = (G_SHORTCUT_TWO_0, G_SHORTCUT_TWO_1, G_SHORTCUT_TWO_2)
(
    AT_ONE,
    AT_TWO,
    AT_THREE,
    AT_FOUR,
    AT_FIVE,
    AT_SHORT,
    AT_SIX,
    AT_SEVEN,
    AT_EIGHT,
    AT_NINE,
    AT_TEN,
    AT_ELEVEN,
    AT_TWELVE,
) = range(13)
SUMS = (
    (2, 256, True),
    (2, 256, True),
    (2, 1024, False),
    (2, 512, True),
    (2, 512, True),
    (2, 2048, False),
    (2, 2048, False),
    (1, 6144, False),
    (2, 512, True),
    (2, 512, True),
    (2, 1024, False),
    (2, 256, True),
    (2, 256, True),
)


def mm(left, right):
    return lax.dot_general(left, right, (((1,), (0,)), ((), ())), preferred_element_type=F32)


def mm_nt(left, right):
    return lax.dot_general(left, right, (((1,), (1,)), ((), ())), preferred_element_type=F32)


def mm_tn(left, right):
    return lax.dot_general(left, right, (((0,), (0,)), ((), ())), preferred_element_type=F32)


def sigmoid(value):
    return 0.5 + 0.5 * jnp.tanh(0.5 * value)


def slope_of(value):
    sigma = sigmoid(value)
    return sigma * (1.0 + value * (1.0 - sigma))


def flat(block):
    return block.reshape(-1, block.shape[-1])


def col_sum(value):
    return jnp.sum(value, axis=0, keepdims=True)


def wide(mask, lanes):
    return jnp.concatenate([mask] * (lanes // 128), axis=1)


def loop(count, body, init=None):
    if init is None:

        def plain(step, carry):
            body(step)
            return carry

        return lax.fori_loop(0, count, plain, 0)
    return lax.fori_loop(0, count, body, init)


def bit_of(number, bit):
    return lax.rem(number // (1 << bit), 2)


class Kernel:
    def __init__(self, sizes, refs):
        self.d_size, self.r_size, self.live_a, self.live_b = sizes
        self.total = self.d_size * self.r_size
        self.__dict__.update(refs)
        self.d = lax.axis_index("dp")
        self.r = lax.axis_index("rows")
        self.me = self.d * self.r_size + self.r
        self.low = (self.total // SHARDS).bit_length() - 1
        self.shard = self.me // (1 << self.low)
        self.r_bits = self.r_size.bit_length() - 1


    def device(self, number):
        return (number // self.r_size, lax.rem(number, self.r_size))

    def greet(self):
        barrier = pltpu.get_barrier_semaphore()

        def one(step):
            pl.semaphore_signal(
                barrier,
                inc=1,
                device_id=self.device(lax.rem(self.me + step + 1, self.total)),
                device_id_type=MESH,
            )

        loop(self.total - 1, one)

    def greeted(self):
        pl.semaphore_wait(pltpu.get_barrier_semaphore(), self.total - 1)

    def direct(self, name):
        return self.sums[name].direct

    def sum_start(self, name, vectors):
        s = self.sums[name]
        for i, vector in enumerate(vectors):
            s.pay[i : i + 1, :] = vector
        if s.direct:

            def send(step):
                further = lax.rem(step + self.total // 4, self.total - 1)
                pltpu.make_async_remote_copy(
                    s.pay,
                    s.near.at[self.me],
                    s.sems.at[0],
                    s.sems.at[1],
                    device_id=self.device(lax.rem(self.me + further + 1, self.total)),
                    device_id_type=MESH,
                ).start()

            loop(self.total - 1, send)
            s.near[self.me] = s.pay[...]
        else:
            for step in range(1, self.r_size):
                pltpu.make_async_remote_copy(
                    s.pay,
                    s.near.at[self.r],
                    s.sems.at[0],
                    s.sems.at[1],
                    device_id=(self.d, lax.rem(self.r + step, self.r_size)),
                    device_id_type=MESH,
                ).start()
            s.near[self.r] = s.pay[...]

    def sum_turn(self, name):
        s = self.sums[name]
        if s.direct:
            return
        several = s.near.at[0 : self.r_size - 1]
        pltpu.make_async_copy(several, several, s.sems.at[1]).wait()
        s.mid[...] = jnp.sum(s.near[...], axis=0)

        def send(step):
            pltpu.make_async_remote_copy(
                s.mid,
                s.far.at[self.d],
                s.sems.at[2],
                s.sems.at[3],
                device_id=(lax.rem(self.d + step + 1, self.d_size), self.r),
                device_id_type=MESH,
            ).start()

        loop(self.d_size - 1, send)
        s.far[self.d] = s.mid[...]

    def sum_finish(self, name):
        s = self.sums[name]
        if s.direct:
            many = s.near.at[0 : self.total - 1]
            pltpu.make_async_copy(many, many, s.sems.at[1]).wait()
            return jnp.sum(s.near[...], axis=0)
        many = s.far.at[0 : self.d_size - 1]
        pltpu.make_async_copy(many, many, s.sems.at[3]).wait()
        return jnp.sum(s.far[...], axis=0)

    def sums_sent(self):
        for s in self.sums:
            if s.direct:
                many = s.near.at[0 : self.total - 1]
                pltpu.make_async_copy(many, many, s.sems.at[0]).wait()
            else:
                several = s.near.at[0 : self.r_size - 1]
                pltpu.make_async_copy(several, several, s.sems.at[0]).wait()
                many = s.far.at[0 : self.d_size - 1]
                pltpu.make_async_copy(many, many, s.sems.at[2]).wait()


    def norm_ready(self, norm, totals, count):
        coef = self.coef[norm]
        mean = totals[0:1] / count
        scale = lax.rsqrt(totals[1:2] / count - mean * mean + EPS)
        factor = scale * self.gain[norm][...]
        coef[0:1, :] = factor
        coef[1:2, :] = self.bias[norm][...] - mean * factor
        coef[2:3, :] = mean
        coef[3:4, :] = scale

    def norm_back_ready(self, norm, first, second, count):
        coef = self.coef[norm]
        factor, mean, scale = coef[0:1, :], coef[2:3, :], coef[3:4, :]
        second = second * scale
        self.grad_gain[norm][...] = second
        self.grad_bias[norm][...] = first
        slant = factor * scale * (second / count)
        coef[4:5, :] = slant
        coef[5:6, :] = factor * (first / count) - mean * slant

    def act(self, norm, value, lanes=slice(None)):
        coef = self.coef[norm]
        return value * coef[0:1, lanes] + coef[1:2, lanes]

    def off_mean(self, norm, value, lanes=slice(None)):
        return value - self.coef[norm][2:3, lanes]

    def back(self, norm, slope, value, mask, lanes=slice(None)):
        coef = self.coef[norm]
        grad = slope * coef[0:1, lanes] - value * coef[4:5, lanes] - coef[5:6, lanes]
        return (grad * mask).astype(BF16)


    def to_strip(self, step, src, dst, slot):
        return pltpu.make_async_remote_copy(
            src,
            dst,
            self.halo_send.at[slot],
            self.halo_recv.at[slot],
            device_id=(self.d, self.r + step),
            device_id_type=MESH,
        )

    def has_strip(self, step):
        return self.r > 0 if step < 0 else self.r < self.r_size - 1

    def edge_send(self, step, value, stage, target, slot):
        count = value.shape[0]
        base = value[0, 0:1].astype(BF16)
        stage[0:count] = (value - base.astype(F32)).astype(BF16)
        stage[count] = jnp.broadcast_to(base.astype(F32), value.shape[1:]).astype(BF16)

        @pl.when(self.has_strip(step))
        def _():
            self.to_strip(step, stage, target, slot).start()

    def edge_sent(self, step, stage, target, slot):
        @pl.when(self.has_strip(step))
        def _():
            self.to_strip(step, stage, target, slot).wait_send()

    def edge_read(self, step, stage, target, slot):
        self.to_strip(-step, stage, target, slot).wait_recv()
        count = target.shape[0] - 1
        return target[0:count].astype(F32) + target[count].astype(F32)[None]


    def place(self, name, shard):
        order = GRADS[name][5]
        if isinstance(shard, int):
            return sum(((shard >> b) & 1) << (BITS - 1 - k) for k, b in enumerate(order))
        where = 0
        for k, b in enumerate(order):
            where = where + bit_of(shard, b) * (1 << (BITS - 1 - k))
        return where

    def halving(self, name, stage):
        order = GRADS[name][5]
        start = 0
        for k in range(stage):
            start = start + bit_of(self.shard, order[k]) * (1 << (BITS - 1 - k))
        half = 1 << (BITS - 1 - stage)
        mine = bit_of(self.shard, order[stage])
        offset = SHARDS - 2 * half
        bit = order[stage] + self.low
        if bit < self.r_bits:
            partner = (self.d, self.r + (1 - 2 * mine) * (1 << bit))
        else:
            partner = (self.d + (1 - 2 * mine) * (1 << (bit - self.r_bits)), self.r)
        return start + mine * half, start + (1 - mine) * half, half, offset, partner

    def grad_copy(self, name, stage):
        array, rows, part, lane, lanes, _ = GRADS[name]
        _, away, half, offset, partner = self.halving(name, stage)
        index = name * BITS + stage
        away = pl.ds(pl.multiple_of((part * SHARDS + away) * rows, 16), half * rows)
        return pltpu.make_async_remote_copy(
            self.grads[array].at[away, lane : lane + lanes],
            self.recv[name].at[pl.ds(offset * rows, half * rows)],
            self.grad_send.at[index],
            self.grad_recv.at[index],
            device_id=partner,
            device_id_type=MESH,
        )

    def grad_start(self, name):
        self.grad_copy(name, 0).start()

    def grad_slot(self, slot):
        for name, stage in SLOTS[slot]:
            self.grad_step(name, stage)

    def grad_step(self, name, stage):
        array, rows, part, lane, lanes, _ = GRADS[name]
        keep, _, half, offset, _ = self.halving(name, stage)
        keep = part * SHARDS + keep
        self.grad_copy(name, stage).wait_recv()
        own, came = self.grads[array], self.recv[name]
        across = slice(lane, lane + lanes)
        if stage < BITS - 1:
            height = 16
            while height * lanes < 65536 and (half * rows) % (2 * height) == 0:
                height *= 2

            def add(step):
                here = pl.ds(pl.multiple_of(keep * rows + step * height, 16), height)
                there = pl.ds(pl.multiple_of(offset * rows + step * height, 16), height)
                own[here, across] = own[here, across] + came[there, :]

            loop(half * rows // height, add)
            self.grad_copy(name, stage + 1).start()
            return
        here = pl.ds(pl.multiple_of(keep * rows, 16), rows)
        there = pl.ds(offset * rows, rows)
        out = self.grad_out[array]
        total = own[here, across].astype(F32) + came[there, :].astype(F32)
        if array == SPATIAL_ONE:
            for tap in range(9):
                out[tap, :, 0:128] = total[tap * 16 : tap * 16 + 8]
                out[tap, :, 128:256] = total[tap * 16 + 8 : tap * 16 + 16]
        elif array == EXPAND_ONE:
            out[:, 0:512] = total[0:8]
            out[:, 512:1024] = total[8:16]
        else:
            out[part * rows : part * rows + rows, across] = total

    def grads_sent(self):
        for name in range(len(GRADS)):
            for stage in range(BITS):
                self.grad_copy(name, stage).wait_send()

    def grad_store(self, name, block, value, lanes=slice(None), row=0):
        array, rows, part, _, _, _ = GRADS[name]
        per = 16 if array == SPATIAL_TWO else rows
        count = 256 // per
        base = (part * SHARDS + self.place(name, block * count)) * rows + row
        for s in range(count):
            where = pl.multiple_of(base + self.place(name, s) * rows, 16)
            self.grads[array][pl.ds(where, per), lanes] = value[s * per : (s + 1) * per].astype(BF16)


    def run(self):
        self.greet()
        pairs = dict(
            xa=(self.xa_in, self.xa),
            xb=(self.xb_in, self.xb),
            w1=(self.w1_in, self.w1),
            ca=(self.ca_in, self.ca),
            cb=(self.cb_in, self.cb),
            w2=(self.w2_in, self.w2),
            w3=(self.w3_in, self.w3),
            w4=(self.w4_in, self.w4),
            ws=(self.ws_in, self.ws),
            w5=(self.w5_in, self.w5),
            w6=(self.w6_in, self.w6),
        )
        loads = SimpleNamespace()
        for i, name in enumerate(pairs):
            copy = pltpu.make_async_copy(*pairs[name], self.load_sem.at[i])
            copy.start()
            setattr(loads, name, copy)

        x, z1, z2, z3, z4, z5 = self.x, self.z1, self.z2, self.z3, self.z4, self.z5
        h1, h2, feed, h4, h5 = self.h1, self.h2, self.feed, self.h4, self.h5
        big, mask = self.big, self.mask
        rows, cols, views, _ = x.shape
        half = cols // 2
        natural = [2 * (k % half) + k // half for k in range(cols)]
        zeros = functools.partial(jnp.zeros, dtype=BF16)

        live_a = self.live[0, self.d]
        live_b = self.live[1, self.d]
        all_a = self.live[0, 0]
        all_b = self.live[1, 0]
        for i in range(1, self.d_size):
            all_a = all_a + self.live[0, i]
            all_b = all_b + self.live[1, i]
        line = jnp.zeros((1, 128), jnp.int32)
        line_a = (line + all_a).astype(F32)
        line_b = (line + all_b).astype(F32)
        full_one = HA * WA * line_a + HB * WB * line_b
        half_one = ((HA + 1) // 2) * ((WA + 1) // 2) * line_a + ((HB + 1) // 2) * (
            (WB + 1) // 2
        ) * line_b
        self.full_count[...] = full_one
        self.half_count[...] = half_one

        def full(lanes):
            return wide(self.full_count[...], lanes)

        def part(lanes):
            return wide(self.half_count[...], lanes)

        def mask_of(row):
            place = lax.broadcasted_iota(jnp.int32, (cols, views, 128), 0)
            column = jnp.where(place < half, 2 * place, 2 * (place - half) + 1)
            view = lax.broadcasted_iota(jnp.int32, (cols, views, 128), 1)
            where = self.r * rows + row
            tall_a = jnp.where(where < HA, live_a, 0)
            tall_b = jnp.where(where < HB, live_b, 0)
            in_a = (view < self.live_a) & (view < tall_a)
            in_b = (view >= self.live_a) & (view - self.live_a < tall_b) & (column < WB)
            return jnp.where(in_a | in_b, 1.0, 0.0).astype(F32)

        def make_mask(row):
            mask[row] = mask_of(row)

        loop(rows, make_mask)
        side, side_2 = self.side, self.side_2
        above_a, below_a, above_2, below_2 = (
            self.edge_a.at[0],
            self.edge_a.at[1],
            self.edge_2.at[0],
            self.edge_2.at[1],
        )

        for ref in (h1, self.dz2):
            lanes = ref.shape[-1]
            ref[0] = zeros((cols + 2, views, lanes))
            ref[rows + 1] = zeros((cols + 2, views, lanes))
            for row in range(1, rows + 1):
                ref[row, 0] = zeros((views, lanes))
                ref[row, cols + 1] = zeros((views, lanes))
        h4[0] = zeros(h4.shape[1:])
        for row in range(1, rows + 1):
            h4[row, half] = zeros((views, h4.shape[-1]))
        self.dz5[rows // 2] = zeros(self.dz5.shape[1:])
        for row in range(rows // 2):
            self.dz5[row, half] = zeros((views, self.dz5.shape[-1]))

        def row_mask(row, lanes):
            return wide(flat(mask[row]), lanes)

        none = jnp.zeros((1, 256), F32)

        loads.xa.wait()
        loads.xb.wait()

        def gather_row(row):
            for k in range(cols):
                c = natural[k]
                near = self.xa[row, c].astype(F32)
                if c < self.xb.shape[1]:
                    rest = self.xb[row, c].astype(F32)
                else:
                    rest = jnp.zeros((self.live_b, near.shape[-1]), F32)
                value = jnp.concatenate([near, rest], axis=0)
                x[row, k] = (value * wide(mask[row, k], value.shape[-1])).astype(BF16)

        loop(rows, gather_row)
        loads.w1.wait()

        def reduce_row(row, carry):
            total, square = carry
            value = mm(flat(x[row]), self.w1[...])
            z1[row] = value.reshape(cols, views, -1)
            return (total + col_sum(value), square + col_sum(value * value))

        sums = loop(rows, reduce_row, (none, none))
        self.greeted()
        self.sum_start(AT_ONE, sums)
        self.sum_turn(AT_ONE)
        self.edge_send(-1, z1[0], side.at[0], below_a, 0)
        self.edge_send(1, z1[rows - 1], side.at[1], above_a, 1)
        loads.ca.wait()
        loads.cb.wait()
        for o in range(rows // 2):
            for p in range(half):
                for h in range(2):
                    lanes = slice(h * LEAF, h * LEAF + LEAF)
                    near = self.ca[o, p, :, lanes].astype(F32)
                    if p < self.cb.shape[1]:
                        rest = self.cb[o, p, :, lanes].astype(F32)
                    else:
                        rest = jnp.zeros((self.live_b, LEAF), F32)
                    self.cot[h, o * half + p] = jnp.concatenate([near, rest], axis=0).astype(BF16)
        self.norm_ready(NARROW, self.sum_finish(AT_ONE), full(256))

        def hidden_of(value, live):
            value = self.act(NARROW, value)
            return (value * sigmoid(value) * live).astype(BF16).reshape(cols, views, -1)

        def hidden_one(row):
            value = hidden_of(flat(z1[row]), row_mask(row, 256))
            for k in range(cols):
                h1[row + 1, natural[k] + 1] = value[k]

        loop(rows, hidden_one)

        def hidden_edge(step, source, slot, row):
            @pl.when(self.has_strip(step))
            def _():
                given = flat(self.edge_read(step, side.at[0], source, slot))
                value = hidden_of(given, wide(flat(mask_of(row)), 256))
                for k in range(cols):
                    h1[row + 1, natural[k] + 1] = value[k]

        loads.w2.wait()

        def conv_row(row, carry):
            total, square = carry
            value = 0.0
            for i in range(3):
                for j in range(3):
                    tap = (i * 3 + j) * 256
                    value = value + mm(flat(h1[row + i, j : j + cols]), self.w2[tap : tap + 256, :])
            value = value.reshape(cols, views, -1)
            ordered = jnp.concatenate([value[c] for c in natural], axis=0)
            z2[row] = ordered.reshape(cols, views, -1)
            kept = ordered * row_mask(row, 256)
            return (total + col_sum(kept), square + col_sum(kept * ordered))

        sums = loop(rows - 2, lambda i, carry: conv_row(i + 1, carry), (none, none))

        hidden_edge(-1, above_a, 1, -1)
        hidden_edge(1, below_a, 0, rows)
        sums = conv_row(rows - 1, conv_row(0, sums))
        self.sum_start(AT_TWO, sums)
        self.sum_turn(AT_TWO)
        self.edge_sent(-1, side.at[0], below_a, 0)
        self.edge_sent(1, side.at[1], above_a, 1)
        self.edge_send(-1, z2[0], side.at[0], below_2, 2)
        self.edge_send(1, z2[rows - 1], side.at[1], above_2, 3)
        loads.w3.wait()
        self.norm_ready(SPATIAL, self.sum_finish(AT_TWO), full(256))

        def hidden_two(row):
            value = self.act(SPATIAL, flat(z2[row]))
            value = (value * sigmoid(value) * row_mask(row, 256)).astype(BF16)
            h2[row] = value.reshape(cols, views, -1)

        loop(rows, hidden_two)

        def expand_row(row, carry):
            given = flat(h2[row])
            done = []
            for n in range(2):
                lanes = slice(n * 512, n * 512 + 512)
                value = mm(given, self.w3[:, lanes])
                z3[row, :, :, lanes] = value.reshape(cols, views, -1)
                done.append((carry[n][0] + col_sum(value), carry[n][1] + col_sum(value * value)))
            return tuple(done)

        nothing = jnp.zeros((1, 512), F32)
        sums = loop(rows, expand_row, ((nothing, nothing), (nothing, nothing)))
        sums = [jnp.concatenate([sums[0][i], sums[1][i]], axis=1) for i in range(2)]
        self.sum_start(AT_THREE, sums)
        self.sum_turn(AT_THREE)
        loads.w4.wait()
        loads.ws.wait()
        self.norm_ready(WIDENED, self.sum_finish(AT_THREE), full(1024))

        def feed_step(step):
            row, pair = step // half, lax.rem(step, half)
            here = pl.ds(pair * 2, 2)
            value = self.act(WIDENED, flat(z3[row, here])) + flat(x[row, here]).astype(F32)
            value = value * sigmoid(value) * wide(flat(mask[row, here]), 1024)
            feed[row, here] = value.astype(BF16).reshape(2, views, -1)

        loop(rows * half, feed_step)

        def squeeze_row(row, carry):
            total, square = carry
            value = mm(flat(feed[row]), self.w4[...])
            z4[row] = value.reshape(cols, views, -1)
            return (total + col_sum(value), square + col_sum(value * value))

        sums = loop(rows, squeeze_row, (nothing, nothing))
        self.sum_start(AT_FOUR, sums)
        self.sum_turn(AT_FOUR)
        self.edge_send(1, z4[rows - 1], side_2, self.edge_4, 4)

        def even(ref):
            return jnp.concatenate([flat(ref[2 * o, 0:half]) for o in range(rows // 2)], axis=0)

        for h in range(2):
            sums = []
            for n in range(2):
                lanes = slice(h * LEAF + n * 512, h * LEAF + n * 512 + 512)
                value = mm(even(feed), self.ws[:, lanes])
                big[2 + h, :, :, n * 512 : n * 512 + 512] = value.reshape(cols, views, -1)
                sums.append((col_sum(value), col_sum(value * value)))
            for i in range(2):
                self.short_sum[i : i + 1, h * LEAF : h * LEAF + LEAF] = jnp.concatenate(
                    [sums[0][i], sums[1][i]], axis=1
                )
        self.sum_start(AT_SHORT, [self.short_sum[0:1, :], self.short_sum[1:2, :]])
        self.norm_ready(SQUEEZE, self.sum_finish(AT_FOUR), full(512))

        def hidden_four(row):
            for p in range(2):
                value = self.act(SQUEEZE, flat(z4[row, p * half : p * half + half]))
                value = value * sigmoid(value) * wide(flat(mask[row, p * half : p * half + half]), 512)
                start = p * (half + 1)
                h4[row + 1, start : start + half] = value.astype(BF16).reshape(half, views, -1)

        loop(rows, hidden_four)
        loads.w5.wait()
        starts = (half, 0, half + 1)

        def taken(i, j):
            return jnp.concatenate(
                [flat(h4[2 * o + i, starts[j] : starts[j] + half]) for o in range(rows // 2)], axis=0
            )

        value = 0.0
        for i in (1, 2, 0):
            if i == 0:

                @pl.when(self.has_strip(-1))
                def _():
                    given = self.edge_read(-1, side_2, self.edge_4, 4)
                    live = mask_of(-1)
                    for p in range(2):
                        here = slice(p * half, p * half + half)
                        point = self.act(SQUEEZE, flat(given[here]))
                        point = point * sigmoid(point) * wide(flat(live[here]), 512)
                        start = p * (half + 1)
                        h4[0, start : start + half] = point.astype(BF16).reshape(half, views, -1)

            for j in range(3):
                tap = (i * 3 + j) * 512
                value = value + mm(taken(i, j), self.w5[tap : tap + 512, :])
        z5[...] = value
        half_mask = jnp.concatenate(
            [flat(mask[2 * o, 0:half]) for o in range(rows // 2)], axis=0
        )
        self.half_mask[...] = half_mask
        kept = value * wide(half_mask, 512)
        self.sum_start(AT_FIVE, (col_sum(kept), col_sum(kept * value)))
        self.sum_turn(AT_FIVE)
        self.sum_turn(AT_SHORT)
        self.edge_sent(1, side_2, self.edge_4, 4)
        row_5 = half * views
        self.edge_send(
            -1,
            z5[0:row_5, :].reshape(half, views, -1),
            side_2.at[0 : half + 1],
            self.edge_5,
            5,
        )
        loads.w6.wait()
        self.norm_ready(STRIDED, self.sum_finish(AT_FIVE), part(512))
        value = self.act(STRIDED, z5[...])
        h5[...] = (value * sigmoid(value) * wide(self.half_mask[...], 512)).astype(BF16)

        for h in range(2):
            sums = []
            for n in range(2):
                lanes = slice(h * LEAF + n * 512, h * LEAF + n * 512 + 512)
                value = mm(h5[...], self.w6[:, lanes])
                big[h, :, :, n * 512 : n * 512 + 512] = value.reshape(cols, views, -1)
                sums.append((col_sum(value), col_sum(value * value)))
            for i in range(2):
                self.main_sum[i : i + 1, h * LEAF : h * LEAF + LEAF] = jnp.concatenate(
                    [sums[0][i], sums[1][i]], axis=1
                )
        self.sum_start(AT_SIX, [self.main_sum[0:1, :], self.main_sum[1:2, :]])
        self.norm_ready(SHORTCUT, self.sum_finish(AT_SHORT), part(2048))
        self.sum_turn(AT_SIX)
        self.norm_ready(OUTPUT, self.sum_finish(AT_SIX), part(2048))

        dh4, cot = self.dh4, self.cot
        zero = jnp.zeros((1, LEAF), F32)
        for h in range(2):
            lanes = slice(h * LEAF, h * LEAF + LEAF)

            def out_step(pair, carry):
                here = pl.ds(pair * 2, 2)
                main, side = flat(big[h, here]), flat(big[2 + h, here])
                value = self.act(OUTPUT, main, lanes) + self.act(SHORTCUT, side, lanes)
                there = wide(self.half_mask[pl.ds(pl.multiple_of(pair * 2 * views, 8), 2 * views), :], LEAF)
                sigma = sigmoid(value)
                given = flat(cot[h, here]).astype(F32)
                slope = given * there * (sigma * (1.0 + value * (1.0 - sigma)))
                cot[h, here] = (value * sigma * there).astype(BF16).reshape(2, views, -1)
                for n in range(2):
                    dh4[2 * h + n, here] = slope[:, n * 512 : n * 512 + 512].reshape(2, views, -1)
                return (
                    carry[0] + col_sum(slope),
                    carry[1] + col_sum(slope * self.off_mean(OUTPUT, main, lanes)),
                    carry[2] + col_sum(slope * self.off_mean(SHORTCUT, side, lanes)),
                )

            sums = loop(half, out_step, (zero, zero, zero))
            for i in range(3):
                start = i * 2 * LEAF + h * LEAF
                self.top_sum[:, start : start + LEAF] = sums[i]
        self.sum_start(AT_SEVEN, [self.top_sum[...]])
        for o in range(rows // 2):
            for p in range(half):
                for h in range(2):
                    lanes = slice(h * LEAF, h * LEAF + LEAF)
                    done = cot[h, o * half + p].astype(F32)
                    self.ca[o, p, :, lanes] = done[0 : self.live_a].astype(BF16)
                    if p < self.cb.shape[1]:
                        self.cb[o, p, :, lanes] = done[self.live_a :].astype(BF16)
        stores = [
            pltpu.make_async_copy(self.ca, self.out_a_to, self.store_sem.at[0]),
            pltpu.make_async_copy(self.cb, self.out_b_to, self.store_sem.at[1]),
        ]
        for copy in stores:
            copy.start()
        self.sum_turn(AT_SEVEN)
        totals = self.sum_finish(AT_SEVEN)
        totals = [totals[:, i * 2 * LEAF : (i + 1) * 2 * LEAF] for i in range(3)]
        self.norm_back_ready(OUTPUT, totals[0], totals[1], part(2048))
        self.norm_back_ready(SHORTCUT, totals[0], totals[2], part(2048))

        dz6, dzs = self.dz6, self.dzs
        for h in range(2):
            lanes = slice(h * LEAF, h * LEAF + LEAF)

            def top_step(pair):
                here = pl.ds(pair * 2, 2)
                there = pl.ds(pl.multiple_of(pair * 2 * views, 16), 2 * views)
                live = wide(self.half_mask[there, :], LEAF)
                slope = jnp.concatenate([flat(dh4[2 * h + n, here]) for n in range(2)], axis=1)
                dz6[there, lanes] = self.back(OUTPUT, slope, flat(big[h, here]), live, lanes)
                dzs[there, lanes] = self.back(SHORTCUT, slope, flat(big[2 + h, here]), live, lanes)

            loop(half, top_step)

        value = mm_nt(dz6[...], self.w6[...]) * slope_of(self.act(STRIDED, z5[...]))
        self.slope5[...] = value
        self.sum_start(AT_EIGHT, (col_sum(value), col_sum(value * self.off_mean(STRIDED, z5[...]))))

        self.edge_sent(-1, side_2.at[0 : half + 1], self.edge_5, 5)
        edge_s = self.edge_4.at[0 : half + 1]
        self.edge_send(
            -1,
            self.slope5[0:row_5, :].reshape(half, views, -1),
            side_2.at[0 : half + 1],
            edge_s,
            6,
        )

        for name in EXPAND_TWO_PARTS:
            first_lane = GRADS[name][3]

            def grad_expand_two(step):
                m, n = step // 2, lax.rem(step, 2)
                left = h5[:, pl.ds(pl.multiple_of(m * 256, 256), 256)]
                lanes = pl.ds(pl.multiple_of(first_lane + n * 512, 512), 512)
                self.grad_store(name, m, mm_tn(left, dz6[:, lanes]), lanes)

            loop(4, grad_expand_two)
            self.grad_start(name)

        def shortcut_back(n):
            lanes = pl.ds(pl.multiple_of(n * 256, 256), 256)
            value = mm_nt(dzs[...], self.ws[lanes, :]).reshape(rows // 2, half, views, -1)
            for o in range(rows // 2):
                big[2 * o, 0:half, :, lanes] = value[o]

        loop(4, shortcut_back)

        def grad_shortcut_two(m):
            here = pl.ds(pl.multiple_of(m * 256, 256), 256)
            left = jnp.concatenate(
                [flat(feed[2 * o, 0:half, :, here]) for o in range(rows // 2)], axis=0
            )
            for name in SHORTCUT_TWO_PARTS:
                lanes = slice(GRADS[name][3], GRADS[name][3] + GRADS[name][4])
                self.grad_store(name, m, mm_tn(left, dzs[:, lanes]), lanes)

        loop(4, grad_shortcut_two)
        for name in SHORTCUT_TWO_PARTS:
            self.grad_start(name)
        self.grad_slot(0)
        self.sum_turn(AT_EIGHT)
        totals = self.sum_finish(AT_EIGHT)
        self.norm_back_ready(STRIDED, totals[0:1], totals[1:2], part(512))
        dz5 = self.dz5
        value = self.back(STRIDED, self.slope5[...], z5[...], wide(self.half_mask[...], 512))
        for o in range(rows // 2):
            dz5[o, 0:half] = value[o * half * views : (o + 1) * half * views].reshape(half, views, -1)
        self.grad_slot(1)
        for i in (1, 2, 0):
            if i == 0:

                @pl.when(self.has_strip(1))
                def _():
                    given = self.edge_read(1, side_2.at[0 : half + 1], edge_s, 6)
                    point = self.edge_read(1, side_2.at[0 : half + 1], self.edge_5, 5)
                    live = wide(flat(mask_of(rows)[0:half]), 512)
                    point = self.back(STRIDED, flat(given), flat(point), live)
                    dz5[rows // 2, 0:half] = point.reshape(half, views, -1)

            lead = 1 if i == 0 else 0
            for j in (1, 2, 0):
                tap = (i * 3 + j) * 512
                start = 1 if j == 0 else 0
                given = jnp.concatenate(
                    [flat(dz5[o + lead, start : start + half]) for o in range(rows // 2)], axis=0
                )
                value = mm_nt(given, self.w5[tap : tap + 512, :]).reshape(rows // 2, half, views, -1)
                spot = slice(0, half) if j == 1 else slice(half, 2 * half)
                for o in range(rows // 2):
                    target = 2 * o if i == 1 else 2 * o + 1
                    if j == 0 or i == 0:
                        dh4[target, spot] = dh4[target, spot] + value[o]
                    else:
                        dh4[target, spot] = value[o]

        def slope_four(step, carry):
            row, p = step // 2, lax.rem(step, 2)
            here = pl.ds(p * half, half)
            before = flat(z4[row, here])
            value = flat(dh4[row, here]) * slope_of(self.act(SQUEEZE, before))
            dh4[row, here] = value.reshape(half, views, -1)
            return (
                carry[0] + col_sum(value),
                carry[1] + col_sum(value * self.off_mean(SQUEEZE, before)),
            )

        sums = loop(rows * 2, slope_four, (nothing, nothing))
        self.sum_start(AT_NINE, sums)
        self.sum_turn(AT_NINE)
        self.grad_slot(2)

        for i, name in enumerate(SPATIAL_TWO_PARTS):

            def grad_spatial_two(step):
                j, m = step // 2, lax.rem(step, 2)
                here = pl.ds(pl.multiple_of(m * 256, 256), 256)
                start = half * ((1 - j) * (2 - j) // 2) + (half + 1) * (j * (j + 1) // 2 - j)
                left = jnp.concatenate(
                    [flat(h4[2 * o + i, pl.ds(start, half), :, here]) for o in range(rows // 2)], axis=0
                )
                right = jnp.concatenate([flat(dz5[o, 0:half]) for o in range(rows // 2)], axis=0)
                self.grad_store(name, m, mm_tn(left, right), row=j * 16)

            loop(6, grad_spatial_two)
            self.grad_start(name)
        self.grad_slot(3)
        totals = self.sum_finish(AT_NINE)
        self.norm_back_ready(SQUEEZE, totals[0:1], totals[1:2], full(512))
        dz4 = self.dz4

        def back_four(step):
            row, p = step // 2, lax.rem(step, 2)
            here = pl.ds(p * half, half)
            value = self.back(
                SQUEEZE, flat(dh4[row, here]), flat(z4[row, here]), wide(flat(mask[row, here]), 512)
            )
            dz4[row, here] = value.reshape(half, views, -1)

        loop(rows * 2, back_four)
        self.grad_slot(4)

        def slope_three(row, carry, even):
            done = []
            for n in range(2):
                lanes = slice(n * 512, n * 512 + 512)
                before = flat(z3[row, :, :, lanes])
                grad = mm_nt(flat(dz4[row]), self.w4[lanes, :])
                if even:
                    count = half * views
                    more = flat(big[row, 0:half, :, lanes])
                    grad = jnp.concatenate([grad[:count] + more, grad[count:]], axis=0)
                point = self.act(WIDENED, before, lanes) + flat(x[row, :, :, lanes]).astype(F32)
                value = grad * slope_of(point)
                big[row, :, :, lanes] = value.reshape(cols, views, -1)
                done.append(
                    (
                        carry[n][0] + col_sum(value),
                        carry[n][1] + col_sum(value * self.off_mean(WIDENED, before, lanes)),
                    )
                )
            return tuple(done)

        def slope_pair(o, carry):
            return slope_three(2 * o + 1, slope_three(2 * o, carry, True), False)

        sums = loop(rows // 2, slope_pair, ((nothing, nothing), (nothing, nothing)))
        sums = [jnp.concatenate([sums[0][i], sums[1][i]], axis=1) for i in range(2)]
        self.sum_start(AT_TEN, sums)
        self.grad_slot(5)

        def grad_reduce_two(m):
            here = pl.ds(pl.multiple_of(m * 256, 256), 256)
            left = feed[:, :, :, here].reshape(-1, 256)
            self.grad_store(G_REDUCE_TWO, m, mm_tn(left, dz4[...].reshape(-1, 512)))

        loop(4, grad_reduce_two)
        self.grad_start(G_REDUCE_TWO)
        self.sum_turn(AT_TEN)
        self.grad_slot(6)
        totals = self.sum_finish(AT_TEN)
        self.norm_back_ready(WIDENED, totals[0:1], totals[1:2], full(1024))
        dz3 = feed

        def back_three(step):
            row, pair = step // half, lax.rem(step, half)
            here = pl.ds(pair * 2, 2)
            live = wide(flat(mask[row, here]), 1024)
            value = self.back(WIDENED, flat(big[row, here]), flat(z3[row, here]), live)
            dz3[row, here] = value.reshape(2, views, -1)

        loop(rows * half, back_three)
        self.grad_slot(7)


        def slope_spatial(row, carry):
            before = flat(z2[row])
            value = mm_nt(flat(dz3[row]), self.w3[...]) * slope_of(self.act(SPATIAL, before))
            dh4[row, :, :, 0:256] = value.reshape(cols, views, -1)
            return (
                carry[0] + col_sum(value),
                carry[1] + col_sum(value * self.off_mean(SPATIAL, before)),
            )

        sums = loop(rows, slope_spatial, (none, none))
        self.sum_start(AT_ELEVEN, sums)
        self.sum_turn(AT_ELEVEN)
        self.edge_sent(-1, side.at[0], below_2, 2)
        self.edge_sent(1, side.at[1], above_2, 3)
        self.edge_send(-1, dh4[0, :, :, 0:256], side.at[0], below_a, 7)
        self.edge_send(1, dh4[rows - 1, :, :, 0:256], side.at[1], above_a, 8)
        self.grad_slot(8)

        left = h2[...].reshape(-1, 256)
        g_low = mm_tn(left, dz3[:, :, :, 0:512].reshape(-1, 512))
        g_high = mm_tn(left, dz3[:, :, :, 512:1024].reshape(-1, 512))
        for s in range(SHARDS):
            at = self.place(G_EXPAND_ONE, s) * 16
            piece = jnp.concatenate([g_low[s * 8 : s * 8 + 8], g_high[s * 8 : s * 8 + 8]], axis=0)
            self.grads[EXPAND_ONE][at : at + 16, :] = piece.astype(BF16)
        self.grad_start(G_EXPAND_ONE)
        self.grad_slot(9)
        totals = self.sum_finish(AT_ELEVEN)
        self.norm_back_ready(SPATIAL, totals[0:1], totals[1:2], full(256))
        dz2 = self.dz2

        def back_two(row):
            value = self.back(SPATIAL, flat(dh4[row, :, :, 0:256]), flat(z2[row]), row_mask(row, 256))
            value = value.reshape(cols, views, -1)
            for k in range(cols):
                dz2[row + 1, natural[k] + 1] = value[k]

        loop(rows, back_two)
        self.grad_slot(10)
        for i in range(3):
            for j in range(3):
                left = h1[i : i + rows, j : j + cols].reshape(-1, 256)
                value = mm_tn(left, dz2[1 : rows + 1, 1 : cols + 1].reshape(-1, 256))
                for s in range(SHARDS):
                    at = self.place(G_SPATIAL_ONE, s) * 144 + (i * 3 + j) * 16
                    piece = value[s * 8 : s * 8 + 8]
                    piece = jnp.concatenate([piece[:, 0:128], piece[:, 128:256]], axis=0)
                    self.grads[SPATIAL_ONE][at : at + 16, :] = piece.astype(BF16)
        self.grad_start(G_SPATIAL_ONE)
        self.grad_slot(11)

        def edge_two(step, slope_from, slope_slot, value_from, value_slot, row):
            @pl.when(self.has_strip(step))
            def _():
                given = flat(self.edge_read(step, side.at[0], slope_from, slope_slot))
                point = flat(self.edge_read(step, side.at[0], value_from, value_slot))
                value = self.back(SPATIAL, given, point, wide(flat(mask_of(row)), 256))
                value = value.reshape(cols, views, -1)
                for k in range(cols):
                    dz2[row + 1, natural[k] + 1] = value[k]

        edge_two(-1, above_a, 8, above_2, 3, -1)
        edge_two(1, below_a, 7, below_2, 2, rows)

        def slope_narrow(row, carry):
            value = 0.0
            for i in range(3):
                for j in range(3):
                    tap = (i * 3 + j) * 256
                    given = flat(dz2[row + 2 - i, 2 - j : 2 - j + cols])
                    value = value + mm_nt(given, self.w2[tap : tap + 256, :])
            value = value.reshape(cols, views, -1)
            value = jnp.concatenate([value[c] for c in natural], axis=0)
            before = flat(z1[row])
            value = value * row_mask(row, 256) * slope_of(self.act(NARROW, before))
            dh4[row, :, :, 0:256] = value.reshape(cols, views, -1)
            return (
                carry[0] + col_sum(value),
                carry[1] + col_sum(value * self.off_mean(NARROW, before)),
            )

        sums = loop(rows, slope_narrow, (none, none))
        self.sum_start(AT_TWELVE, sums)
        self.sum_turn(AT_TWELVE)
        self.grad_slot(12)
        totals = self.sum_finish(AT_TWELVE)
        self.norm_back_ready(NARROW, totals[0:1], totals[1:2], full(256))
        dz1 = h2

        def back_one(row):
            value = self.back(NARROW, flat(dh4[row, :, :, 0:256]), flat(z1[row]), row_mask(row, 256))
            dz1[row] = value.reshape(cols, views, -1)

        loop(rows, back_one)

        def grad_reduce_one(m):
            here = pl.ds(pl.multiple_of(m * 256, 256), 256)
            left = x[:, :, :, here].reshape(-1, 256)
            self.grad_store(G_REDUCE_ONE, m, mm_tn(left, dz1[...].reshape(-1, 256)))

        loop(4, grad_reduce_one)
        self.grad_start(G_REDUCE_ONE)
        self.grad_slot(13)

        def input_row(row):
            for n in range(2):
                lanes = slice(n * 512, n * 512 + 512)
                value = mm_nt(flat(dz1[row]), self.w1[lanes, :]) + flat(big[row, :, :, lanes])
                value = value.reshape(cols, views, -1)
                for k in range(cols):
                    self.xa[row, natural[k], :, lanes] = value[k, 0 : self.live_a].astype(BF16)
                    if natural[k] < self.xb.shape[1]:
                        self.xb[row, natural[k], :, lanes] = value[k, self.live_a :].astype(BF16)

        loop(rows, input_row)
        for i, pair in enumerate(((self.xa, self.in_a_to), (self.xb, self.in_b_to))):
            copy = pltpu.make_async_copy(*pair, self.store_sem.at[2 + i])
            copy.start()
            stores.append(copy)

        self.grad_slot(14)
        for copy in stores:
            copy.wait()
        self.sums_sent()
        self.grads_sent()

        self.edge_sent(-1, side_2.at[0 : half + 1], edge_s, 6)
        self.edge_sent(-1, side.at[0], below_a, 7)
        self.edge_sent(1, side.at[1], above_a, 8)


def settle(*refs):
    half = len(refs) // 2
    for i in range(half):
        refs[half + i][...] = refs[i][...]


def settled(values):
    inside = pl.BlockSpec(memory_space=pltpu.VMEM)
    return pl.pallas_call(
        settle,
        out_shape=[jax.ShapeDtypeStruct(v.shape, v.dtype) for v in values],
        in_specs=[inside] * len(values),
        out_specs=[inside] * len(values),
    )(*values)


def sum_of(pay, near, mid, far, sems):
    return SimpleNamespace(direct=far is None, pay=pay, near=near, mid=mid, far=far, sems=sems)


def both_blocks(given, live_views, weights, gains, biases):
    d_size, r_size = lax.axis_size("dp"), lax.axis_size("rows")
    total = d_size * r_size
    rows, cols, views_a, c_in = given[0].shape
    views_b = given[1].shape[2]
    views = views_a + views_b
    half = cols // 2
    c_mid, c_mid2, c_out = gains[0].shape[1], gains[3].shape[1], gains[5].shape[1]
    pixels = (rows // 2) * half * views
    vmem, dma = pltpu.VMEM, pltpu.SemaphoreType.DMA
    anywhere = pl.BlockSpec(memory_space=pl.ANY)
    inside = pl.BlockSpec(memory_space=pltpu.VMEM)

    def full(lanes, kind):
        return vmem((rows, cols, views, lanes), kind)

    def like(value):
        return vmem(value.shape, value.dtype)

    sums = []
    for count, lanes, straight in SUMS:
        direct = straight and total <= 32
        sums.append(
            dict(
                pay=vmem((count, lanes), F32),
                near=vmem((total if direct else r_size, count, lanes), F32),
                mid=None if direct else vmem((count, lanes), F32),
                far=None if direct else vmem((d_size, count, lanes), F32),
                sems=dma((4,)),
            )
        )
    w = weights
    scratch = dict(
        xa=like(given[0]),
        xb=like(given[1]),
        ca=like(given[2]),
        cb=like(given[3]),
        x=full(c_in, BF16),
        w1=like(w[0]),
        w2=like(w[1]),
        w3=like(w[2]),
        w4=like(w[3]),
        w5=like(w[4]),
        w6=like(w[5]),
        ws=like(w[6]),
        cot=vmem((2, cols, views, LEAF), BF16),
        mask=full(128, F32),
        half_mask=vmem((pixels, 128), F32),
        full_count=vmem((1, 128), F32),
        half_count=vmem((1, 128), F32),
        z1=full(c_mid, F32),
        z2=full(c_mid, F32),
        z3=full(c_in, F32),
        z4=full(c_mid2, F32),
        z5=vmem((pixels, c_mid2), F32),
        h1=vmem((rows + 2, cols + 2, views, c_mid), BF16),
        h2=full(c_mid, BF16),
        feed=full(c_in, BF16),
        h4=vmem((rows + 1, cols + 1, views, c_mid2), BF16),
        h5=vmem((pixels, c_mid2), BF16),
        big=full(c_in, F32),
        short_sum=vmem((2, c_out), F32),
        main_sum=vmem((2, c_out), F32),
        top_sum=vmem((1, 3 * c_out), F32),
        dz6=vmem((pixels, c_out), BF16),
        dzs=vmem((pixels, c_out), BF16),
        slope5=vmem((pixels, c_mid2), F32),
        dz5=vmem((rows // 2 + 1, half + 1, views, c_mid2), BF16),
        dh4=full(c_mid2, F32),
        dz4=full(c_mid2, BF16),
        dz2=vmem((rows + 2, cols + 2, views, c_mid), BF16),
        g2=vmem((SHARDS * 144, 128), BF16),
        g3=vmem((SHARDS * 16, 512), BF16),
        load_sem=dma((11,)),
        store_sem=dma((4,)),
        side=vmem((2, cols + 1, views, c_mid), BF16),
        edge_a=vmem((2, cols + 1, views, c_mid), BF16),
        edge_2=vmem((2, cols + 1, views, c_mid), BF16),
        side_2=vmem((cols + 1, views, c_mid2), BF16),
        edge_4=vmem((cols + 1, views, c_mid2), BF16),
        edge_5=vmem((half + 1, views, c_mid2), BF16),
        halo_send=dma((9,)),
        halo_recv=dma((9,)),
        grad_send=dma((len(GRADS) * BITS,)),
        grad_recv=dma((len(GRADS) * BITS,)),
        coef=[vmem((8, gain.shape[1]), F32) for gain in gains],
        recv=[vmem(((SHARDS - 1) * height, lanes), BF16) for _, height, _, _, lanes, _ in GRADS],
        sums=sums,
    )
    grad_shapes = ((32, 256), (9, 8, 256), (8, 1024), (32, 512), (144, 512), (16, 2048), (32, 2048))
    ins = dict(
        live=live_views,
        xa_in=given[0],
        xb_in=given[1],
        ca_in=given[2],
        cb_in=given[3],
        w1_in=w[0],
        w2_in=w[1],
        w3_in=w[2],
        w4_in=w[3],
        w5_in=w[4],
        w6_in=w[5],
        ws_in=w[6],
        gain=list(gains),
        bias=list(biases),
    )
    shape = jax.ShapeDtypeStruct
    outs = dict(
        out_a_to=shape(given[2].shape, BF16),
        out_b_to=shape(given[3].shape, BF16),
        in_a_to=shape(given[0].shape, BF16),
        in_b_to=shape(given[1].shape, BF16),
        grad_out=[shape(s, F32) for s in grad_shapes],
        grad_gain=[shape(g.shape, F32) for g in gains],
        grad_bias=[shape(g.shape, F32) for g in gains],
    )
    parts = []
    trees = []
    for group in (ins, outs, scratch):
        leaves, tree = jax.tree.flatten(group, is_leaf=lambda v: not isinstance(v, (dict, list, type(None))))
        parts.append(leaves)
        trees.append(tree)
    in_specs = dict(ins)
    for name in ins:
        in_specs[name] = [inside] * len(gains) if isinstance(ins[name], list) else anywhere
    in_specs.update(live=pl.BlockSpec(memory_space=pltpu.SMEM))
    out_specs = {
        name: [inside] * len(outs[name]) if isinstance(outs[name], list) else anywhere for name in outs
    }
    spec_leaves = [
        jax.tree.flatten(group, is_leaf=lambda v: isinstance(v, pl.BlockSpec))[0]
        for group in (in_specs, out_specs)
    ]

    def body(*refs):
        fields = {}
        start = 0
        for leaves, tree in zip(parts, trees):
            fields.update(jax.tree.unflatten(tree, refs[start : start + len(leaves)]))
            start += len(leaves)
        g = SimpleNamespace(**fields)
        fields.update(
            grads=[g.w2, g.g2, g.g3, g.w4, g.w5, g.w6, g.ws],
            sums=[sum_of(**s) for s in g.sums],
        )
        Kernel((d_size, r_size, views_a, views_b), fields).run()

    results = pl.pallas_call(
        body,
        out_shape=parts[1],
        in_specs=spec_leaves[0],
        out_specs=spec_leaves[1],
        scratch_shapes=parts[2],
        compiler_params=pltpu.CompilerParams(
            collective_id=0, has_side_effects=True, vmem_limit_bytes=64 * 2**20 - 65536 * 4
        ),
        cost_estimate=pl.CostEstimate(flops=16 * 10**9, bytes_accessed=30 * 10**6, transcendentals=4 * 10**6),
    )(*parts[0])
    done = SimpleNamespace(**jax.tree.unflatten(trees[1], results))
    plain = settled([done.out_a_to, done.in_a_to, *done.grad_out, *done.grad_gain, *done.grad_bias])
    return plain[0], done.out_b_to, plain[1], done.in_b_to, list(plain[2:9]), plain[9:]


def on_device(input_a, input_b, live_views, *rest):
    weights, params, cotangents = rest[:7], rest[7:21], rest[21:]
    gains = [value.reshape(1, -1) for value in params[0::2]]
    biases = [value.reshape(1, -1) for value in params[1::2]]
    reduce_one, spatial_one, expand_one, reduce_two, spatial_two, expand_two, shortcut_two = weights
    weights = (
        reduce_one,
        spatial_one.transpose(1, 2, 0, 3).reshape(-1, spatial_one.shape[-1]),
        expand_one,
        reduce_two,
        spatial_two.transpose(1, 2, 0, 3).reshape(-1, spatial_two.shape[-1]),
        expand_two,
        shortcut_two,
    )
    given = [value.transpose(0, 2, 1, 3) for value in (input_a, input_b, *cotangents)]
    *moved, grads, norms = both_blocks(given, live_views.T, weights, gains, biases)
    maps = [value.transpose(0, 2, 1, 3) for value in moved]
    grads[1] = grads[1].reshape(3, 3, -1, grads[1].shape[-1]).transpose(2, 0, 1, 3)
    grads[4] = grads[4].reshape(3, 3, -1, grads[4].shape[-1]).transpose(2, 0, 1, 3)
    if lax.axis_size("dp") * lax.axis_size("rows") > SHARDS:
        grads = [lax.psum_scatter(g, "rows", scatter_dimension=0, tiled=True) for g in grads]
    small = []
    for i in range(7):
        small += [norms[i].reshape(-1), norms[7 + i].reshape(-1)]
    return (*maps, *grads, *small)


def solution(mesh):
    split = P("rows", "dp", None, None)
    whole = P()
    shard = P(("dp", "rows"), None)
    shard_4 = P(("dp", "rows"), None, None, None)
    return jax.shard_map(
        on_device,
        mesh=mesh,
        in_specs=(split, split) + (whole,) * 22 + (split, split),
        out_specs=(split,) * 4
        + (shard, shard_4, shard, shard, shard_4, shard, shard)
        + (whole,) * 14,
        check_vma=False,
    )
```
